32 devices in a mesh: blk: 8 (over y, x, core), col: 4 (over z).
Axes of the slice: x: 2, y: 2, z: 4, core: 2. Of those that a mesh axis runs over, the one named last changes fastest.
Arguments:
- features: bfloat16 [4096, 768], P(('blk', 'col')), may hold values from -6 to 6
- node_order: int32 [32, 128], P(('blk', 'col')), may hold values from 0 to 127, each once within a row
- weight: bfloat16 [768, 256], replicated, may hold values from -0.21875 to 0.21875
- cotangent: bfloat16 [4096, 256], P(('blk', 'col')), may hold values from -6 to 6
- tile_list: int32 [768, 2], P(('blk', 'col')), may hold values from -1 to 31, as said below
- tile_values: bfloat16 [768, 128, 128], P(('blk', 'col')), may hold values from -0.15625 to 0.15625
Outputs:
- hidden: bfloat16 [4096, 256], P(('blk', 'col'))
- x_grad: bfloat16 [4096, 768], P(('blk', 'col'))
- weight_grad: float32 [768, 256], replicated
The draws below stay inside these ranges and needn't reach their ends.
Inputs may be any that keep to these rules, and one draw needn't show every extreme that they name: `tile_list`: slots held by one device come in groups of 3, group g taking tiles whose column block is among the 1 block that device (blk index g, the holder's col index) holds. A live slot's row block is among the 4 blocks of the holder's blk index; an empty slot has row block -1 and a valid column block. Every device has at least one full group.
All inputs are finite; a program needn't handle non-finite values.
Results may differ from the reference program's by a relative error of at most 0.0075.
Values may be sent and summed in bfloat16 or wider, within the bound.
A program may use at most 128 MiB of HBM per device.

```python
import jax
import jax.numpy as jnp
from jax import lax

FIN = 768
HID = 256
TILE = 128
SLOTS = 3
CB = 1
RB = 4
NB = 32
NODES = 4096
TILES = 768
N_BLK = 8
N_COL = 4


def draw_tile_list(key, part):
    key = jax.random.fold_in(key, 11)
    keys = jax.random.split(key, 4)
    devices = N_BLK * N_COL
    level = jax.random.randint(keys[0], (devices, 1), 1, SLOTS + 1)
    raw_count = jax.random.randint(keys[1], (devices, N_BLK), 0, SLOTS + 1)
    live_count = jnp.minimum(raw_count, level)
    device_ids = jnp.arange(devices, dtype=jnp.int32)[:, None]
    group_ids = jnp.arange(N_BLK, dtype=jnp.int32)[None, :]
    live_count = jnp.where(group_ids == device_ids % N_BLK, SLOTS, live_count)
    slot_ids = jnp.arange(SLOTS, dtype=jnp.int32)
    live = slot_ids[None, None, :] < live_count[:, :, None]
    blk_of = device_ids // N_COL
    col_of = device_ids % N_COL
    row_pick = jax.random.randint(keys[2], (devices, N_BLK, SLOTS), 0, RB)
    col_pick = jax.random.randint(keys[3], (devices, N_BLK, SLOTS), 0, CB)
    row_block = blk_of[:, :, None] * RB + row_pick
    col_block = group_ids[:, :, None] * RB + col_of[:, :, None] * CB + col_pick
    row_block = jnp.where(live, row_block, -1)
    return jnp.stack([row_block.reshape(-1), col_block.reshape(-1)], axis=1).astype(jnp.int32)


def strengthened(drawn, own_key, source, target, blocks, factor):
    def block_of(dim):
        return (jnp.arange(drawn.shape[dim]) // (drawn.shape[dim] // blocks)).reshape((-1,) + (1,) * (drawn.ndim - 1 - dim))

    near = jax.random.permutation(own_key, blocks)[block_of(target)]
    second = (block_of(target) + blocks // 2) % blocks
    return jnp.where((block_of(source) == near) | (block_of(source) == second), factor * drawn, drawn)


def block_scale(stream_key, shape, pieces, least, top_value):
    gain, own = 1.0, jax.random.fold_in(stream_key, 6)
    for dim, parts in pieces:
        heights = jnp.exp(jax.random.uniform(jax.random.fold_in(own, dim), (parts,), jnp.float32, least / len(pieces), top_value / len(pieces)))
        gain = gain * jnp.repeat(heights, shape[dim] // parts).reshape([-1 if axis == dim else 1 for axis in range(len(shape))])
    return gain


def normal_values(stream_key, dims, width, reach, shards=(), kind=jnp.bfloat16):
    entries = width * jax.random.normal(stream_key, dims, jnp.float32)
    if shards:
        entries = entries * block_scale(stream_key, dims, shards, -0.22, 0.18)
    return jnp.clip(entries, -reach, reach).astype(kind)


def heavy_noise(key, shape, deviation, most, shards, heavy, kind=jnp.bfloat16):
    result = deviation * jax.random.normal(key, shape, jnp.float32)
    if shards:
        result = result * block_scale(key, shape, shards, -0.22, 0.18)
    return jnp.clip(strengthened(result, jax.random.fold_in(key, 3), *heavy), -most, most).astype(kind)


def setup_inputs(seed: int = 0) -> dict:
    splits = jax.random.split(jax.random.key(seed), 7)
    features = heavy_noise(splits[0], (NODES, FIN), 1.0, 6.0, ((0, 32),), (0, 1, 32, 2.75))
    node_order = jax.vmap(lambda own: jax.random.permutation(own, TILE))(jax.random.split(splits[1], NB)).reshape((NB, TILE)).astype(jnp.int32)
    weight = normal_values(splits[2], (FIN, HID), FIN ** -0.5, 0.21875)
    cotangent = normal_values(splits[3], (NODES, HID), 1.0, 6.0, ((0, 32),))
    tile_list = draw_tile_list(jax.random.fold_in(splits[6], 71), 0)
    tile_values = normal_values(splits[5], (TILES, TILE, TILE), (TILE * SLOTS * N_BLK // (2 * CB)) ** -0.5, 0.15625, ((0, 32),))
    return dict(features=features, node_order=node_order, weight=weight, cotangent=cotangent, tile_list=tile_list, tile_values=tile_values)


def gelu_tanh(values):
    return jax.nn.gelu(values, approximate=True)

def reference(features, node_order, weight, cotangent, tile_list, tile_values):
    blocks3 = features.reshape(NB, TILE, FIN)
    reordered = jnp.take_along_axis(blocks3, node_order[:, :, None], axis=1).reshape(NODES, FIN)
    panel = jnp.dot(reordered, weight, preferred_element_type=jnp.float32).astype(jnp.bfloat16)
    row_ids = tile_list[:, 0]
    col_ids = tile_list[:, 1]
    safe_rows = jnp.where(row_ids >= 0, row_ids, NB).astype(jnp.int32)
    per_dev = SLOTS * N_BLK
    group_rows = safe_rows.reshape(N_BLK * N_COL, per_dev)
    group_cols = col_ids.reshape(N_BLK * N_COL, per_dev)
    group_tiles = tile_values.reshape(N_BLK * N_COL, per_dev, TILE, TILE)
    panel3 = panel.reshape(NB, TILE, HID)

    def forward_step(total, item):
        tiles_now, rows_now, cols_now = item
        picked = panel3[cols_now].astype(jnp.float32)
        product = jnp.einsum('sij,sjf->sif', tiles_now.astype(jnp.float32), picked)
        return (total.at[rows_now].add(product), None)
    start_fwd = jnp.zeros((NB + 1, TILE, HID), jnp.float32)
    total_fwd, _ = lax.scan(forward_step, start_fwd, (group_tiles, group_rows, group_cols))
    agg = total_fwd[:NB].reshape(NODES, HID)
    hidden = gelu_tanh(agg).astype(jnp.bfloat16)
    _, pull = jax.vjp(gelu_tanh, agg)
    agg_grad = pull(cotangent.astype(jnp.float32))[0].astype(jnp.bfloat16)
    grad_pad = jnp.concatenate([agg_grad.reshape(NB, TILE, HID), jnp.zeros((1, TILE, HID), jnp.bfloat16)], axis=0)

    def backward_step(total, item):
        tiles_now, rows_now, cols_now = item
        picked = grad_pad[rows_now].astype(jnp.float32)
        product = jnp.einsum('sij,sif->sjf', tiles_now.astype(jnp.float32), picked)
        return (total.at[cols_now].add(product), None)
    start_bwd = jnp.zeros((NB, TILE, HID), jnp.float32)
    total_bwd, _ = lax.scan(backward_step, start_bwd, (group_tiles, group_rows, group_cols))
    panel_grad = total_bwd.reshape(NODES, HID).astype(jnp.bfloat16)
    weight_grad = jnp.dot(reordered.T, panel_grad, preferred_element_type=jnp.float32) * NODES ** (-0.5)
    row_grad = jnp.dot(panel_grad, weight.T, preferred_element_type=jnp.float32).astype(jnp.bfloat16)
    placed = jnp.zeros((NB, TILE, FIN), jnp.bfloat16)
    block_ids = jnp.arange(NB, dtype=jnp.int32)[:, None]
    placed = placed.at[block_ids, node_order].set(row_grad.reshape(NB, TILE, FIN))
    x_grad = placed.reshape(NODES, FIN)
    return (hidden, x_grad, weight_grad)
```

```python
import functools

import jax
import jax.numpy as jnp
from jax import lax
from jax.experimental import pallas as pl
from jax.experimental.pallas import tpu as pltpu
from jax.sharding import PartitionSpec as P

SLOTS = 3
MESH = pl.DeviceIdType.MESH
F32 = jnp.float32
BF16 = jnp.bfloat16


def dot(a, b):
    return jnp.dot(a, b, preferred_element_type=F32)


def kernel(
    dims, scale,
    feat_h, order_h, weight_h, cot_h, list_ref, tiles_h,
    hidden_ref, xgrad_ref, wgrad_ref,
    feat, order, weight, cot, tiles,
    adj, adj_t, feat_t, panels, part, part16, agg_in, grads, pg_part, pg16,
    pair_in, chip_out, chip_in, dw_part, dw16, dw_pair, dw_sum, dw_sum16, dw_chip,
    dw_col, dw_all,
    in_sem, ag_s, ag_r, rc_s, rc_r, gc_s, gc_r, pp_s, pp_r, pc_s, pc_r,
    dp_s, dp_r, dc_s, dc_r, dz_s, dz_r, dg_s, dg_r, dh_s, dh_r, di_s, di_r,
):
    n_blk, n_col, tile, fin, hid = dims
    n_chip = n_blk // 2
    half = hid // 2
    b = lax.axis_index("blk")
    c = lax.axis_index("col")
    chip = b // 2
    core = b % 2
    sib = b + 1 - 2 * core
    sends = []

    def rows(i, n=tile):
        return pl.ds(pl.multiple_of(i * n, n), n)

    def send(src, dst, s_sem, r_sem, blk, col):
        copy = pltpu.make_async_remote_copy(
            src_ref=src, dst_ref=dst, send_sem=s_sem, recv_sem=r_sem,
            device_id=(blk, col), device_id_type=MESH,
        )
        copy.start()
        sends.append(copy)

    def arrive(dst, s_sem, r_sem):
        pltpu.make_async_remote_copy(
            src_ref=dst, dst_ref=dst, send_sem=s_sem, recv_sem=r_sem,
            device_id=(sib, c), device_id_type=MESH,
        ).wait_recv()

    def other_chips():
        return [(k, (chip + k) % n_chip, (chip + n_chip - k) % n_chip) for k in range(1, n_chip)]

    def other_cols():
        return [(k, (c + k) % n_col, (c + n_col - k) % n_col) for k in range(1, n_col)]

    loads = []
    for i, (src, dst) in enumerate(
        ((feat_h, feat), (weight_h, weight), (order_h, order), (tiles_h, tiles), (cot_h, cot))
    ):
        copy = pltpu.make_async_copy(src, dst, in_sem.at[i])
        copy.start()
        loads.append(copy)

    barrier = pltpu.get_barrier_semaphore()
    peers = [(sib, c)]
    peers += [(2 * to + core, c) for _, to, _ in other_chips()]
    peers += [(b, to) for _, to, _ in other_cols()]
    for peer in peers:
        pl.semaphore_signal(barrier, inc=1, device_id=peer, device_id_type=MESH)

    loads[0].wait()
    loads[1].wait()
    loads[2].wait()
    place = (
        lax.broadcasted_iota(jnp.int32, (tile, tile), 0) == order[...]
    ).astype(F32).astype(BF16)
    mixed = dot(feat[...], weight[...]).astype(BF16)
    panel = lax.dot_general(
        place, mixed, (((0,), (0,)), ((), ())), preferred_element_type=F32
    ).astype(BF16)
    panels[rows(b), :] = panel
    pl.semaphore_wait(barrier, len(peers))

    for k, to, _ in other_chips():
        send(panels.at[rows(b)], panels.at[rows(b)], ag_s.at[k], ag_r.at[b], 2 * to + core, c)
    send(panels.at[rows(b)], panels.at[rows(b)], ag_s.at[0], ag_r.at[b], sib, c)

    loads[3].wait()

    def build(g, _):
        held = [tiles[g * SLOTS + s] for s in range(SLOTS)]
        ids = [list_ref[g * SLOTS + s, 0] - b * n_col for s in range(SLOTS)]
        for r in range(n_col):
            block = jnp.zeros((tile, tile), BF16)
            for t, i in zip(held, ids):
                block = block + jnp.where(i == r, t, jnp.zeros_like(t))
            adj[r * tile:(r + 1) * tile, rows(g)] = block
        return 0

    lax.fori_loop(0, n_blk, build, 0)

    for k, _, src in other_chips():
        at = panels.at[rows(2 * src + core)]
        arrive(at, ag_s.at[k], ag_r.at[2 * src + core])
        send(at, at, ag_s.at[n_chip + k], ag_r.at[2 * src + core], sib, c)
    arrive(panels.at[rows(sib)], ag_s.at[0], ag_r.at[sib])
    for k, _, src in other_chips():
        at = 2 * src + 1 - core
        arrive(panels.at[rows(at)], ag_s.at[k], ag_r.at[at])

    step = 4 * tile if n_col % 4 == 0 else tile

    def forward(i, _):
        got = dot(adj[rows(i, step), :], panels[...])
        part[rows(i, step), :] = got
        part16[rows(i, step), :] = got.astype(BF16)
        return 0

    lax.fori_loop(0, n_col * tile // step, forward, 0)
    for k, to, _ in other_cols():
        send(part16.at[rows(to)], agg_in.at[rows(c)], rc_s.at[k], rc_r.at[c], b, to)

    def turn(g, _):
        for r in range(n_col):
            adj_t[rows(g), r * tile:(r + 1) * tile] = (
                adj[r * tile:(r + 1) * tile, rows(g)].T
            )
        return 0

    lax.fori_loop(0, n_blk, turn, 0)
    for i in range(fin // tile):
        feat_t[i * tile:(i + 1) * tile, :] = feat[:, i * tile:(i + 1) * tile].T
    loads[4].wait()

    agg = part[rows(c), :]
    for k, _, src in other_cols():
        arrive(agg_in.at[rows(src)], rc_s.at[k], rc_r.at[src])
        agg = agg + agg_in[rows(src), :].astype(F32)

    root = 0.7978845608028654
    inner = root * (agg + 0.044715 * agg * agg * agg)
    th = jnp.tanh(inner)
    slope = 0.5 * (1.0 + th) + 0.5 * agg * (1.0 - th * th) * (
        root * (1.0 + 3 * 0.044715 * agg * agg)
    )
    grads[rows(c), :] = (cot[...].astype(F32) * slope).astype(BF16)
    for k, to, _ in other_cols():
        send(grads.at[rows(c)], grads.at[rows(c)], gc_s.at[k], gc_r.at[c], b, to)
    hidden_ref[...] = (0.5 * agg * (1.0 + th)).astype(BF16)
    for k, _, src in other_cols():
        arrive(grads.at[rows(src)], gc_s.at[k], gc_r.at[src])

    bstep = 4 * tile if n_blk % 4 == 0 else tile

    def backward(i, _):
        got = dot(adj_t[rows(i, bstep), :], grads[...])
        pg_part[rows(i, bstep), :] = got
        pg16[rows(i, bstep), :] = got.astype(BF16)
        return 0

    lax.fori_loop(0, n_blk * tile // bstep, backward, 0)
    order_out = other_chips() + [(0, chip, chip)]
    for k, to, _ in order_out:
        send(
            pg16.at[rows(2 * to + 1 - core)], pair_in.at[rows(to)],
            pp_s.at[k], pp_r.at[to], sib, c,
        )
    for k, to, _ in order_out[:-1]:
        arrive(pair_in.at[rows(to)], pp_s.at[k], pp_r.at[to])
        both = pg_part[rows(2 * to + core), :] + pair_in[rows(to), :].astype(F32)
        chip_out[rows(to), :] = both.astype(BF16)
        send(
            chip_out.at[rows(to)], chip_in.at[rows(chip)],
            pc_s.at[k], pc_r.at[chip], 2 * to + core, c,
        )
    arrive(pair_in.at[rows(chip)], pp_s.at[0], pp_r.at[chip])
    total = pg_part[rows(b), :] + pair_in[rows(chip), :].astype(F32)
    for k, _, src in other_chips():
        arrive(chip_in.at[rows(src)], pc_s.at[k], pc_r.at[src])
        total = total + chip_in[rows(src), :].astype(F32)
    back = dot(place, total.astype(BF16)).astype(BF16)

    term = dot(feat_t[...], back)
    dw_part[0] = term[:, :half]
    dw_part[1] = term[:, half:]
    dw16[0] = term[:, :half].astype(BF16)
    dw16[1] = term[:, half:].astype(BF16)
    send(dw16.at[1 - core], dw_pair, dp_s.at[0], dp_r.at[0], sib, c)
    xgrad_ref[...] = lax.dot_general(
        back, weight[...], (((1,), (1,)), ((), ())), preferred_element_type=F32
    ).astype(BF16)
    arrive(dw_pair, dp_s.at[0], dp_r.at[0])
    both = dw_part[core] + dw_pair[...].astype(F32)
    dw_sum[...] = both
    dw_sum16[...] = both.astype(BF16)
    r1 = fin // n_chip
    for k, to, _ in other_chips():
        send(
            dw_sum16.at[rows(to, r1)], dw_chip.at[rows(chip, r1)],
            dc_s.at[k], dc_r.at[chip], 2 * to + core, c,
        )
    piece = dw_sum[rows(chip, r1), :]
    for k, _, src in other_chips():
        arrive(dw_chip.at[rows(src, r1)], dc_s.at[k], dc_r.at[src])
        piece = piece + dw_chip[rows(src, r1), :].astype(F32)
    dw_sum[0:r1, :] = piece
    dw_sum16[rows(chip, r1), :] = piece.astype(BF16)
    if r1 % (16 * n_col) == 0:
        r2 = r1 // n_col
        for k, to, _ in other_cols():
            send(
                dw_sum16.at[rows(chip * n_col + to, r2)], dw_col.at[rows(c, r2)],
                dz_s.at[k], dz_r.at[c], b, to,
            )
        piece = dw_sum[rows(c, r2), :]
        for k, _, src in other_cols():
            arrive(dw_col.at[rows(src, r2)], dz_s.at[k], dz_r.at[src])
            piece = piece + dw_col[rows(src, r2), :].astype(F32)
        mine = chip * n_col + c
        dw_all[core, rows(mine, r2), :] = piece.astype(BF16)
        for k, to, _ in other_cols():
            at = dw_all.at[core, rows(mine, r2)]
            send(at, at, dg_s.at[k], dg_r.at[c], b, to)
        for k, _, src in other_cols():
            at = dw_all.at[core, rows(chip * n_col + src, r2)]
            arrive(at, dg_s.at[k], dg_r.at[src])
    else:
        dw_col[rows(c, r1), :] = piece.astype(BF16)
        for k, to, _ in other_cols():
            at = dw_col.at[rows(c, r1)]
            send(at, at, dz_s.at[k], dz_r.at[c], b, to)
        for k, _, src in other_cols():
            arrive(dw_col.at[rows(src, r1)], dz_s.at[k], dz_r.at[src])
        piece = dw_col[0:r1, :].astype(F32)
        for i in range(1, n_col):
            piece = piece + dw_col[i * r1:(i + 1) * r1, :].astype(F32)
        dw_all[core, rows(chip, r1), :] = piece.astype(BF16)
    at = dw_all.at[core, rows(chip, r1)]
    for k, to, _ in other_chips():
        send(at, at, dh_s.at[k], dh_r.at[chip], 2 * to + core, c)
    send(at, at, di_s.at[0], di_r.at[chip], sib, c)
    for k, _, src in other_chips():
        at = dw_all.at[core, rows(src, r1)]
        arrive(at, dh_s.at[k], dh_r.at[src])
        send(at, at, di_s.at[k], di_r.at[src], sib, c)
    for k, _, src in [(0, chip, chip)] + other_chips():
        arrive(dw_all.at[1 - core, rows(src, r1)], di_s.at[k], di_r.at[src])
    wgrad_ref[:, :half] = dw_all[0].astype(F32) * scale
    wgrad_ref[:, half:] = dw_all[1].astype(F32) * scale
    for copy in sends:
        copy.wait_send()


def per_device(features, node_order, weight, cotangent, tile_list, tile_values):
    n_blk, n_col = lax.axis_size("blk"), lax.axis_size("col")
    slots, tile, _ = tile_values.shape
    fin, hid = weight.shape
    n_chip = n_blk // 2
    scale = float(n_blk * n_col * tile) ** -0.5
    r1 = fin // n_chip
    dma = lambda n: pltpu.SemaphoreType.DMA((n,))
    vmem = pltpu.VMEM
    scratch = [
        vmem((tile, fin), BF16), vmem((1, tile), jnp.int32), vmem((fin, hid), BF16),
        vmem((tile, hid), BF16), vmem((slots, tile, tile), BF16),
        vmem((n_col * tile, n_blk * tile), BF16), vmem((n_blk * tile, n_col * tile), BF16),
        vmem((fin, tile), BF16), vmem((n_blk * tile, hid), BF16),
        vmem((n_col * tile, hid), F32), vmem((n_col * tile, hid), BF16),
        vmem((n_col * tile, hid), BF16), vmem((n_col * tile, hid), BF16),
        vmem((n_blk * tile, hid), F32), vmem((n_blk * tile, hid), BF16),
        vmem((n_chip * tile, hid), BF16), vmem((n_chip * tile, hid), BF16),
        vmem((n_chip * tile, hid), BF16),
        vmem((2, fin, hid // 2), F32), vmem((2, fin, hid // 2), BF16),
        vmem((fin, hid // 2), BF16), vmem((fin, hid // 2), F32),
        vmem((fin, hid // 2), BF16), vmem((fin, hid // 2), BF16),
        vmem((n_col * r1, hid // 2), BF16), vmem((2, fin, hid // 2), BF16),
        dma(5), dma(2 * n_chip), dma(n_blk), dma(n_col), dma(n_col), dma(n_col), dma(n_col),
        dma(n_chip), dma(n_chip), dma(n_chip), dma(n_chip),
        dma(1), dma(1), dma(n_chip), dma(n_chip), dma(n_col), dma(n_col),
        dma(n_col), dma(n_col), dma(n_chip), dma(n_chip), dma(n_chip), dma(n_chip),
    ]
    hbm = pl.BlockSpec(memory_space=pl.ANY)
    inside = pl.BlockSpec(memory_space=pltpu.VMEM)
    return pl.pallas_call(
        functools.partial(kernel, (n_blk, n_col, tile, fin, hid), scale),
        out_shape=(
            jax.ShapeDtypeStruct((tile, hid), BF16),
            jax.ShapeDtypeStruct((tile, fin), BF16),
            jax.ShapeDtypeStruct((fin, hid), F32),
        ),
        in_specs=[hbm, hbm, hbm, hbm, pl.BlockSpec(memory_space=pltpu.SMEM), hbm],
        out_specs=(inside, inside, inside),
        scratch_shapes=scratch,
        compiler_params=pltpu.CompilerParams(
            collective_id=0, has_side_effects=True, vmem_limit_bytes=60 * 1024 * 1024
        ),
        cost_estimate=pl.CostEstimate(
            flops=4 * slots * tile * tile * hid, bytes_accessed=4 * 1024 * 1024,
            transcendentals=tile * hid,
        ),
    )(features, node_order, weight, cotangent, tile_list, tile_values)


def solution(mesh):
    in_specs = (
        P(("blk", "col"), None),
        P(("blk", "col"), None),
        P(),
        P(("blk", "col"), None),
        P(("blk", "col"), None),
        P(("blk", "col"), None, None),
    )
    out_specs = (P(("blk", "col"), None), P(("blk", "col"), None), P())
    return jax.shard_map(
        per_device, mesh=mesh, in_specs=in_specs, out_specs=out_specs, check_vma=False
    )
```

```python
import functools

import jax
import jax.numpy as jnp
from jax import lax
from jax.experimental import pallas as pl
from jax.experimental.pallas import tpu as pltpu
from jax.sharding import PartitionSpec as P

SLOTS = 3
MESH = pl.DeviceIdType.MESH
F32 = jnp.float32
BF16 = jnp.bfloat16


def dot(a, b):
    return jnp.dot(a, b, preferred_element_type=F32)


def kernel(
    dims,
    feat_h, order_h, weight_h, cot_h, list_ref, tiles_h,
    hidden_h, xgrad_h, wgrad_h,
    feat, order, weight, cot, tiles, hidden, xgrad,
    adj, adj_t, feat_t, feat_all, panels, part, part16, agg_in, grads, pg_part, pg16,
    pair_in, both16, chip_in, dw_sum, dw16, dw_chip, dw_mid, dw_mid16, dw_col, dw_all,
    in_sem, out_sem, ag_s, ag_r, rc_s, rc_r, gc_s, gc_r, pp_s, pp_r, pc_s, pc_r,
    fe_s, fe_r, dc_s, dc_r, dz_s, dz_r, dg_s, dg_r, dh_s, dh_r, di_s, di_r,
):
    n_blk, n_col, tile, fin, hid, r1, r2 = dims
    n_chip = n_blk // 2
    half = hid // 2
    fhalf = fin // 2
    b = lax.axis_index("blk")
    c = lax.axis_index("col")
    chip = b // 2
    core = b % 2
    sib = b + 1 - 2 * core
    sends = []

    def rows(i, n=tile):
        return pl.ds(pl.multiple_of(i * n, n), n)

    def send(src, dst, s_sem, r_sem, blk, col):
        copy = pltpu.make_async_remote_copy(
            src_ref=src, dst_ref=dst, send_sem=s_sem, recv_sem=r_sem,
            device_id=(blk, col), device_id_type=MESH,
        )
        copy.start()
        sends.append(copy)

    def arrive(dst, s_sem, r_sem):
        pltpu.make_async_remote_copy(
            src_ref=dst, dst_ref=dst, send_sem=s_sem, recv_sem=r_sem,
            device_id=(sib, c), device_id_type=MESH,
        ).wait_recv()

    chips = [(k, (chip + k) % n_chip, (chip + n_chip - k) % n_chip) for k in range(1, n_chip)]
    cols = [(k, (c + k) % n_col, (c + n_col - k) % n_col) for k in range(1, n_col)]

    loads = []
    for i, (src, dst) in enumerate(
        ((feat_h, feat), (weight_h, weight), (order_h, order), (tiles_h, tiles), (cot_h, cot))
    ):
        copy = pltpu.make_async_copy(src, dst, in_sem.at[i])
        copy.start()
        loads.append(copy)

    barrier = pltpu.get_barrier_semaphore()
    peers = [(sib, c)]
    peers += [(2 * to + core, c) for _, to, _ in chips]
    peers += [(2 * to + 1 - core, c) for _, to, _ in chips]
    peers += [(b, to) for _, to, _ in cols]
    for peer in peers:
        pl.semaphore_signal(barrier, inc=1, device_id=peer, device_id_type=MESH)

    loads[0].wait()
    loads[1].wait()
    loads[2].wait()
    place = (
        lax.broadcasted_iota(jnp.int32, (tile, tile), 0) == order[...]
    ).astype(F32).astype(BF16)
    mixed = dot(feat[...], weight[...]).astype(BF16)
    panel = lax.dot_general(
        place, mixed, (((0,), (0,)), ((), ())), preferred_element_type=F32
    ).astype(BF16)
    for h in range(2):
        panels[h, rows(b), :] = panel[:, h * half:(h + 1) * half]
    pl.semaphore_wait(barrier, len(peers))

    for h in range(2):
        at = panels.at[h, rows(b)]
        for k, to, _ in chips:
            send(at, at, ag_s.at[h, k], ag_r.at[h, b], 2 * to + core, c)
        send(at, at, ag_s.at[h, 0], ag_r.at[h, b], sib, c)

    loads[3].wait()

    def build(g, _):
        held = [tiles[g * SLOTS + s] for s in range(SLOTS)]
        ids = [list_ref[0, g * SLOTS + s] - b * n_col for s in range(SLOTS)]
        for r in range(n_col):
            block = jnp.zeros((tile, tile), BF16)
            for t, i in zip(held, ids):
                block = block + jnp.where(i == r, t, jnp.zeros_like(t))
            adj[r * tile:(r + 1) * tile, rows(g)] = block
        return 0

    lax.fori_loop(0, n_blk, build, 0)
    feat_t[...] = lax.dot_general(
        feat[...], place, (((0,), (0,)), ((), ())), preferred_element_type=F32
    ).astype(BF16)
    feat_all[:, rows(b)] = feat_t[rows(core, fhalf), :]

    step = 4 * tile if n_col % 4 == 0 else tile
    for h in range(2):
        for k, _, src in chips:
            at = panels.at[h, rows(2 * src + core)]
            arrive(at, ag_s.at[h, k], ag_r.at[h, 2 * src + core])
            send(at, at, ag_s.at[h, n_chip + k], ag_r.at[h, 2 * src + core], sib, c)
        arrive(panels.at[h, rows(sib)], ag_s.at[h, 0], ag_r.at[h, sib])
        for k, _, src in chips:
            at = 2 * src + 1 - core
            arrive(panels.at[h, rows(at)], ag_s.at[h, k], ag_r.at[h, at])

        def forward(i, _):
            got = dot(adj[rows(i, step), :], panels[h])
            part[h, rows(i, step), :] = got
            part16[h, rows(i, step), :] = got.astype(BF16)
            return 0

        lax.fori_loop(0, n_col * tile // step, forward, 0)
        for k, to, _ in cols:
            send(part16.at[h, rows(to)], agg_in.at[h, rows(c)], rc_s.at[h, k], rc_r.at[h, c], b, to)

    for k, to, _ in chips:
        for q in range(2):
            at = feat_all.at[:, rows(b)]
            send(feat_t.at[pl.ds(q * fhalf, fhalf)], at, fe_s.at[2 * k + q], fe_r.at[b], 2 * to + q, c)
    send(feat_t.at[rows(1 - core, fhalf)], feat_all.at[:, rows(b)], fe_s.at[0], fe_r.at[b], sib, c)

    def turn(g, _):
        for r in range(n_col):
            adj_t[rows(g), r * tile:(r + 1) * tile] = (
                adj[r * tile:(r + 1) * tile, rows(g)].T
            )
        return 0

    turned = adj_t.shape[0] > tile
    if turned:
        lax.fori_loop(0, n_blk, turn, 0)
    loads[4].wait()

    root = 0.7978845608028654
    for h in range(2):
        agg = part[h, rows(c), :]
        for k, _, src in cols:
            arrive(agg_in.at[h, rows(src)], rc_s.at[h, k], rc_r.at[h, src])
            agg = agg + agg_in[h, rows(src), :].astype(F32)
        inner = root * (agg + 0.044715 * agg * agg * agg)
        th = jnp.tanh(inner)
        slope = 0.5 * (1.0 + th) + 0.5 * agg * (1.0 - th * th) * (
            root * (1.0 + 3 * 0.044715 * agg * agg)
        )
        lanes = slice(h * half, (h + 1) * half)
        grads[h, rows(c), :] = (cot[:, lanes].astype(F32) * slope).astype(BF16)
        at = grads.at[h, rows(c)]
        for k, to, _ in cols:
            send(at, at, gc_s.at[h, k], gc_r.at[h, c], b, to)
        hidden[:, lanes] = (0.5 * agg * (1.0 + th)).astype(BF16)
    outs = [pltpu.make_async_copy(hidden, hidden_h, out_sem.at[0])]
    outs[0].start()

    bstep = 4 * tile if n_blk % 4 == 0 else tile
    for h in range(2):
        for k, _, src in cols:
            arrive(grads.at[h, rows(src)], gc_s.at[h, k], gc_r.at[h, src])

        def backward(i, _):
            if turned:
                got = dot(adj_t[rows(i, bstep), :], grads[h])
            else:
                got = lax.dot_general(
                    adj[:, rows(i, bstep)], grads[h], (((0,), (0,)), ((), ())),
                    preferred_element_type=F32,
                )
            pg_part[h, rows(i, bstep), :] = got
            pg16[h, rows(i, bstep), :] = got.astype(BF16)
            return 0

        lax.fori_loop(0, n_blk * tile // bstep, backward, 0)
        send(pg16.at[h], pair_in.at[h], pp_s.at[h], pp_r.at[h], sib, c)

    for k, _, src in chips:
        for q in range(2):
            at = feat_all.at[:, rows(2 * src + q)]
            arrive(at, fe_s.at[0], fe_r.at[2 * src + q])
    arrive(feat_all.at[:, rows(sib)], fe_s.at[0], fe_r.at[sib])

    for h in range(2):
        arrive(pair_in.at[h], pp_s.at[h], pp_r.at[h])
        both16[h] = (pg_part[h] + pair_in[h].astype(F32)).astype(BF16)
        term = dot(feat_all[...], both16[h])
        dw_sum[h, 0:fhalf, :] = term
        dw16[h, 0:fhalf, :] = term.astype(BF16)
        if n_chip * r1 > fhalf:
            rest = jnp.zeros((n_chip * r1 - fhalf, half), F32)
            dw_sum[h, fhalf:, :] = rest
            dw16[h, fhalf:, :] = rest.astype(BF16)
        for k, to, _ in chips:
            send(
                dw16.at[h, rows(to, r1)], dw_chip.at[h, rows(chip, r1)],
                dc_s.at[h, k], dc_r.at[h, chip], 2 * to + core, c,
            )
    for h in range(2):
        for k, to, _ in chips:
            send(
                both16.at[h, rows(2 * to + core)], chip_in.at[h, rows(chip)],
                pc_s.at[h, k], pc_r.at[h, chip], 2 * to + core, c,
            )
    for h in range(2):
        piece = dw_sum[h, rows(chip, r1), :]
        for k, _, src in chips:
            arrive(dw_chip.at[h, rows(src, r1)], dc_s.at[h, k], dc_r.at[h, src])
            piece = piece + dw_chip[h, rows(src, r1), :].astype(F32)
        dw_mid[h, 0:r1, :] = piece
        dw_mid16[h, 0:r1, :] = piece.astype(BF16)
        if n_col * r2 > r1:
            rest = jnp.zeros((n_col * r2 - r1, half), F32)
            dw_mid[h, r1:, :] = rest
            dw_mid16[h, r1:, :] = rest.astype(BF16)
        for k, to, _ in cols:
            send(
                dw_mid16.at[h, rows(to, r2)], dw_col.at[h, rows(c, r2)],
                dz_s.at[h, k], dz_r.at[h, c], b, to,
            )
    for h in range(2):
        piece = dw_mid[h, rows(c, r2), :]
        for k, _, src in cols:
            arrive(dw_col.at[h, rows(src, r2)], dz_s.at[h, k], dz_r.at[h, src])
            piece = piece + dw_col[h, rows(src, r2), :].astype(F32)
        dw_all[core, h, chip, rows(c, r2), :] = piece.astype(BF16)
        at = dw_all.at[core, h, chip, rows(c, r2)]
        for k, to, _ in cols:
            send(at, at, dg_s.at[h, k], dg_r.at[h, c], b, to)

    sums = []
    for h in range(2):
        total = pg_part[h, rows(b), :] + pair_in[h, rows(b), :].astype(F32)
        for k, _, src in chips:
            arrive(chip_in.at[h, rows(src)], pc_s.at[h, k], pc_r.at[h, src])
            total = total + chip_in[h, rows(src), :].astype(F32)
        sums.append(total.astype(BF16))
    back = dot(place, jnp.concatenate(sums, axis=1)).astype(BF16)
    xgrad[...] = lax.dot_general(
        back, weight[...], (((1,), (1,)), ((), ())), preferred_element_type=F32
    ).astype(BF16)
    outs.append(pltpu.make_async_copy(xgrad, xgrad_h, out_sem.at[1]))
    outs[1].start()

    for h in range(2):
        for k, _, src in cols:
            at = dw_all.at[core, h, chip, rows(src, r2)]
            arrive(at, dg_s.at[h, k], dg_r.at[h, src])
        at = dw_all.at[core, h, chip, pl.ds(0, r1)]
        for k, to, _ in chips:
            send(at, at, dh_s.at[h, k], dh_r.at[h, chip], 2 * to + core, c)
        send(at, at, di_s.at[h, 0], di_r.at[h, chip], sib, c)
    for h in range(2):
        for k, _, src in chips:
            at = dw_all.at[core, h, src, pl.ds(0, r1)]
            arrive(at, dh_s.at[h, k], dh_r.at[h, src])
            send(at, at, di_s.at[h, k], di_r.at[h, src], sib, c)
    for h in range(2):
        for k, _, src in [(0, chip, chip)] + chips:
            at = dw_all.at[1 - core, h, src, pl.ds(0, r1)]
            arrive(at, di_s.at[h, k], di_r.at[h, src])
    for copy in sends:
        copy.wait_send()
    outs.append(pltpu.make_async_copy(dw_all.at[:, :, :, pl.ds(0, r1)], wgrad_h, out_sem.at[2]))
    outs[2].start()
    for copy in outs:
        copy.wait()


def finish(scale, r1, hidden_in, xgrad_in, wgrad_in, hidden_ref, xgrad_ref, wgrad_ref):
    hidden_ref[...] = hidden_in[...]
    xgrad_ref[...] = xgrad_in[...]
    _, _, n_chip, _, half = wgrad_in.shape
    fhalf = wgrad_ref.shape[0] // 2
    for core in range(2):
        for chip in range(n_chip):
            count = min(r1, fhalf - chip * r1)
            if count > 0:
                start = core * fhalf + chip * r1
                for h in range(2):
                    wgrad_ref[start:start + count, h * half:(h + 1) * half] = (
                        wgrad_in[core, h, chip, 0:count, :].astype(F32) * scale
                    )


def per_device(features, node_order, weight, cotangent, tile_list, tile_values):
    n_blk, n_col = lax.axis_size("blk"), lax.axis_size("col")
    slots, tile, _ = tile_values.shape
    fin, hid = weight.shape
    n_chip = n_blk // 2
    half, fhalf = hid // 2, fin // 2
    scale = float(n_blk * n_col * tile) ** -0.5
    r1 = -(-fhalf // (16 * n_chip)) * 16
    r2 = -(-r1 // (16 * n_col)) * 16
    dma = lambda *n: pltpu.SemaphoreType.DMA(n)
    vmem = pltpu.VMEM
    wide, tall = n_blk * tile, n_col * tile
    turned = wide * tall <= 2 ** 21
    scratch = [
        vmem((tile, fin), BF16), vmem((1, tile), jnp.int32), vmem((fin, hid), BF16),
        vmem((tile, hid), BF16), vmem((slots, tile, tile), BF16),
        vmem((tile, hid), BF16), vmem((tile, fin), BF16),
        vmem((tall, wide), BF16), vmem((wide if turned else tile, tall), BF16),
        vmem((fin, tile), BF16), vmem((fhalf, wide), BF16),
        vmem((2, wide, half), BF16),
        vmem((2, tall, half), F32), vmem((2, tall, half), BF16), vmem((2, tall, half), BF16),
        vmem((2, tall, half), BF16),
        vmem((2, wide, half), F32), vmem((2, wide, half), BF16), vmem((2, wide, half), BF16),
        vmem((2, wide, half), BF16), vmem((2, n_chip * tile, half), BF16),
        vmem((2, n_chip * r1, half), F32), vmem((2, n_chip * r1, half), BF16),
        vmem((2, n_chip * r1, half), BF16),
        vmem((2, n_col * r2, half), F32), vmem((2, n_col * r2, half), BF16),
        vmem((2, n_col * r2, half), BF16), vmem((2, 2, n_chip, n_col * r2, half), BF16),
        dma(5), dma(3), dma(2, 2 * n_chip), dma(2, n_blk),
        dma(2, n_col), dma(2, n_col), dma(2, n_col), dma(2, n_col),
        dma(2), dma(2), dma(2, n_chip), dma(2, n_chip),
        dma(2 * n_chip), dma(n_blk), dma(2, n_chip), dma(2, n_chip),
        dma(2, n_col), dma(2, n_col), dma(2, n_col), dma(2, n_col),
        dma(2, n_chip), dma(2, n_chip), dma(2, n_chip), dma(2, n_chip),
    ]
    hbm = pl.BlockSpec(memory_space=pl.ANY)
    inside = pl.BlockSpec(memory_space=pltpu.VMEM)
    limit = 60 * 1024 * 1024
    hidden, xgrad, wgrad = pl.pallas_call(
        functools.partial(kernel, (n_blk, n_col, tile, fin, hid, r1, r2)),
        out_shape=(
            jax.ShapeDtypeStruct((tile, hid), BF16),
            jax.ShapeDtypeStruct((tile, fin), BF16),
            jax.ShapeDtypeStruct((2, 2, n_chip, r1, half), BF16),
        ),
        in_specs=[hbm, hbm, hbm, hbm, pl.BlockSpec(memory_space=pltpu.SMEM), hbm],
        out_specs=(hbm, hbm, hbm),
        scratch_shapes=scratch,
        compiler_params=pltpu.CompilerParams(
            collective_id=0, has_side_effects=True, vmem_limit_bytes=limit
        ),
        cost_estimate=pl.CostEstimate(
            flops=4 * slots * tile * tile * hid, bytes_accessed=4 * 1024 * 1024,
            transcendentals=tile * hid,
        ),
    )(features, node_order, weight, cotangent, tile_list.T, tile_values)
    return pl.pallas_call(
        functools.partial(finish, scale, r1),
        out_shape=(
            jax.ShapeDtypeStruct((tile, hid), BF16),
            jax.ShapeDtypeStruct((tile, fin), BF16),
            jax.ShapeDtypeStruct((fin, hid), F32),
        ),
        in_specs=[inside] * 3,
        out_specs=(inside,) * 3,
        compiler_params=pltpu.CompilerParams(vmem_limit_bytes=limit),
    )(hidden, xgrad, wgrad)


def solution(mesh):
    in_specs = (
        P(("blk", "col"), None),
        P(("blk", "col"), None),
        P(),
        P(("blk", "col"), None),
        P(("blk", "col"), None),
        P(("blk", "col"), None, None),
    )
    out_specs = (P(("blk", "col"), None), P(("blk", "col"), None), P())
    return jax.shard_map(
        per_device, mesh=mesh, in_specs=in_specs, out_specs=out_specs, check_vma=False
    )
```

```python
import functools

import jax
import jax.numpy as jnp
from jax import lax
from jax.experimental import pallas as pl
from jax.experimental.pallas import tpu as pltpu
from jax.sharding import PartitionSpec as P

SLOTS = 3
MESH = pl.DeviceIdType.MESH
F32 = jnp.float32
BF16 = jnp.bfloat16


def dot(a, b):
    return jnp.dot(a, b, preferred_element_type=F32)


def kernel(
    dims,
    feat_h, order_h, weight_h, cot_h, list_ref, tiles_h,
    hidden_h, xgrad_h, wgrad_h,
    feat, order, weight, cot, tiles, hidden, xgrad,
    adj, adj_t, feat_t, feat_all, panels, part, part16, agg_in, grads, pg_part, pg16,
    pair_in, both16, chip_in, dw_sum, dw16, dw_in, dw_mid, dw_mid16, dw_col, dw_all,
    in_sem, out_sem, ag_s, ag_r, rc_s, rc_r, gc_s, gc_r, pp_s, pp_r, pc_s, pc_r,
    fe_s, fe_r, dc_s, dc_r, dz_s, dz_r, dg_s, dg_r, dh_s, dh_r, di_s, di_r,
):
    n_blk, n_col, tile, fin, hid, r1, r2, direct = dims
    n_chip = n_blk // 2
    half = hid // 2
    fhalf = fin // 2
    n_own = fhalf // r1
    b = lax.axis_index("blk")
    c = lax.axis_index("col")
    chip = b // 2
    core = b % 2
    sib = b + 1 - 2 * core
    sends = []

    def rows(i, n=tile):
        return pl.ds(pl.multiple_of(i * n, n), n)

    def send(src, dst, s_sem, r_sem, blk, col, only=None):
        copy = pltpu.make_async_remote_copy(
            src_ref=src, dst_ref=dst, send_sem=s_sem, recv_sem=r_sem,
            device_id=(blk, col), device_id_type=MESH,
        )
        if only is None:
            copy.start()
        else:
            pl.when(only)(copy.start)
        sends.append((copy, only))

    def arrive(dst, s_sem, r_sem):
        pltpu.make_async_remote_copy(
            src_ref=dst, dst_ref=dst, send_sem=s_sem, recv_sem=r_sem,
            device_id=(sib, c), device_id_type=MESH,
        ).wait_recv()

    chips = [(k, (chip + k) % n_chip, (chip + n_chip - k) % n_chip) for k in range(1, n_chip)]
    cols = [(k, (c + k) % n_col, (c + n_col - k) % n_col) for k in range(1, n_col)]

    loads = []
    for i, (src, dst) in enumerate(
        ((feat_h, feat), (weight_h, weight), (order_h, order), (tiles_h, tiles), (cot_h, cot))
    ):
        copy = pltpu.make_async_copy(src, dst, in_sem.at[i])
        copy.start()
        loads.append(copy)

    barrier = pltpu.get_barrier_semaphore()
    peers = [(sib, c)]
    peers += [(2 * to + core, c) for _, to, _ in chips]
    peers += [(2 * to + 1 - core, c) for _, to, _ in chips]
    peers += [(b, to) for _, to, _ in cols]
    if direct:
        peers += [(2 * to + core, at) for _, to, _ in chips for _, at, _ in cols]
    for peer in peers:
        pl.semaphore_signal(barrier, inc=1, device_id=peer, device_id_type=MESH)

    loads[0].wait()
    loads[1].wait()
    loads[2].wait()
    place = (
        lax.broadcasted_iota(jnp.int32, (tile, tile), 0) == order[...]
    ).astype(F32).astype(BF16)
    mixed = dot(feat[...], weight[...]).astype(BF16)
    panel = lax.dot_general(
        place, mixed, (((0,), (0,)), ((), ())), preferred_element_type=F32
    ).astype(BF16)
    for h in range(2):
        panels[h, rows(b), :] = panel[:, h * half:(h + 1) * half]
    pl.semaphore_wait(barrier, len(peers))

    for h in range(2):
        at = panels.at[h, rows(b)]
        for k, to, _ in chips:
            send(at, at, ag_s.at[h, k], ag_r.at[h, b], 2 * to + core, c)
        send(at, at, ag_s.at[h, 0], ag_r.at[h, b], sib, c)

    loads[3].wait()

    def build(g, _):
        held = [tiles[g * SLOTS + s] for s in range(SLOTS)]
        ids = [list_ref[0, g * SLOTS + s] - b * n_col for s in range(SLOTS)]
        for r in range(n_col):
            block = jnp.zeros((tile, tile), BF16)
            for t, i in zip(held, ids):
                block = block + jnp.where(i == r, t, jnp.zeros_like(t))
            adj[r * tile:(r + 1) * tile, rows(g)] = block
        return 0

    lax.fori_loop(0, n_blk, build, 0)
    feat_t[...] = lax.dot_general(
        feat[...], place, (((0,), (0,)), ((), ())), preferred_element_type=F32
    ).astype(BF16)
    feat_all[:, rows(b)] = feat_t[rows(core, fhalf), :]

    step = 4 * tile if n_col % 4 == 0 else tile
    for h in range(2):
        for k, _, src in chips:
            at = panels.at[h, rows(2 * src + core)]
            arrive(at, ag_s.at[h, k], ag_r.at[h, 2 * src + core])
            send(at, at, ag_s.at[h, n_chip + k], ag_r.at[h, 2 * src + core], sib, c)
        arrive(panels.at[h, rows(sib)], ag_s.at[h, 0], ag_r.at[h, sib])
        for k, _, src in chips:
            at = 2 * src + 1 - core
            arrive(panels.at[h, rows(at)], ag_s.at[h, k], ag_r.at[h, at])

        def forward(i, _):
            got = dot(adj[rows(i, step), :], panels[h])
            part[h, rows(i, step), :] = got
            part16[h, rows(i, step), :] = got.astype(BF16)
            return 0

        lax.fori_loop(0, n_col * tile // step, forward, 0)
        for k, to, _ in cols:
            send(part16.at[h, rows(to)], agg_in.at[h, rows(c)], rc_s.at[h, k], rc_r.at[h, c], b, to)

    for k, to, _ in chips:
        for q in range(2):
            at = feat_all.at[:, rows(b)]
            send(feat_t.at[pl.ds(q * fhalf, fhalf)], at, fe_s.at[2 * k + q], fe_r.at[b], 2 * to + q, c)
    send(feat_t.at[rows(1 - core, fhalf)], feat_all.at[:, rows(b)], fe_s.at[0], fe_r.at[b], sib, c)

    def turn(g, _):
        for r in range(n_col):
            adj_t[rows(g), r * tile:(r + 1) * tile] = (
                adj[r * tile:(r + 1) * tile, rows(g)].T
            )
        return 0

    turned = adj_t.shape[0] > tile
    if turned:
        lax.fori_loop(0, n_blk, turn, 0)
    loads[4].wait()

    root = 0.7978845608028654
    for h in range(2):
        agg = part[h, rows(c), :]
        for k, _, src in cols:
            arrive(agg_in.at[h, rows(src)], rc_s.at[h, k], rc_r.at[h, src])
            agg = agg + agg_in[h, rows(src), :].astype(F32)
        inner = root * (agg + 0.044715 * agg * agg * agg)
        th = jnp.tanh(inner)
        slope = 0.5 * (1.0 + th) + 0.5 * agg * (1.0 - th * th) * (
            root * (1.0 + 3 * 0.044715 * agg * agg)
        )
        lanes = slice(h * half, (h + 1) * half)
        grads[h, rows(c), :] = (cot[:, lanes].astype(F32) * slope).astype(BF16)
        at = grads.at[h, rows(c)]
        for k, to, _ in cols:
            send(at, at, gc_s.at[h, k], gc_r.at[h, c], b, to)
        hidden[:, lanes] = (0.5 * agg * (1.0 + th)).astype(BF16)
    outs = [pltpu.make_async_copy(hidden, hidden_h, out_sem.at[0])]
    outs[0].start()

    bstep = 4 * tile if n_blk % 4 == 0 else tile
    others = [
        ((chip + i) % n_chip, (c + j) % n_col, (chip + n_chip - i) % n_chip, (c + n_col - j) % n_col)
        for i in range(n_chip) for j in range(n_col) if i + j > 0
    ]
    mine = chip * n_col + c

    def pair_start(h):
        for k, _, src in cols:
            arrive(grads.at[h, rows(src)], gc_s.at[h, k], gc_r.at[h, src])

        def backward(i, _):
            if turned:
                got = dot(adj_t[rows(i, bstep), :], grads[h])
            else:
                got = lax.dot_general(
                    adj[:, rows(i, bstep)], grads[h], (((0,), (0,)), ((), ())),
                    preferred_element_type=F32,
                )
            pg_part[h, rows(i, bstep), :] = got
            pg16[h, rows(i, bstep), :] = got.astype(BF16)
            return 0

        lax.fori_loop(0, n_blk * tile // bstep, backward, 0)
        send(pg16.at[h], pair_in.at[h], pp_s.at[h], pp_r.at[h], sib, c)

    def features_arrive():
        for k, _, src in chips:
            for q in range(2):
                at = feat_all.at[:, rows(2 * src + q)]
                arrive(at, fe_s.at[0], fe_r.at[2 * src + q])
        arrive(feat_all.at[:, rows(sib)], fe_s.at[0], fe_r.at[sib])

    def terms_start(h):
        arrive(pair_in.at[h], pp_s.at[h], pp_r.at[h])
        both16[h] = (pg_part[h] + pair_in[h].astype(F32)).astype(BF16)
        term = dot(feat_all[...], both16[h])
        dw_sum[h, 0:fhalf, :] = term
        dw16[h, 0:fhalf, :] = term.astype(BF16)
        if direct:
            for i, (to, to_col, _, _) in enumerate(others):
                owner = to * n_col + to_col
                send(
                    dw16.at[h, rows(owner, r1)], dw_in.at[h, rows(mine, r1)],
                    dc_s.at[h, i], dc_r.at[h, mine], 2 * to + core, to_col, owner < n_own,
                )
            return
        if n_chip * r1 > fhalf:
            rest = jnp.zeros((n_chip * r1 - fhalf, half), F32)
            dw_sum[h, fhalf:, :] = rest
            dw16[h, fhalf:, :] = rest.astype(BF16)
        for k, to, _ in chips:
            send(
                dw16.at[h, rows(to, r1)], dw_in.at[h, rows(chip, r1)],
                dc_s.at[h, k], dc_r.at[h, chip], 2 * to + core, c,
            )

    def owners_start(h):
        for k, to, _ in chips:
            send(
                both16.at[h, rows(2 * to + core)], chip_in.at[h, rows(chip)],
                pc_s.at[h, k], pc_r.at[h, chip], 2 * to + core, c,
            )

    def result_start(h):
        if direct:
            @pl.when(mine < n_own)
            def _():
                piece = dw_sum[h, rows(mine, r1), :]
                for i, (_, _, src, src_col) in enumerate(others):
                    at = src * n_col + src_col
                    arrive(dw_in.at[h, rows(at, r1)], dc_s.at[h, i], dc_r.at[h, at])
                    piece = piece + dw_in[h, rows(at, r1), :].astype(F32)
                dw_all[core, h, rows(mine, r1), :] = piece.astype(BF16)

            at = dw_all.at[core, h, rows(mine, r1)]
            for i, (to, to_col, _, _) in enumerate(others):
                send(at, at, dg_s.at[h, i], dg_r.at[h, mine], 2 * to + core, to_col, mine < n_own)
            send(at, at, di_s.at[h, mine], di_r.at[h, mine], sib, c, mine < n_own)
            return
        piece = dw_sum[h, rows(chip, r1), :]
        for k, _, src in chips:
            arrive(dw_in.at[h, rows(src, r1)], dc_s.at[h, k], dc_r.at[h, src])
            piece = piece + dw_in[h, rows(src, r1), :].astype(F32)
        dw_mid[h, 0:r1, :] = piece
        dw_mid16[h, 0:r1, :] = piece.astype(BF16)
        if n_col * r2 > r1:
            rest = jnp.zeros((n_col * r2 - r1, half), F32)
            dw_mid[h, r1:, :] = rest
            dw_mid16[h, r1:, :] = rest.astype(BF16)
        for k, to, _ in cols:
            send(
                dw_mid16.at[h, rows(to, r2)], dw_col.at[h, rows(c, r2)],
                dz_s.at[h, k], dz_r.at[h, c], b, to,
            )
        piece = dw_mid[h, rows(c, r2), :]
        for k, _, src in cols:
            arrive(dw_col.at[h, rows(src, r2)], dz_s.at[h, k], dz_r.at[h, src])
            piece = piece + dw_col[h, rows(src, r2), :].astype(F32)
        dw_all[core, h, chip, rows(c, r2), :] = piece.astype(BF16)
        at = dw_all.at[core, h, chip, rows(c, r2)]
        for k, to, _ in cols:
            send(at, at, dg_s.at[h, k], dg_r.at[h, c], b, to)
        for k, _, src in cols:
            at = dw_all.at[core, h, chip, rows(src, r2)]
            arrive(at, dg_s.at[h, k], dg_r.at[h, src])
        at = dw_all.at[core, h, chip, pl.ds(0, r1)]
        for k, to, _ in chips:
            send(at, at, dh_s.at[h, k], dh_r.at[h, chip], 2 * to + core, c)
        send(at, at, di_s.at[h, chip], di_r.at[h, chip], sib, c)

    def result_pass(h):
        if direct:
            for i, (_, _, src, src_col) in enumerate(others):
                owner = src * n_col + src_col
                at = dw_all.at[core, h, rows(owner, r1)]

                @pl.when(owner < n_own)
                def _():
                    arrive(at, dg_s.at[h, i], dg_r.at[h, owner])

                send(at, at, di_s.at[h, owner], di_r.at[h, owner], sib, c, owner < n_own)
            return
        for k, _, src in chips:
            at = dw_all.at[core, h, src, pl.ds(0, r1)]
            arrive(at, dh_s.at[h, k], dh_r.at[h, src])
            send(at, at, di_s.at[h, src], di_r.at[h, src], sib, c)

    def result_arrive(h):
        if direct:
            for owner in range(n_own):
                at = dw_all.at[1 - core, h, rows(owner, r1)]
                arrive(at, di_s.at[h, owner], di_r.at[h, owner])
            return
        for src in range(n_chip):
            at = dw_all.at[1 - core, h, src, pl.ds(0, r1)]
            arrive(at, di_s.at[h, src], di_r.at[h, src])

    def own_features():
        sums = []
        for h in range(2):
            total = pg_part[h, rows(b), :] + pair_in[h, rows(b), :].astype(F32)
            for k, _, src in chips:
                arrive(chip_in.at[h, rows(src)], pc_s.at[h, k], pc_r.at[h, src])
                total = total + chip_in[h, rows(src), :].astype(F32)
            sums.append(total.astype(BF16))
        back = dot(place, jnp.concatenate(sums, axis=1)).astype(BF16)
        xgrad[...] = lax.dot_general(
            back, weight[...], (((1,), (1,)), ((), ())), preferred_element_type=F32
        ).astype(BF16)
        outs.append(pltpu.make_async_copy(xgrad, xgrad_h, out_sem.at[1]))
        outs[1].start()

    pair_start(0)
    features_arrive()
    terms_start(0)
    owners_start(0)
    pair_start(1)
    result_start(0)
    terms_start(1)
    owners_start(1)
    result_pass(0)
    result_start(1)
    own_features()
    result_pass(1)
    result_arrive(0)
    result_arrive(1)
    if direct:
        outs.append(pltpu.make_async_copy(dw_all, wgrad_h, out_sem.at[2]))
    else:
        outs.append(
            pltpu.make_async_copy(dw_all.at[:, :, :, pl.ds(0, r1)], wgrad_h, out_sem.at[2])
        )
    outs[2].start()
    for copy, only in sends:
        if only is None:
            copy.wait_send()
        else:
            pl.when(only)(copy.wait_send)
    for copy in outs:
        copy.wait()


def finish(scale, r1, hidden_in, xgrad_in, wgrad_in, hidden_ref, xgrad_ref, wgrad_ref):
    hidden_ref[...] = hidden_in[...]
    xgrad_ref[...] = xgrad_in[...]
    n_part, half = wgrad_in.shape[2], wgrad_in.shape[4]
    fhalf = wgrad_ref.shape[0] // 2
    for core in range(2):
        for i in range(n_part):
            count = min(r1, fhalf - i * r1)
            if count > 0:
                start = core * fhalf + i * r1
                for h in range(2):
                    wgrad_ref[start:start + count, h * half:(h + 1) * half] = (
                        wgrad_in[core, h, i, 0:count, :].astype(F32) * scale
                    )


def per_device(features, node_order, weight, cotangent, tile_list, tile_values):
    n_blk, n_col = lax.axis_size("blk"), lax.axis_size("col")
    slots, tile, _ = tile_values.shape
    fin, hid = weight.shape
    n_chip = n_blk // 2
    half, fhalf = hid // 2, fin // 2
    scale = float(n_blk * n_col * tile) ** -0.5
    direct = n_chip * n_col <= 16
    n_sum = n_chip * n_col if direct else n_chip
    r1 = -(-fhalf // (16 * n_sum)) * 16
    direct = direct and fhalf % r1 == 0
    r2 = 16 if direct else -(-r1 // (16 * n_col)) * 16
    padded = fhalf if direct else n_chip * r1
    dma = lambda *n: pltpu.SemaphoreType.DMA(n)
    vmem = pltpu.VMEM
    wide, tall = n_blk * tile, n_col * tile
    turned = wide * tall <= 2 ** 21
    scratch = [
        vmem((tile, fin), BF16), vmem((1, tile), jnp.int32), vmem((fin, hid), BF16),
        vmem((tile, hid), BF16), vmem((slots, tile, tile), BF16),
        vmem((tile, hid), BF16), vmem((tile, fin), BF16),
        vmem((tall, wide), BF16), vmem((wide if turned else tile, tall), BF16),
        vmem((fin, tile), BF16), vmem((fhalf, wide), BF16),
        vmem((2, wide, half), BF16),
        vmem((2, tall, half), F32), vmem((2, tall, half), BF16), vmem((2, tall, half), BF16),
        vmem((2, tall, half), BF16),
        vmem((2, wide, half), F32), vmem((2, wide, half), BF16), vmem((2, wide, half), BF16),
        vmem((2, wide, half), BF16), vmem((2, n_chip * tile, half), BF16),
        vmem((2, padded, half), F32), vmem((2, padded, half), BF16),
        vmem((2, n_sum * r1, half), BF16),
        vmem((2, n_col * r2, half), F32), vmem((2, n_col * r2, half), BF16),
        vmem((2, n_col * r2, half), BF16), vmem((2, 2, fhalf, half) if direct else (2, 2, n_chip, n_col * r2, half), BF16),
        dma(5), dma(3), dma(2, 2 * n_chip), dma(2, n_blk),
        dma(2, n_col), dma(2, n_col), dma(2, n_col), dma(2, n_col),
        dma(2), dma(2), dma(2, n_chip), dma(2, n_chip),
        dma(2 * n_chip), dma(n_blk), dma(2, n_sum), dma(2, n_sum),
        dma(2, n_col), dma(2, n_col), dma(2, n_sum + n_col), dma(2, n_sum + n_col),
        dma(2, n_chip), dma(2, n_chip), dma(2, n_sum), dma(2, n_sum),
    ]
    far = pl.BlockSpec(memory_space=pltpu.HBM)
    free = pl.BlockSpec(memory_space=pl.ANY)
    inside = pl.BlockSpec(memory_space=pltpu.VMEM)
    limit = 60 * 1024 * 1024
    hidden, xgrad, wgrad = pl.pallas_call(
        functools.partial(kernel, (n_blk, n_col, tile, fin, hid, r1, r2, direct)),
        out_shape=(
            jax.ShapeDtypeStruct((tile, hid), BF16),
            jax.ShapeDtypeStruct((tile, fin), BF16),
            jax.ShapeDtypeStruct(
                (2, 2, fhalf, half) if direct else (2, 2, n_chip, r1, half), BF16
            ),
        ),
        in_specs=[far, far, far, far, pl.BlockSpec(memory_space=pltpu.SMEM), far],
        out_specs=(free, free, free),
        scratch_shapes=scratch,
        compiler_params=pltpu.CompilerParams(
            collective_id=0, has_side_effects=True, vmem_limit_bytes=limit
        ),
        cost_estimate=pl.CostEstimate(
            flops=4 * slots * tile * tile * hid, bytes_accessed=4 * 1024 * 1024,
            transcendentals=tile * hid,
        ),
    )(features, node_order, weight, cotangent, tile_list.T, tile_values)
    if direct:
        wgrad, r1 = wgrad.reshape(2, 2, 1, fhalf, half), fhalf
    return pl.pallas_call(
        functools.partial(finish, scale, r1),
        out_shape=(
            jax.ShapeDtypeStruct((tile, hid), BF16),
            jax.ShapeDtypeStruct((tile, fin), BF16),
            jax.ShapeDtypeStruct((fin, hid), F32),
        ),
        in_specs=[inside] * 3,
        out_specs=(inside,) * 3,
        compiler_params=pltpu.CompilerParams(vmem_limit_bytes=limit),
    )(hidden, xgrad, wgrad)


def solution(mesh):
    in_specs = (
        P(("blk", "col"), None),
        P(("blk", "col"), None),
        P(),
        P(("blk", "col"), None),
        P(("blk", "col"), None),
        P(("blk", "col"), None, None),
    )
    out_specs = (P(("blk", "col"), None), P(("blk", "col"), None), P())
    return jax.shard_map(
        per_device, mesh=mesh, in_specs=in_specs, out_specs=out_specs, check_vma=False
    )
```

```python
import functools

import jax
import jax.numpy as jnp
from jax import lax
from jax.experimental import pallas as pl
from jax.experimental.pallas import tpu as pltpu
from jax.sharding import PartitionSpec as P

SLOTS = 3
MESH = pl.DeviceIdType.MESH
F32 = jnp.float32
BF16 = jnp.bfloat16


def dot(a, b):
    return jnp.dot(a, b, preferred_element_type=F32)


def kernel(
    dims,
    feat_h, order_h, weight_h, cot_h, list_ref, tiles_h,
    hidden_h, xgrad_h, wgrad_h,
    feat, order, weight, cot, tiles, hidden, xgrad,
    adj, adj_t, feat_t, feat_all, panels, part, part16, agg_in, grads, pg_part, pg16,
    pair_in, both16, chip_in, dw_sum, dw16, dw_in, dw_mid, dw_mid16, dw_col, dw_all,
    in_sem, out_sem, ag_s, ag_r, rc_s, rc_r, gc_s, gc_r, pp_s, pp_r, pc_s, pc_r,
    fe_s, fe_r, dc_s, dc_r, dz_s, dz_r, dg_s, dg_r, dh_s, dh_r, di_s, di_r,
):
    n_blk, n_col, tile, fin, hid, r1, r2, direct = dims
    n_chip = n_blk // 2
    half = hid // 2
    fhalf = fin // 2
    n_own = fhalf // r1
    b = lax.axis_index("blk")
    c = lax.axis_index("col")
    chip = b // 2
    core = b % 2
    sib = b + 1 - 2 * core
    sends = []

    def rows(i, n=tile):
        return pl.ds(pl.multiple_of(i * n, n), n)

    def send(src, dst, s_sem, r_sem, blk, col, only=None):
        copy = pltpu.make_async_remote_copy(
            src_ref=src, dst_ref=dst, send_sem=s_sem, recv_sem=r_sem,
            device_id=(blk, col), device_id_type=MESH,
        )
        if only is None:
            copy.start()
        else:
            pl.when(only)(copy.start)
        sends.append((copy, only))

    def arrive(dst, s_sem, r_sem):
        pltpu.make_async_remote_copy(
            src_ref=dst, dst_ref=dst, send_sem=s_sem, recv_sem=r_sem,
            device_id=(sib, c), device_id_type=MESH,
        ).wait_recv()

    chips = [(k, (chip + k) % n_chip, (chip + n_chip - k) % n_chip) for k in range(1, n_chip)]
    cols = [(k, (c + k) % n_col, (c + n_col - k) % n_col) for k in range(1, n_col)]

    loads = []
    for i, (src, dst) in enumerate(
        ((feat_h, feat), (weight_h, weight), (order_h, order), (tiles_h, tiles), (cot_h, cot))
    ):
        copy = pltpu.make_async_copy(src, dst, in_sem.at[i])
        copy.start()
        loads.append(copy)

    barrier = pltpu.get_barrier_semaphore()
    peers = [(sib, c)]
    peers += [(2 * to + core, c) for _, to, _ in chips]
    peers += [(2 * to + 1 - core, c) for _, to, _ in chips]
    peers += [(b, to) for _, to, _ in cols]
    if direct:
        peers += [(2 * to + core, at) for _, to, _ in chips for _, at, _ in cols]
    for peer in peers:
        pl.semaphore_signal(barrier, inc=1, device_id=peer, device_id_type=MESH)

    loads[0].wait()
    loads[1].wait()
    loads[2].wait()
    place = (
        lax.broadcasted_iota(jnp.int32, (tile, tile), 0) == order[...]
    ).astype(F32).astype(BF16)
    mixed = dot(feat[...], weight[...]).astype(BF16)
    panel = lax.dot_general(
        place, mixed, (((0,), (0,)), ((), ())), preferred_element_type=F32
    ).astype(BF16)
    for h in range(2):
        panels[h, rows(b), :] = panel[:, h * half:(h + 1) * half]
    pl.semaphore_wait(barrier, len(peers))

    for h in range(2):
        at = panels.at[h, rows(b)]
        for k, to, _ in chips:
            send(at, at, ag_s.at[h, k], ag_r.at[h, b], 2 * to + core, c)
        send(at, at, ag_s.at[h, 0], ag_r.at[h, b], sib, c)

    loads[3].wait()

    def build(g, _):
        held = [tiles[g * SLOTS + s] for s in range(SLOTS)]
        ids = [list_ref[0, g * SLOTS + s] - b * n_col for s in range(SLOTS)]
        for r in range(n_col):
            block = jnp.zeros((tile, tile), BF16)
            for t, i in zip(held, ids):
                block = block + jnp.where(i == r, t, jnp.zeros_like(t))
            adj[r * tile:(r + 1) * tile, rows(g)] = block
        return 0

    lax.fori_loop(0, n_blk, build, 0)
    feat_t[...] = lax.dot_general(
        feat[...], place, (((0,), (0,)), ((), ())), preferred_element_type=F32
    ).astype(BF16)
    feat_all[:, rows(b)] = feat_t[rows(core, fhalf), :]

    step = 4 * tile if n_col % 4 == 0 else tile
    for h in range(2):
        for k, _, src in chips:
            at = panels.at[h, rows(2 * src + core)]
            arrive(at, ag_s.at[h, k], ag_r.at[h, 2 * src + core])
            send(at, at, ag_s.at[h, n_chip + k], ag_r.at[h, 2 * src + core], sib, c)
        arrive(panels.at[h, rows(sib)], ag_s.at[h, 0], ag_r.at[h, sib])
        for k, _, src in chips:
            at = 2 * src + 1 - core
            arrive(panels.at[h, rows(at)], ag_s.at[h, k], ag_r.at[h, at])

        def forward(i, _):
            got = dot(adj[rows(i, step), :], panels[h])
            part[h, rows(i, step), :] = got
            part16[h, rows(i, step), :] = got.astype(BF16)
            return 0

        lax.fori_loop(0, n_col * tile // step, forward, 0)
        for k, to, _ in cols:
            send(part16.at[h, rows(to)], agg_in.at[h, rows(c)], rc_s.at[h, k], rc_r.at[h, c], b, to)

    for k, to, _ in chips:
        for q in range(2):
            at = feat_all.at[:, rows(b)]
            send(feat_t.at[pl.ds(q * fhalf, fhalf)], at, fe_s.at[2 * k + q], fe_r.at[b], 2 * to + q, c)
    send(feat_t.at[rows(1 - core, fhalf)], feat_all.at[:, rows(b)], fe_s.at[0], fe_r.at[b], sib, c)

    def turn(g, _):
        for r in range(n_col):
            adj_t[rows(g), r * tile:(r + 1) * tile] = (
                adj[r * tile:(r + 1) * tile, rows(g)].T
            )
        return 0

    turned = adj_t.shape[0] > tile
    if turned:
        lax.fori_loop(0, n_blk, turn, 0)
    loads[4].wait()

    root = 0.7978845608028654
    for h in range(2):
        agg = part[h, rows(c), :]
        for k, _, src in cols:
            arrive(agg_in.at[h, rows(src)], rc_s.at[h, k], rc_r.at[h, src])
            agg = agg + agg_in[h, rows(src), :].astype(F32)
        inner = root * (agg + 0.044715 * agg * agg * agg)
        th = jnp.tanh(inner)
        slope = 0.5 * (1.0 + th) + 0.5 * agg * (1.0 - th * th) * (
            root * (1.0 + 3 * 0.044715 * agg * agg)
        )
        lanes = slice(h * half, (h + 1) * half)
        grads[h, rows(c), :] = (cot[:, lanes].astype(F32) * slope).astype(BF16)
        at = grads.at[h, rows(c)]
        for k, to, _ in cols:
            send(at, at, gc_s.at[h, k], gc_r.at[h, c], b, to)
        hidden[:, lanes] = (0.5 * agg * (1.0 + th)).astype(BF16)
    outs = [pltpu.make_async_copy(hidden, hidden_h, out_sem.at[0])]
    outs[0].start()

    bstep = 4 * tile if n_blk % 4 == 0 else tile
    others = [
        ((chip + i) % n_chip, (c + j) % n_col, (chip + n_chip - i) % n_chip, (c + n_col - j) % n_col)
        for i in range(n_chip) for j in range(n_col) if i + j > 0
    ]
    mine = chip * n_col + c

    def pair_start(h):
        for k, _, src in cols:
            arrive(grads.at[h, rows(src)], gc_s.at[h, k], gc_r.at[h, src])

        def backward(i, _):
            if turned:
                got = dot(adj_t[rows(i, bstep), :], grads[h])
            else:
                got = lax.dot_general(
                    adj[:, rows(i, bstep)], grads[h], (((0,), (0,)), ((), ())),
                    preferred_element_type=F32,
                )
            pg_part[h, rows(i, bstep), :] = got
            pg16[h, rows(i, bstep), :] = got.astype(BF16)
            return 0

        lax.fori_loop(0, n_blk * tile // bstep, backward, 0)
        send(pg16.at[h], pair_in.at[h], pp_s.at[h], pp_r.at[h], sib, c)

    def features_arrive():
        for k, _, src in chips:
            for q in range(2):
                at = feat_all.at[:, rows(2 * src + q)]
                arrive(at, fe_s.at[0], fe_r.at[2 * src + q])
        arrive(feat_all.at[:, rows(sib)], fe_s.at[0], fe_r.at[sib])

    def terms_start(h):
        arrive(pair_in.at[h], pp_s.at[h], pp_r.at[h])
        both16[h] = (pg_part[h] + pair_in[h].astype(F32)).astype(BF16)
        term = dot(feat_all[...], both16[h])
        dw_sum[h, 0:fhalf, :] = term
        dw16[h, 0:fhalf, :] = term.astype(BF16)
        if direct:
            for i, (to, to_col, _, _) in enumerate(others):
                owner = to * n_col + to_col
                send(
                    dw16.at[h, rows(owner, r1)], dw_in.at[h, rows(mine, r1)],
                    dc_s.at[h, i], dc_r.at[h, mine], 2 * to + core, to_col, owner < n_own,
                )
            return
        if n_chip * r1 > fhalf:
            rest = jnp.zeros((n_chip * r1 - fhalf, half), F32)
            dw_sum[h, fhalf:, :] = rest
            dw16[h, fhalf:, :] = rest.astype(BF16)
        for k, to, _ in chips:
            send(
                dw16.at[h, rows(to, r1)], dw_in.at[h, rows(chip, r1)],
                dc_s.at[h, k], dc_r.at[h, chip], 2 * to + core, c,
            )

    def owners_start(h):
        for k, to, _ in chips:
            send(
                both16.at[h, rows(2 * to + core)], chip_in.at[h, rows(chip)],
                pc_s.at[h, k], pc_r.at[h, chip], 2 * to + core, c,
            )

    def result_start(h):
        if direct:
            @pl.when(mine < n_own)
            def _():
                piece = dw_sum[h, rows(mine, r1), :]
                for i, (_, _, src, src_col) in enumerate(others):
                    at = src * n_col + src_col
                    arrive(dw_in.at[h, rows(at, r1)], dc_s.at[h, i], dc_r.at[h, at])
                    piece = piece + dw_in[h, rows(at, r1), :].astype(F32)
                dw_all[core, h, rows(mine, r1), :] = piece.astype(BF16)

            at = dw_all.at[core, h, rows(mine, r1)]
            for i, (to, to_col, _, _) in enumerate(others):
                send(at, at, dg_s.at[h, i], dg_r.at[h, mine], 2 * to + core, to_col, mine < n_own)
            send(at, at, di_s.at[h, mine], di_r.at[h, mine], sib, c, mine < n_own)
            return
        piece = dw_sum[h, rows(chip, r1), :]
        for k, _, src in chips:
            arrive(dw_in.at[h, rows(src, r1)], dc_s.at[h, k], dc_r.at[h, src])
            piece = piece + dw_in[h, rows(src, r1), :].astype(F32)
        dw_mid[h, 0:r1, :] = piece
        dw_mid16[h, 0:r1, :] = piece.astype(BF16)
        if n_col * r2 > r1:
            rest = jnp.zeros((n_col * r2 - r1, half), F32)
            dw_mid[h, r1:, :] = rest
            dw_mid16[h, r1:, :] = rest.astype(BF16)
        for k, to, _ in cols:
            send(
                dw_mid16.at[h, rows(to, r2)], dw_col.at[h, rows(c, r2)],
                dz_s.at[h, k], dz_r.at[h, c], b, to,
            )
        piece = dw_mid[h, rows(c, r2), :]
        for k, _, src in cols:
            arrive(dw_col.at[h, rows(src, r2)], dz_s.at[h, k], dz_r.at[h, src])
            piece = piece + dw_col[h, rows(src, r2), :].astype(F32)
        dw_all[core, h, chip, rows(c, r2), :] = piece.astype(BF16)
        at = dw_all.at[core, h, chip, rows(c, r2)]
        for k, to, _ in cols:
            send(at, at, dg_s.at[h, k], dg_r.at[h, c], b, to)
        for k, _, src in cols:
            at = dw_all.at[core, h, chip, rows(src, r2)]
            arrive(at, dg_s.at[h, k], dg_r.at[h, src])
        at = dw_all.at[core, h, chip, pl.ds(0, r1)]
        for k, to, _ in chips:
            send(at, at, dh_s.at[h, k], dh_r.at[h, chip], 2 * to + core, c)
        send(at, at, di_s.at[h, chip], di_r.at[h, chip], sib, c)

    def result_pass(h):
        if direct:
            for i, (_, _, src, src_col) in enumerate(others):
                owner = src * n_col + src_col
                at = dw_all.at[core, h, rows(owner, r1)]

                @pl.when(owner < n_own)
                def _():
                    arrive(at, dg_s.at[h, i], dg_r.at[h, owner])

                send(at, at, di_s.at[h, owner], di_r.at[h, owner], sib, c, owner < n_own)
            return
        for k, _, src in chips:
            at = dw_all.at[core, h, src, pl.ds(0, r1)]
            arrive(at, dh_s.at[h, k], dh_r.at[h, src])
            send(at, at, di_s.at[h, src], di_r.at[h, src], sib, c)

    def result_arrive(h):
        if direct:
            for owner in range(n_own):
                at = dw_all.at[1 - core, h, rows(owner, r1)]
                arrive(at, di_s.at[h, owner], di_r.at[h, owner])
            return
        for src in range(n_chip):
            at = dw_all.at[1 - core, h, src, pl.ds(0, r1)]
            arrive(at, di_s.at[h, src], di_r.at[h, src])

    def own_features():
        sums = []
        for h in range(2):
            total = pg_part[h, rows(b), :] + pair_in[h, rows(b), :].astype(F32)
            for k, _, src in chips:
                arrive(chip_in.at[h, rows(src)], pc_s.at[h, k], pc_r.at[h, src])
                total = total + chip_in[h, rows(src), :].astype(F32)
            sums.append(total.astype(BF16))
        back = dot(place, jnp.concatenate(sums, axis=1)).astype(BF16)
        xgrad[...] = lax.dot_general(
            back, weight[...], (((1,), (1,)), ((), ())), preferred_element_type=F32
        ).astype(BF16)
        outs.append(pltpu.make_async_copy(xgrad, xgrad_h, out_sem.at[1]))
        outs[1].start()

    pair_start(0)
    features_arrive()
    terms_start(0)
    owners_start(0)
    pair_start(1)
    result_start(0)
    terms_start(1)
    owners_start(1)
    result_pass(0)
    result_start(1)
    own_features()
    result_pass(1)
    result_arrive(0)
    result_arrive(1)
    if direct:
        outs.append(pltpu.make_async_copy(dw_all, wgrad_h, out_sem.at[2]))
    else:
        outs.append(
            pltpu.make_async_copy(dw_all.at[:, :, :, pl.ds(0, r1)], wgrad_h, out_sem.at[2])
        )
    outs[2].start()
    for copy, only in sends:
        if only is None:
            copy.wait_send()
        else:
            pl.when(only)(copy.wait_send)
    for copy in outs:
        copy.wait()


def finish(scale, r1, hidden_in, xgrad_in, wgrad_in, hidden_ref, xgrad_ref, wgrad_ref):
    hidden_ref[...] = hidden_in[...]
    xgrad_ref[...] = xgrad_in[...]
    n_part, half = wgrad_in.shape[2], wgrad_in.shape[4]
    fhalf = wgrad_ref.shape[0] // 2
    for core in range(2):
        for i in range(n_part):
            count = min(r1, fhalf - i * r1)
            if count > 0:
                start = core * fhalf + i * r1
                for h in range(2):
                    wgrad_ref[start:start + count, h * half:(h + 1) * half] = (
                        wgrad_in[core, h, i, 0:count, :].astype(F32) * scale
                    )


def per_device(features, node_order, weight, cotangent, tile_list, tile_values):
    n_blk, n_col = lax.axis_size("blk"), lax.axis_size("col")
    slots, tile, _ = tile_values.shape
    fin, hid = weight.shape
    n_chip = n_blk // 2
    half, fhalf = hid // 2, fin // 2
    scale = float(n_blk * n_col * tile) ** -0.5
    direct = False
    n_sum = n_chip * n_col if direct else n_chip
    r1 = -(-fhalf // (16 * n_sum)) * 16
    direct = direct and fhalf % r1 == 0
    r2 = 16 if direct else -(-r1 // (16 * n_col)) * 16
    padded = fhalf if direct else n_chip * r1
    dma = lambda *n: pltpu.SemaphoreType.DMA(n)
    vmem = pltpu.VMEM
    wide, tall = n_blk * tile, n_col * tile
    turned = wide * tall <= 2 ** 21
    scratch = [
        vmem((tile, fin), BF16), vmem((1, tile), jnp.int32), vmem((fin, hid), BF16),
        vmem((tile, hid), BF16), vmem((slots, tile, tile), BF16),
        vmem((tile, hid), BF16), vmem((tile, fin), BF16),
        vmem((tall, wide), BF16), vmem((wide if turned else tile, tall), BF16),
        vmem((fin, tile), BF16), vmem((fhalf, wide), BF16),
        vmem((2, wide, half), BF16),
        vmem((2, tall, half), F32), vmem((2, tall, half), BF16), vmem((2, tall, half), BF16),
        vmem((2, tall, half), BF16),
        vmem((2, wide, half), F32), vmem((2, wide, half), BF16), vmem((2, wide, half), BF16),
        vmem((2, wide, half), BF16), vmem((2, n_chip * tile, half), BF16),
        vmem((2, padded, half), F32), vmem((2, padded, half), BF16),
        vmem((2, n_sum * r1, half), BF16),
        vmem((2, n_col * r2, half), F32), vmem((2, n_col * r2, half), BF16),
        vmem((2, n_col * r2, half), BF16), vmem((2, 2, fhalf, half) if direct else (2, 2, n_chip, n_col * r2, half), BF16),
        dma(5), dma(3), dma(2, 2 * n_chip), dma(2, n_blk),
        dma(2, n_col), dma(2, n_col), dma(2, n_col), dma(2, n_col),
        dma(2), dma(2), dma(2, n_chip), dma(2, n_chip),
        dma(2 * n_chip), dma(n_blk), dma(2, n_sum), dma(2, n_sum),
        dma(2, n_col), dma(2, n_col), dma(2, n_sum + n_col), dma(2, n_sum + n_col),
        dma(2, n_chip), dma(2, n_chip), dma(2, n_sum), dma(2, n_sum),
    ]
    far = pl.BlockSpec(memory_space=pltpu.HBM)
    free = pl.BlockSpec(memory_space=pl.ANY)
    inside = pl.BlockSpec(memory_space=pltpu.VMEM)
    limit = 60 * 1024 * 1024
    hidden, xgrad, wgrad = pl.pallas_call(
        functools.partial(kernel, (n_blk, n_col, tile, fin, hid, r1, r2, direct)),
        out_shape=(
            jax.ShapeDtypeStruct((tile, hid), BF16),
            jax.ShapeDtypeStruct((tile, fin), BF16),
            jax.ShapeDtypeStruct(
                (2, 2, fhalf, half) if direct else (2, 2, n_chip, r1, half), BF16
            ),
        ),
        in_specs=[far, far, far, far, pl.BlockSpec(memory_space=pltpu.SMEM), far],
        out_specs=(free, free, free),
        scratch_shapes=scratch,
        compiler_params=pltpu.CompilerParams(
            collective_id=0, has_side_effects=True, vmem_limit_bytes=limit
        ),
        cost_estimate=pl.CostEstimate(
            flops=4 * slots * tile * tile * hid, bytes_accessed=4 * 1024 * 1024,
            transcendentals=tile * hid,
        ),
    )(features, node_order, weight, cotangent, tile_list.T, tile_values)
    if direct:
        wgrad, r1 = wgrad.reshape(2, 2, 1, fhalf, half), fhalf
    return pl.pallas_call(
        functools.partial(finish, scale, r1),
        out_shape=(
            jax.ShapeDtypeStruct((tile, hid), BF16),
            jax.ShapeDtypeStruct((tile, fin), BF16),
            jax.ShapeDtypeStruct((fin, hid), F32),
        ),
        in_specs=[inside] * 3,
        out_specs=(inside,) * 3,
        compiler_params=pltpu.CompilerParams(vmem_limit_bytes=limit),
    )(hidden, xgrad, wgrad)


def solution(mesh):
    in_specs = (
        P(("blk", "col"), None),
        P(("blk", "col"), None),
        P(),
        P(("blk", "col"), None),
        P(("blk", "col"), None),
        P(("blk", "col"), None, None),
    )
    out_specs = (P(("blk", "col"), None), P(("blk", "col"), None), P())
    return jax.shard_map(
        per_device, mesh=mesh, in_specs=in_specs, out_specs=out_specs, check_vma=False
    )
```

```python
import functools

import jax
import jax.numpy as jnp
from jax import lax
from jax.experimental import pallas as pl
from jax.experimental.pallas import tpu as pltpu
from jax.sharding import PartitionSpec as P

SLOTS = 3
MESH = pl.DeviceIdType.MESH
F32 = jnp.float32
BF16 = jnp.bfloat16


def dot(a, b):
    return jnp.dot(a, b, preferred_element_type=F32)


def kernel(
    dims,
    feat_h, order_h, weight_h, cot_h, list_ref, tiles_h,
    hidden_h, xgrad_h, wgrad_h,
    feat, order, weight, cot, tiles, hidden, xgrad,
    adj, adj_t, feat_t, feat_all, panels, part, part16, agg_in, grads, pg_part, pg16,
    pair_in, both16, chip_in, dw_sum, dw16, dw_in, dw_mid, dw_mid16, dw_col, dw_all,
    in_sem, out_sem, ag_s, ag_r, rc_s, rc_r, gc_s, gc_r, pp_s, pp_r, pc_s, pc_r,
    fe_s, fe_r, dc_s, dc_r, dz_s, dz_r, dg_s, dg_r, dh_s, dh_r, di_s, di_r,
):
    n_blk, n_col, tile, fin, hid, r1, r2, direct = dims
    n_chip = n_blk // 2
    half = hid // 2
    fhalf = fin // 2
    n_own = fhalf // r1
    b = lax.axis_index("blk")
    c = lax.axis_index("col")
    chip = b // 2
    core = b % 2
    sib = b + 1 - 2 * core
    sends = []

    def rows(i, n=tile):
        return pl.ds(pl.multiple_of(i * n, n), n)

    def send(src, dst, s_sem, r_sem, blk, col, only=None):
        copy = pltpu.make_async_remote_copy(
            src_ref=src, dst_ref=dst, send_sem=s_sem, recv_sem=r_sem,
            device_id=(blk, col), device_id_type=MESH,
        )
        if only is None:
            copy.start()
        else:
            pl.when(only)(copy.start)
        sends.append((copy, only))

    def arrive(dst, s_sem, r_sem):
        pltpu.make_async_remote_copy(
            src_ref=dst, dst_ref=dst, send_sem=s_sem, recv_sem=r_sem,
            device_id=(sib, c), device_id_type=MESH,
        ).wait_recv()

    chips = [(k, (chip + k) % n_chip, (chip + n_chip - k) % n_chip) for k in range(1, n_chip)]
    cols = [(k, (c + k) % n_col, (c + n_col - k) % n_col) for k in range(1, n_col)]

    loads = []
    for i, (src, dst) in enumerate(
        ((feat_h, feat), (weight_h, weight), (order_h, order), (tiles_h, tiles), (cot_h, cot))
    ):
        copy = pltpu.make_async_copy(src, dst, in_sem.at[i])
        copy.start()
        loads.append(copy)

    barrier = pltpu.get_barrier_semaphore()
    peers = [(sib, c)]
    peers += [(2 * to + core, c) for _, to, _ in chips]
    peers += [(2 * to + 1 - core, c) for _, to, _ in chips]
    peers += [(b, to) for _, to, _ in cols]
    if direct:
        peers += [(2 * to + core, at) for _, to, _ in chips for _, at, _ in cols]
    for peer in peers:
        pl.semaphore_signal(barrier, inc=1, device_id=peer, device_id_type=MESH)

    loads[0].wait()
    loads[1].wait()
    loads[2].wait()
    place = (
        lax.broadcasted_iota(jnp.int32, (tile, tile), 0) == order[...]
    ).astype(F32).astype(BF16)
    mixed = dot(feat[...], weight[...]).astype(BF16)
    panel = lax.dot_general(
        place, mixed, (((0,), (0,)), ((), ())), preferred_element_type=F32
    ).astype(BF16)
    for h in range(2):
        panels[h, rows(b), :] = panel[:, h * half:(h + 1) * half]
    pl.semaphore_wait(barrier, len(peers))

    for h in range(2):
        at = panels.at[h, rows(b)]
        for k, to, _ in chips:
            send(at, at, ag_s.at[h, k], ag_r.at[h, b], 2 * to + core, c)
        send(at, at, ag_s.at[h, 0], ag_r.at[h, b], sib, c)

    loads[3].wait()

    def build(g, _):
        held = [tiles[g * SLOTS + s] for s in range(SLOTS)]
        ids = [list_ref[0, g * SLOTS + s] - b * n_col for s in range(SLOTS)]
        for r in range(n_col):
            block = jnp.zeros((tile, tile), BF16)
            for t, i in zip(held, ids):
                block = block + jnp.where(i == r, t, jnp.zeros_like(t))
            adj[r * tile:(r + 1) * tile, rows(g)] = block
        return 0

    lax.fori_loop(0, n_blk, build, 0)
    feat_t[...] = lax.dot_general(
        feat[...], place, (((0,), (0,)), ((), ())), preferred_element_type=F32
    ).astype(BF16)
    feat_all[:, rows(b)] = feat_t[rows(core, fhalf), :]

    step = 4 * tile if n_col % 4 == 0 else tile
    for h in range(2):
        for k, _, src in chips:
            at = panels.at[h, rows(2 * src + core)]
            arrive(at, ag_s.at[h, k], ag_r.at[h, 2 * src + core])
            send(at, at, ag_s.at[h, n_chip + k], ag_r.at[h, 2 * src + core], sib, c)
        arrive(panels.at[h, rows(sib)], ag_s.at[h, 0], ag_r.at[h, sib])
        for k, _, src in chips:
            at = 2 * src + 1 - core
            arrive(panels.at[h, rows(at)], ag_s.at[h, k], ag_r.at[h, at])

        def forward(i, _):
            got = dot(adj[rows(i, step), :], panels[h])
            part[h, rows(i, step), :] = got
            part16[h, rows(i, step), :] = got.astype(BF16)
            return 0

        lax.fori_loop(0, n_col * tile // step, forward, 0)
        for k, to, _ in cols:
            send(part16.at[h, rows(to)], agg_in.at[h, rows(c)], rc_s.at[h, k], rc_r.at[h, c], b, to)

    for k, to, _ in chips:
        for q in range(2):
            at = feat_all.at[:, rows(b)]
            send(feat_t.at[pl.ds(q * fhalf, fhalf)], at, fe_s.at[2 * k + q], fe_r.at[b], 2 * to + q, c)
    send(feat_t.at[rows(1 - core, fhalf)], feat_all.at[:, rows(b)], fe_s.at[0], fe_r.at[b], sib, c)

    def turn(g, _):
        for r in range(n_col):
            adj_t[rows(g), r * tile:(r + 1) * tile] = (
                adj[r * tile:(r + 1) * tile, rows(g)].T
            )
        return 0

    turned = adj_t.shape[0] > tile
    if turned:
        lax.fori_loop(0, n_blk, turn, 0)
    loads[4].wait()

    root = 0.7978845608028654
    for h in range(2):
        agg = part[h, rows(c), :]
        for k, _, src in cols:
            arrive(agg_in.at[h, rows(src)], rc_s.at[h, k], rc_r.at[h, src])
            agg = agg + agg_in[h, rows(src), :].astype(F32)
        inner = root * (agg + 0.044715 * agg * agg * agg)
        th = jnp.tanh(inner)
        slope = 0.5 * (1.0 + th) + 0.5 * agg * (1.0 - th * th) * (
            root * (1.0 + 3 * 0.044715 * agg * agg)
        )
        lanes = slice(h * half, (h + 1) * half)
        grads[h, rows(c), :] = (cot[:, lanes].astype(F32) * slope).astype(BF16)
        at = grads.at[h, rows(c)]
        for k, to, _ in cols:
            send(at, at, gc_s.at[h, k], gc_r.at[h, c], b, to)
        hidden[:, lanes] = (0.5 * agg * (1.0 + th)).astype(BF16)
    outs = [pltpu.make_async_copy(hidden, hidden_h, out_sem.at[0])]
    outs[0].start()

    bstep = 4 * tile if n_blk % 4 == 0 else tile
    others = [
        ((chip + i) % n_chip, (c + j) % n_col, (chip + n_chip - i) % n_chip, (c + n_col - j) % n_col)
        for i in range(n_chip) for j in range(n_col) if i + j > 0
    ]
    mine = chip * n_col + c

    def pair_start(h):
        for k, _, src in cols:
            arrive(grads.at[h, rows(src)], gc_s.at[h, k], gc_r.at[h, src])

        def backward(i, _):
            if turned:
                got = dot(adj_t[rows(i, bstep), :], grads[h])
            else:
                got = lax.dot_general(
                    adj[:, rows(i, bstep)], grads[h], (((0,), (0,)), ((), ())),
                    preferred_element_type=F32,
                )
            pg_part[h, rows(i, bstep), :] = got
            pg16[h, rows(i, bstep), :] = got.astype(BF16)
            return 0

        lax.fori_loop(0, n_blk * tile // bstep, backward, 0)
        send(pg16.at[h], pair_in.at[h], pp_s.at[h], pp_r.at[h], sib, c)

    def features_arrive():
        for k, _, src in chips:
            for q in range(2):
                at = feat_all.at[:, rows(2 * src + q)]
                arrive(at, fe_s.at[0], fe_r.at[2 * src + q])
        arrive(feat_all.at[:, rows(sib)], fe_s.at[0], fe_r.at[sib])

    def terms_start(h):
        arrive(pair_in.at[h], pp_s.at[h], pp_r.at[h])
        both16[h] = (pg_part[h] + pair_in[h].astype(F32)).astype(BF16)
        term = dot(feat_all[...], both16[h])
        dw_sum[h, 0:fhalf, :] = term
        dw16[h, 0:fhalf, :] = term.astype(BF16)
        if direct:
            for i, (to, to_col, _, _) in enumerate(others):
                owner = to * n_col + to_col
                send(
                    dw16.at[h, rows(owner, r1)], dw_in.at[h, rows(mine, r1)],
                    dc_s.at[h, i], dc_r.at[h, mine], 2 * to + core, to_col, owner < n_own,
                )
            return
        if n_chip * r1 > fhalf:
            rest = jnp.zeros((n_chip * r1 - fhalf, half), F32)
            dw_sum[h, fhalf:, :] = rest
            dw16[h, fhalf:, :] = rest.astype(BF16)
        for k, to, _ in chips:
            send(
                dw16.at[h, rows(to, r1)], dw_in.at[h, rows(chip, r1)],
                dc_s.at[h, k], dc_r.at[h, chip], 2 * to + core, c,
            )

    def owners_start(h):
        for k, to, _ in chips:
            send(
                both16.at[h, rows(2 * to + core)], chip_in.at[h, rows(chip)],
                pc_s.at[h, k], pc_r.at[h, chip], 2 * to + core, c,
            )

    def result_start(h):
        if direct:
            @pl.when(mine < n_own)
            def _():
                piece = dw_sum[h, rows(mine, r1), :]
                for i, (_, _, src, src_col) in enumerate(others):
                    at = src * n_col + src_col
                    arrive(dw_in.at[h, rows(at, r1)], dc_s.at[h, i], dc_r.at[h, at])
                    piece = piece + dw_in[h, rows(at, r1), :].astype(F32)
                dw_all[core, h, rows(mine, r1), :] = piece.astype(BF16)

            at = dw_all.at[core, h, rows(mine, r1)]
            for i, (to, to_col, _, _) in enumerate(others):
                send(at, at, dg_s.at[h, i], dg_r.at[h, mine], 2 * to + core, to_col, mine < n_own)
            send(at, at, di_s.at[h, mine], di_r.at[h, mine], sib, c, mine < n_own)
            return
        piece = dw_sum[h, rows(chip, r1), :]
        for k, _, src in chips:
            arrive(dw_in.at[h, rows(src, r1)], dc_s.at[h, k], dc_r.at[h, src])
            piece = piece + dw_in[h, rows(src, r1), :].astype(F32)
        dw_mid[h, 0:r1, :] = piece
        dw_mid16[h, 0:r1, :] = piece.astype(BF16)
        if n_col * r2 > r1:
            rest = jnp.zeros((n_col * r2 - r1, half), F32)
            dw_mid[h, r1:, :] = rest
            dw_mid16[h, r1:, :] = rest.astype(BF16)
        for k, to, _ in cols:
            send(
                dw_mid16.at[h, rows(to, r2)], dw_col.at[h, rows(c, r2)],
                dz_s.at[h, k], dz_r.at[h, c], b, to,
            )
        piece = dw_mid[h, rows(c, r2), :]
        for k, _, src in cols:
            arrive(dw_col.at[h, rows(src, r2)], dz_s.at[h, k], dz_r.at[h, src])
            piece = piece + dw_col[h, rows(src, r2), :].astype(F32)
        dw_all[core, h, chip, rows(c, r2), :] = piece.astype(BF16)
        at = dw_all.at[core, h, chip, rows(c, r2)]
        for k, to, _ in cols:
            send(at, at, dg_s.at[h, k], dg_r.at[h, c], b, to)
        for k, _, src in cols:
            at = dw_all.at[core, h, chip, rows(src, r2)]
            arrive(at, dg_s.at[h, k], dg_r.at[h, src])
        at = dw_all.at[core, h, chip, pl.ds(0, r1)]
        for k, to, _ in chips:
            send(at, at, dh_s.at[h, k], dh_r.at[h, chip], 2 * to + core, c)
        send(at, at, di_s.at[h, chip], di_r.at[h, chip], sib, c)

    def result_pass(h):
        if direct:
            for i, (_, _, src, src_col) in enumerate(others):
                owner = src * n_col + src_col
                at = dw_all.at[core, h, rows(owner, r1)]

                @pl.when(owner < n_own)
                def _():
                    arrive(at, dg_s.at[h, i], dg_r.at[h, owner])

                send(at, at, di_s.at[h, owner], di_r.at[h, owner], sib, c, owner < n_own)
            return
        for k, _, src in chips:
            at = dw_all.at[core, h, src, pl.ds(0, r1)]
            arrive(at, dh_s.at[h, k], dh_r.at[h, src])
            send(at, at, di_s.at[h, src], di_r.at[h, src], sib, c)

    def result_arrive(h):
        if direct:
            for owner in range(n_own):
                at = dw_all.at[1 - core, h, rows(owner, r1)]
                arrive(at, di_s.at[h, owner], di_r.at[h, owner])
            return
        for src in range(n_chip):
            at = dw_all.at[1 - core, h, src, pl.ds(0, r1)]
            arrive(at, di_s.at[h, src], di_r.at[h, src])

    def own_features():
        sums = []
        for h in range(2):
            total = pg_part[h, rows(b), :] + pair_in[h, rows(b), :].astype(F32)
            for k, _, src in chips:
                arrive(chip_in.at[h, rows(src)], pc_s.at[h, k], pc_r.at[h, src])
                total = total + chip_in[h, rows(src), :].astype(F32)
            sums.append(total.astype(BF16))
        back = dot(place, jnp.concatenate(sums, axis=1)).astype(BF16)
        xgrad[...] = lax.dot_general(
            back, weight[...], (((1,), (1,)), ((), ())), preferred_element_type=F32
        ).astype(BF16)
        outs.append(pltpu.make_async_copy(xgrad, xgrad_h, out_sem.at[1]))
        outs[1].start()

    pair_start(0)
    pair_start(1)
    features_arrive()
    terms_start(0)
    terms_start(1)
    owners_start(0)
    owners_start(1)
    result_start(0)
    result_start(1)
    own_features()
    result_pass(0)
    result_pass(1)
    result_arrive(0)
    result_arrive(1)
    if direct:
        outs.append(pltpu.make_async_copy(dw_all, wgrad_h, out_sem.at[2]))
    else:
        outs.append(
            pltpu.make_async_copy(dw_all.at[:, :, :, pl.ds(0, r1)], wgrad_h, out_sem.at[2])
        )
    outs[2].start()
    for copy, only in sends:
        if only is None:
            copy.wait_send()
        else:
            pl.when(only)(copy.wait_send)
    for copy in outs:
        copy.wait()


def finish(scale, r1, hidden_in, xgrad_in, wgrad_in, hidden_ref, xgrad_ref, wgrad_ref):
    hidden_ref[...] = hidden_in[...]
    xgrad_ref[...] = xgrad_in[...]
    n_part, half = wgrad_in.shape[2], wgrad_in.shape[4]
    fhalf = wgrad_ref.shape[0] // 2
    for core in range(2):
        for i in range(n_part):
            count = min(r1, fhalf - i * r1)
            if count > 0:
                start = core * fhalf + i * r1
                for h in range(2):
                    wgrad_ref[start:start + count, h * half:(h + 1) * half] = (
                        wgrad_in[core, h, i, 0:count, :].astype(F32) * scale
                    )


def per_device(features, node_order, weight, cotangent, tile_list, tile_values):
    n_blk, n_col = lax.axis_size("blk"), lax.axis_size("col")
    slots, tile, _ = tile_values.shape
    fin, hid = weight.shape
    n_chip = n_blk // 2
    half, fhalf = hid // 2, fin // 2
    scale = float(n_blk * n_col * tile) ** -0.5
    direct = n_chip * n_col <= 16
    n_sum = n_chip * n_col if direct else n_chip
    r1 = -(-fhalf // (16 * n_sum)) * 16
    direct = direct and fhalf % r1 == 0
    r2 = 16 if direct else -(-r1 // (16 * n_col)) * 16
    padded = fhalf if direct else n_chip * r1
    dma = lambda *n: pltpu.SemaphoreType.DMA(n)
    vmem = pltpu.VMEM
    wide, tall = n_blk * tile, n_col * tile
    turned = wide * tall <= 2 ** 21
    scratch = [
        vmem((tile, fin), BF16), vmem((1, tile), jnp.int32), vmem((fin, hid), BF16),
        vmem((tile, hid), BF16), vmem((slots, tile, tile), BF16),
        vmem((tile, hid), BF16), vmem((tile, fin), BF16),
        vmem((tall, wide), BF16), vmem((wide if turned else tile, tall), BF16),
        vmem((fin, tile), BF16), vmem((fhalf, wide), BF16),
        vmem((2, wide, half), BF16),
        vmem((2, tall, half), F32), vmem((2, tall, half), BF16), vmem((2, tall, half), BF16),
        vmem((2, tall, half), BF16),
        vmem((2, wide, half), F32), vmem((2, wide, half), BF16), vmem((2, wide, half), BF16),
        vmem((2, wide, half), BF16), vmem((2, n_chip * tile, half), BF16),
        vmem((2, padded, half), F32), vmem((2, padded, half), BF16),
        vmem((2, n_sum * r1, half), BF16),
        vmem((2, n_col * r2, half), F32), vmem((2, n_col * r2, half), BF16),
        vmem((2, n_col * r2, half), BF16), vmem((2, 2, fhalf, half) if direct else (2, 2, n_chip, n_col * r2, half), BF16),
        dma(5), dma(3), dma(2, 2 * n_chip), dma(2, n_blk),
        dma(2, n_col), dma(2, n_col), dma(2, n_col), dma(2, n_col),
        dma(2), dma(2), dma(2, n_chip), dma(2, n_chip),
        dma(2 * n_chip), dma(n_blk), dma(2, n_sum), dma(2, n_sum),
        dma(2, n_col), dma(2, n_col), dma(2, n_sum + n_col), dma(2, n_sum + n_col),
        dma(2, n_chip), dma(2, n_chip), dma(2, n_sum), dma(2, n_sum),
    ]
    far = pl.BlockSpec(memory_space=pltpu.HBM)
    free = pl.BlockSpec(memory_space=pl.ANY)
    inside = pl.BlockSpec(memory_space=pltpu.VMEM)
    limit = 60 * 1024 * 1024
    hidden, xgrad, wgrad = pl.pallas_call(
        functools.partial(kernel, (n_blk, n_col, tile, fin, hid, r1, r2, direct)),
        out_shape=(
            jax.ShapeDtypeStruct((tile, hid), BF16),
            jax.ShapeDtypeStruct((tile, fin), BF16),
            jax.ShapeDtypeStruct(
                (2, 2, fhalf, half) if direct else (2, 2, n_chip, r1, half), BF16
            ),
        ),
        in_specs=[far, far, far, far, pl.BlockSpec(memory_space=pltpu.SMEM), far],
        out_specs=(free, free, free),
        scratch_shapes=scratch,
        compiler_params=pltpu.CompilerParams(
            collective_id=0, has_side_effects=True, vmem_limit_bytes=limit
        ),
        cost_estimate=pl.CostEstimate(
            flops=4 * slots * tile * tile * hid, bytes_accessed=4 * 1024 * 1024,
            transcendentals=tile * hid,
        ),
    )(features, node_order, weight, cotangent, tile_list.T, tile_values)
    if direct:
        wgrad, r1 = wgrad.reshape(2, 2, 1, fhalf, half), fhalf
    return pl.pallas_call(
        functools.partial(finish, scale, r1),
        out_shape=(
            jax.ShapeDtypeStruct((tile, hid), BF16),
            jax.ShapeDtypeStruct((tile, fin), BF16),
            jax.ShapeDtypeStruct((fin, hid), F32),
        ),
        in_specs=[inside] * 3,
        out_specs=(inside,) * 3,
        compiler_params=pltpu.CompilerParams(vmem_limit_bytes=limit),
    )(hidden, xgrad, wgrad)


def solution(mesh):
    in_specs = (
        P(("blk", "col"), None),
        P(("blk", "col"), None),
        P(),
        P(("blk", "col"), None),
        P(("blk", "col"), None),
        P(("blk", "col"), None, None),
    )
    out_specs = (P(("blk", "col"), None), P(("blk", "col"), None), P())
    return jax.shard_map(
        per_device, mesh=mesh, in_specs=in_specs, out_specs=out_specs, check_vma=False
    )
```

```python
import functools

import jax
import jax.numpy as jnp
from jax import lax
from jax.experimental import pallas as pl
from jax.experimental.pallas import tpu as pltpu
from jax.sharding import PartitionSpec as P

SLOTS = 3
MESH = pl.DeviceIdType.MESH
F32 = jnp.float32
BF16 = jnp.bfloat16


def dot(a, b):
    return jnp.dot(a, b, preferred_element_type=F32)


def kernel(
    dims,
    feat_h, order_h, weight_h, cot_h, list_ref, tiles_h,
    hidden_h, xgrad_h, wgrad_h,
    feat, order, weight, cot, tiles, hidden, xgrad,
    adj, adj_t, feat_t, feat_all, panels, part, part16, agg_in, grads, pg_part, pg16,
    pair_in, both16, chip_in, dw_sum, dw16, dw_in, dw_mid, dw_mid16, dw_col, dw_all,
    in_sem, out_sem, ag_s, ag_r, rc_s, rc_r, gc_s, gc_r, pp_s, pp_r, pc_s, pc_r,
    fe_s, fe_r, dc_s, dc_r, dz_s, dz_r, dg_s, dg_r, dh_s, dh_r, di_s, di_r,
):
    n_blk, n_col, tile, fin, hid, r1, r2, direct = dims
    n_chip = n_blk // 2
    half = hid // 2
    fhalf = fin // 2
    n_own = fhalf // r1
    b = lax.axis_index("blk")
    c = lax.axis_index("col")
    chip = b // 2
    core = b % 2
    sib = b + 1 - 2 * core
    sends = []

    def rows(i, n=tile):
        return pl.ds(pl.multiple_of(i * n, n), n)

    def send(src, dst, s_sem, r_sem, blk, col, only=None):
        copy = pltpu.make_async_remote_copy(
            src_ref=src, dst_ref=dst, send_sem=s_sem, recv_sem=r_sem,
            device_id=(blk, col), device_id_type=MESH,
        )
        if only is None:
            copy.start()
        else:
            pl.when(only)(copy.start)
        sends.append((copy, only))

    def arrive(dst, s_sem, r_sem):
        pltpu.make_async_remote_copy(
            src_ref=dst, dst_ref=dst, send_sem=s_sem, recv_sem=r_sem,
            device_id=(sib, c), device_id_type=MESH,
        ).wait_recv()

    chips = [(k, (chip + k) % n_chip, (chip + n_chip - k) % n_chip) for k in range(1, n_chip)]
    cols = [(k, (c + k) % n_col, (c + n_col - k) % n_col) for k in range(1, n_col)]

    loads = []
    for i, (src, dst) in enumerate(
        ((feat_h, feat), (weight_h, weight), (order_h, order), (tiles_h, tiles), (cot_h, cot))
    ):
        copy = pltpu.make_async_copy(src, dst, in_sem.at[i])
        copy.start()
        loads.append(copy)

    barrier = pltpu.get_barrier_semaphore()
    peers = [(sib, c)]
    peers += [(2 * to + core, c) for _, to, _ in chips]
    peers += [(2 * to + 1 - core, c) for _, to, _ in chips]
    peers += [(b, to) for _, to, _ in cols]
    if direct:
        peers += [(2 * to + core, at) for _, to, _ in chips for _, at, _ in cols]
    for peer in peers:
        pl.semaphore_signal(barrier, inc=1, device_id=peer, device_id_type=MESH)

    loads[0].wait()
    loads[1].wait()
    loads[2].wait()
    place = (
        lax.broadcasted_iota(jnp.int32, (tile, tile), 0) == order[...]
    ).astype(F32).astype(BF16)
    mixed = dot(feat[...], weight[...]).astype(BF16)
    panel = lax.dot_general(
        place, mixed, (((0,), (0,)), ((), ())), preferred_element_type=F32
    ).astype(BF16)
    for h in range(2):
        panels[h, rows(b), :] = panel[:, h * half:(h + 1) * half]
    pl.semaphore_wait(barrier, len(peers))

    for h in range(2):
        at = panels.at[h, rows(b)]
        for k, to, _ in chips:
            send(at, at, ag_s.at[h, k], ag_r.at[h, b], 2 * to + core, c)
        send(at, at, ag_s.at[h, 0], ag_r.at[h, b], sib, c)

    feat_t[...] = lax.dot_general(
        feat[...], place, (((0,), (0,)), ((), ())), preferred_element_type=F32
    ).astype(BF16)
    feat_all[:, rows(b)] = feat_t[rows(core, fhalf), :]

    for k, to, _ in chips:
        for q in range(2):
            at = feat_all.at[:, rows(b)]
            send(feat_t.at[pl.ds(q * fhalf, fhalf)], at, fe_s.at[2 * k + q], fe_r.at[b], 2 * to + q, c)
    send(feat_t.at[rows(1 - core, fhalf)], feat_all.at[:, rows(b)], fe_s.at[0], fe_r.at[b], sib, c)

    loads[3].wait()

    def build(g, _):
        held = [tiles[g * SLOTS + s] for s in range(SLOTS)]
        ids = [list_ref[0, g * SLOTS + s] - b * n_col for s in range(SLOTS)]
        for r in range(n_col):
            block = jnp.zeros((tile, tile), BF16)
            for t, i in zip(held, ids):
                block = block + jnp.where(i == r, t, jnp.zeros_like(t))
            adj[r * tile:(r + 1) * tile, rows(g)] = block
        return 0

    lax.fori_loop(0, n_blk, build, 0)
    step = 4 * tile if n_col % 4 == 0 else tile
    for h in range(2):
        for k, _, src in chips:
            at = panels.at[h, rows(2 * src + core)]
            arrive(at, ag_s.at[h, k], ag_r.at[h, 2 * src + core])
            send(at, at, ag_s.at[h, n_chip + k], ag_r.at[h, 2 * src + core], sib, c)
        arrive(panels.at[h, rows(sib)], ag_s.at[h, 0], ag_r.at[h, sib])
        for k, _, src in chips:
            at = 2 * src + 1 - core
            arrive(panels.at[h, rows(at)], ag_s.at[h, k], ag_r.at[h, at])

        def forward(i, _):
            got = dot(adj[rows(i, step), :], panels[h])
            part[h, rows(i, step), :] = got
            part16[h, rows(i, step), :] = got.astype(BF16)
            return 0

        lax.fori_loop(0, n_col * tile // step, forward, 0)
        for k, to, _ in cols:
            send(part16.at[h, rows(to)], agg_in.at[h, rows(c)], rc_s.at[h, k], rc_r.at[h, c], b, to)

    def turn(g, _):
        for r in range(n_col):
            adj_t[rows(g), r * tile:(r + 1) * tile] = (
                adj[r * tile:(r + 1) * tile, rows(g)].T
            )
        return 0

    turned = adj_t.shape[0] > tile
    if turned:
        lax.fori_loop(0, n_blk, turn, 0)
    loads[4].wait()

    root = 0.7978845608028654
    for h in range(2):
        agg = part[h, rows(c), :]
        for k, _, src in cols:
            arrive(agg_in.at[h, rows(src)], rc_s.at[h, k], rc_r.at[h, src])
            agg = agg + agg_in[h, rows(src), :].astype(F32)
        inner = root * (agg + 0.044715 * agg * agg * agg)
        th = jnp.tanh(inner)
        slope = 0.5 * (1.0 + th) + 0.5 * agg * (1.0 - th * th) * (
            root * (1.0 + 3 * 0.044715 * agg * agg)
        )
        lanes = slice(h * half, (h + 1) * half)
        grads[h, rows(c), :] = (cot[:, lanes].astype(F32) * slope).astype(BF16)
        at = grads.at[h, rows(c)]
        for k, to, _ in cols:
            send(at, at, gc_s.at[h, k], gc_r.at[h, c], b, to)
        hidden[:, lanes] = (0.5 * agg * (1.0 + th)).astype(BF16)
    outs = [pltpu.make_async_copy(hidden, hidden_h, out_sem.at[0])]
    outs[0].start()

    bstep = 4 * tile if n_blk % 4 == 0 else tile
    others = [
        ((chip + i) % n_chip, (c + j) % n_col, (chip + n_chip - i) % n_chip, (c + n_col - j) % n_col)
        for i in range(n_chip) for j in range(n_col) if i + j > 0
    ]
    mine = chip * n_col + c

    def pair_start(h):
        for k, _, src in cols:
            arrive(grads.at[h, rows(src)], gc_s.at[h, k], gc_r.at[h, src])

        def backward(i, _):
            if turned:
                got = dot(adj_t[rows(i, bstep), :], grads[h])
            else:
                got = lax.dot_general(
                    adj[:, rows(i, bstep)], grads[h], (((0,), (0,)), ((), ())),
                    preferred_element_type=F32,
                )
            pg_part[h, rows(i, bstep), :] = got
            pg16[h, rows(i, bstep), :] = got.astype(BF16)
            return 0

        lax.fori_loop(0, n_blk * tile // bstep, backward, 0)
        send(pg16.at[h], pair_in.at[h], pp_s.at[h], pp_r.at[h], sib, c)

    def features_arrive():
        for k, _, src in chips:
            for q in range(2):
                at = feat_all.at[:, rows(2 * src + q)]
                arrive(at, fe_s.at[0], fe_r.at[2 * src + q])
        arrive(feat_all.at[:, rows(sib)], fe_s.at[0], fe_r.at[sib])

    def terms_start(h):
        arrive(pair_in.at[h], pp_s.at[h], pp_r.at[h])
        both16[h] = (pg_part[h] + pair_in[h].astype(F32)).astype(BF16)
        term = dot(feat_all[...], both16[h])
        dw_sum[h, 0:fhalf, :] = term
        dw16[h, 0:fhalf, :] = term.astype(BF16)
        if direct:
            for i, (to, to_col, _, _) in enumerate(others):
                owner = to * n_col + to_col
                send(
                    dw16.at[h, rows(owner, r1)], dw_in.at[h, rows(mine, r1)],
                    dc_s.at[h, i], dc_r.at[h, mine], 2 * to + core, to_col, owner < n_own,
                )
            return
        if n_chip * r1 > fhalf:
            rest = jnp.zeros((n_chip * r1 - fhalf, half), F32)
            dw_sum[h, fhalf:, :] = rest
            dw16[h, fhalf:, :] = rest.astype(BF16)
        for k, to, _ in chips:
            send(
                dw16.at[h, rows(to, r1)], dw_in.at[h, rows(chip, r1)],
                dc_s.at[h, k], dc_r.at[h, chip], 2 * to + core, c,
            )

    def owners_start(h):
        for k, to, _ in chips:
            send(
                both16.at[h, rows(2 * to + core)], chip_in.at[h, rows(chip)],
                pc_s.at[h, k], pc_r.at[h, chip], 2 * to + core, c,
            )

    def result_start(h):
        if direct:
            @pl.when(mine < n_own)
            def _():
                piece = dw_sum[h, rows(mine, r1), :]
                for i, (_, _, src, src_col) in enumerate(others):
                    at = src * n_col + src_col
                    arrive(dw_in.at[h, rows(at, r1)], dc_s.at[h, i], dc_r.at[h, at])
                    piece = piece + dw_in[h, rows(at, r1), :].astype(F32)
                dw_all[core, h, rows(mine, r1), :] = piece.astype(BF16)

            at = dw_all.at[core, h, rows(mine, r1)]
            for i, (to, to_col, _, _) in enumerate(others):
                send(at, at, dg_s.at[h, i], dg_r.at[h, mine], 2 * to + core, to_col, mine < n_own)
            send(at, at, di_s.at[h, mine], di_r.at[h, mine], sib, c, mine < n_own)
            return
        piece = dw_sum[h, rows(chip, r1), :]
        for k, _, src in chips:
            arrive(dw_in.at[h, rows(src, r1)], dc_s.at[h, k], dc_r.at[h, src])
            piece = piece + dw_in[h, rows(src, r1), :].astype(F32)
        dw_mid[h, 0:r1, :] = piece
        dw_mid16[h, 0:r1, :] = piece.astype(BF16)
        if n_col * r2 > r1:
            rest = jnp.zeros((n_col * r2 - r1, half), F32)
            dw_mid[h, r1:, :] = rest
            dw_mid16[h, r1:, :] = rest.astype(BF16)
        for k, to, _ in cols:
            send(
                dw_mid16.at[h, rows(to, r2)], dw_col.at[h, rows(c, r2)],
                dz_s.at[h, k], dz_r.at[h, c], b, to,
            )
        piece = dw_mid[h, rows(c, r2), :]
        for k, _, src in cols:
            arrive(dw_col.at[h, rows(src, r2)], dz_s.at[h, k], dz_r.at[h, src])
            piece = piece + dw_col[h, rows(src, r2), :].astype(F32)
        dw_all[core, h, chip, rows(c, r2), :] = piece.astype(BF16)
        at = dw_all.at[core, h, chip, rows(c, r2)]
        for k, to, _ in cols:
            send(at, at, dg_s.at[h, k], dg_r.at[h, c], b, to)
        for k, _, src in cols:
            at = dw_all.at[core, h, chip, rows(src, r2)]
            arrive(at, dg_s.at[h, k], dg_r.at[h, src])
        at = dw_all.at[core, h, chip, pl.ds(0, r1)]
        for k, to, _ in chips:
            send(at, at, dh_s.at[h, k], dh_r.at[h, chip], 2 * to + core, c)
        send(at, at, di_s.at[h, chip], di_r.at[h, chip], sib, c)

    def result_pass(h):
        if direct:
            for i, (_, _, src, src_col) in enumerate(others):
                owner = src * n_col + src_col
                at = dw_all.at[core, h, rows(owner, r1)]

                @pl.when(owner < n_own)
                def _():
                    arrive(at, dg_s.at[h, i], dg_r.at[h, owner])

                send(at, at, di_s.at[h, owner], di_r.at[h, owner], sib, c, owner < n_own)
            return
        for k, _, src in chips:
            at = dw_all.at[core, h, src, pl.ds(0, r1)]
            arrive(at, dh_s.at[h, k], dh_r.at[h, src])
            send(at, at, di_s.at[h, src], di_r.at[h, src], sib, c)

    def result_arrive(h):
        if direct:
            for owner in range(n_own):
                at = dw_all.at[1 - core, h, rows(owner, r1)]
                arrive(at, di_s.at[h, owner], di_r.at[h, owner])
            return
        for src in range(n_chip):
            at = dw_all.at[1 - core, h, src, pl.ds(0, r1)]
            arrive(at, di_s.at[h, src], di_r.at[h, src])

    def own_features():
        sums = []
        for h in range(2):
            total = pg_part[h, rows(b), :] + pair_in[h, rows(b), :].astype(F32)
            for k, _, src in chips:
                arrive(chip_in.at[h, rows(src)], pc_s.at[h, k], pc_r.at[h, src])
                total = total + chip_in[h, rows(src), :].astype(F32)
            sums.append(total.astype(BF16))
        back = dot(place, jnp.concatenate(sums, axis=1)).astype(BF16)
        xgrad[...] = lax.dot_general(
            back, weight[...], (((1,), (1,)), ((), ())), preferred_element_type=F32
        ).astype(BF16)
        outs.append(pltpu.make_async_copy(xgrad, xgrad_h, out_sem.at[1]))
        outs[1].start()

    pair_start(0)
    pair_start(1)
    features_arrive()
    terms_start(0)
    terms_start(1)
    owners_start(0)
    owners_start(1)
    result_start(0)
    result_start(1)
    own_features()
    result_pass(0)
    result_pass(1)
    result_arrive(0)
    result_arrive(1)
    if direct:
        outs.append(pltpu.make_async_copy(dw_all, wgrad_h, out_sem.at[2]))
    else:
        outs.append(
            pltpu.make_async_copy(dw_all.at[:, :, :, pl.ds(0, r1)], wgrad_h, out_sem.at[2])
        )
    outs[2].start()
    for copy, only in sends:
        if only is None:
            copy.wait_send()
        else:
            pl.when(only)(copy.wait_send)
    for copy in outs:
        copy.wait()


def finish(scale, r1, hidden_in, xgrad_in, wgrad_in, hidden_ref, xgrad_ref, wgrad_ref):
    hidden_ref[...] = hidden_in[...]
    xgrad_ref[...] = xgrad_in[...]
    n_part, half = wgrad_in.shape[2], wgrad_in.shape[4]
    fhalf = wgrad_ref.shape[0] // 2
    for core in range(2):
        for i in range(n_part):
            count = min(r1, fhalf - i * r1)
            if count > 0:
                start = core * fhalf + i * r1
                for h in range(2):
                    wgrad_ref[start:start + count, h * half:(h + 1) * half] = (
                        wgrad_in[core, h, i, 0:count, :].astype(F32) * scale
                    )


def per_device(features, node_order, weight, cotangent, tile_list, tile_values):
    n_blk, n_col = lax.axis_size("blk"), lax.axis_size("col")
    slots, tile, _ = tile_values.shape
    fin, hid = weight.shape
    n_chip = n_blk // 2
    half, fhalf = hid // 2, fin // 2
    scale = float(n_blk * n_col * tile) ** -0.5
    direct = n_chip * n_col <= 16
    n_sum = n_chip * n_col if direct else n_chip
    r1 = -(-fhalf // (16 * n_sum)) * 16
    direct = direct and fhalf % r1 == 0
    r2 = 16 if direct else -(-r1 // (16 * n_col)) * 16
    padded = fhalf if direct else n_chip * r1
    dma = lambda *n: pltpu.SemaphoreType.DMA(n)
    vmem = pltpu.VMEM
    wide, tall = n_blk * tile, n_col * tile
    turned = wide * tall <= 2 ** 21
    scratch = [
        vmem((tile, fin), BF16), vmem((1, tile), jnp.int32), vmem((fin, hid), BF16),
        vmem((tile, hid), BF16), vmem((slots, tile, tile), BF16),
        vmem((tile, hid), BF16), vmem((tile, fin), BF16),
        vmem((tall, wide), BF16), vmem((wide if turned else tile, tall), BF16),
        vmem((fin, tile), BF16), vmem((fhalf, wide), BF16),
        vmem((2, wide, half), BF16),
        vmem((2, tall, half), F32), vmem((2, tall, half), BF16), vmem((2, tall, half), BF16),
        vmem((2, tall, half), BF16),
        vmem((2, wide, half), F32), vmem((2, wide, half), BF16), vmem((2, wide, half), BF16),
        vmem((2, wide, half), BF16), vmem((2, n_chip * tile, half), BF16),
        vmem((2, padded, half), F32), vmem((2, padded, half), BF16),
        vmem((2, n_sum * r1, half), BF16),
        vmem((2, n_col * r2, half), F32), vmem((2, n_col * r2, half), BF16),
        vmem((2, n_col * r2, half), BF16), vmem((2, 2, fhalf, half) if direct else (2, 2, n_chip, n_col * r2, half), BF16),
        dma(5), dma(3), dma(2, 2 * n_chip), dma(2, n_blk),
        dma(2, n_col), dma(2, n_col), dma(2, n_col), dma(2, n_col),
        dma(2), dma(2), dma(2, n_chip), dma(2, n_chip),
        dma(2 * n_chip), dma(n_blk), dma(2, n_sum), dma(2, n_sum),
        dma(2, n_col), dma(2, n_col), dma(2, n_sum + n_col), dma(2, n_sum + n_col),
        dma(2, n_chip), dma(2, n_chip), dma(2, n_sum), dma(2, n_sum),
    ]
    far = pl.BlockSpec(memory_space=pltpu.HBM)
    free = pl.BlockSpec(memory_space=pl.ANY)
    inside = pl.BlockSpec(memory_space=pltpu.VMEM)
    limit = 60 * 1024 * 1024
    hidden, xgrad, wgrad = pl.pallas_call(
        functools.partial(kernel, (n_blk, n_col, tile, fin, hid, r1, r2, direct)),
        out_shape=(
            jax.ShapeDtypeStruct((tile, hid), BF16),
            jax.ShapeDtypeStruct((tile, fin), BF16),
            jax.ShapeDtypeStruct(
                (2, 2, fhalf, half) if direct else (2, 2, n_chip, r1, half), BF16
            ),
        ),
        in_specs=[far, far, far, far, pl.BlockSpec(memory_space=pltpu.SMEM), far],
        out_specs=(free, free, free),
        scratch_shapes=scratch,
        compiler_params=pltpu.CompilerParams(
            collective_id=0, has_side_effects=True, vmem_limit_bytes=limit
        ),
        cost_estimate=pl.CostEstimate(
            flops=4 * slots * tile * tile * hid, bytes_accessed=4 * 1024 * 1024,
            transcendentals=tile * hid,
        ),
    )(features, node_order, weight, cotangent, tile_list.T, tile_values)
    if direct:
        wgrad, r1 = wgrad.reshape(2, 2, 1, fhalf, half), fhalf
    return pl.pallas_call(
        functools.partial(finish, scale, r1),
        out_shape=(
            jax.ShapeDtypeStruct((tile, hid), BF16),
            jax.ShapeDtypeStruct((tile, fin), BF16),
            jax.ShapeDtypeStruct((fin, hid), F32),
        ),
        in_specs=[inside] * 3,
        out_specs=(inside,) * 3,
        compiler_params=pltpu.CompilerParams(vmem_limit_bytes=limit),
    )(hidden, xgrad, wgrad)


def solution(mesh):
    in_specs = (
        P(("blk", "col"), None),
        P(("blk", "col"), None),
        P(),
        P(("blk", "col"), None),
        P(("blk", "col"), None),
        P(("blk", "col"), None, None),
    )
    out_specs = (P(("blk", "col"), None), P(("blk", "col"), None), P())
    return jax.shard_map(
        per_device, mesh=mesh, in_specs=in_specs, out_specs=out_specs, check_vma=False
    )
```

```python
import functools

import jax
import jax.numpy as jnp
from jax import lax
from jax.experimental import pallas as pl
from jax.experimental.pallas import tpu as pltpu
from jax.sharding import PartitionSpec as P

SLOTS = 3
MESH = pl.DeviceIdType.MESH
F32 = jnp.float32
BF16 = jnp.bfloat16


def dot(a, b):
    return jnp.dot(a, b, preferred_element_type=F32)


def kernel(
    dims,
    feat_h, order_h, weight_h, cot_h, list_ref, tiles_h,
    hidden_h, xgrad_h, wgrad_h,
    feat, order, weight, cot, tiles, hidden, xgrad,
    adj, adj_t, feat_t, feat_all, panels, part, part16, agg_in, grads, pg_part, pg16,
    pair_in, both16, chip_in, dw_sum, dw16, dw_in, dw_mid, dw_mid16, dw_col, dw_all,
    in_sem, out_sem, ag_s, ag_r, rc_s, rc_r, gc_s, gc_r, pp_s, pp_r, pc_s, pc_r,
    fe_s, fe_r, dc_s, dc_r, dz_s, dz_r, dg_s, dg_r, dh_s, dh_r, di_s, di_r,
):
    n_blk, n_col, tile, fin, hid, r1, r2, direct = dims
    n_chip = n_blk // 2
    half = hid // 2
    fhalf = fin // 2
    n_own = fhalf // r1
    b = lax.axis_index("blk")
    c = lax.axis_index("col")
    chip = b // 2
    core = b % 2
    sib = b + 1 - 2 * core
    sends = []

    def rows(i, n=tile):
        return pl.ds(pl.multiple_of(i * n, n), n)

    def send(src, dst, s_sem, r_sem, blk, col, only=None, keep=True):
        copy = pltpu.make_async_remote_copy(
            src_ref=src, dst_ref=dst, send_sem=s_sem, recv_sem=r_sem,
            device_id=(blk, col), device_id_type=MESH,
        )
        if only is None:
            copy.start()
        else:
            pl.when(only)(copy.start)
        if keep:
            sends.append((copy, only))

    def arrive(dst, s_sem, r_sem):
        pltpu.make_async_remote_copy(
            src_ref=dst, dst_ref=dst, send_sem=s_sem, recv_sem=r_sem,
            device_id=(sib, c), device_id_type=MESH,
        ).wait_recv()

    def sent(like, s_sem):
        pltpu.make_async_remote_copy(
            src_ref=like, dst_ref=like, send_sem=s_sem, recv_sem=pp_r.at[0],
            device_id=(sib, c), device_id_type=MESH,
        ).wait_send()

    chips = [(k, (chip + k) % n_chip, (chip + n_chip - k) % n_chip) for k in range(1, n_chip)]
    cols = [(k, (c + k) % n_col, (c + n_col - k) % n_col) for k in range(1, n_col)]

    loads = []
    for i, (src, dst) in enumerate(
        ((feat_h, feat), (weight_h, weight), (order_h, order), (tiles_h, tiles), (cot_h, cot))
    ):
        copy = pltpu.make_async_copy(src, dst, in_sem.at[i])
        copy.start()
        loads.append(copy)

    barrier = pltpu.get_barrier_semaphore()
    peers = [(sib, c)]
    peers += [(2 * to + core, c) for _, to, _ in chips]
    peers += [(2 * to + 1 - core, c) for _, to, _ in chips]
    peers += [(b, to) for _, to, _ in cols]
    if direct:
        peers += [(2 * to + core, at) for _, to, _ in chips for _, at, _ in cols]
    for peer in peers:
        pl.semaphore_signal(barrier, inc=1, device_id=peer, device_id_type=MESH)

    loads[0].wait()
    loads[1].wait()
    loads[2].wait()
    place = (
        lax.broadcasted_iota(jnp.int32, (tile, tile), 0) == order[...]
    ).astype(F32).astype(BF16)
    mixed = dot(feat[...], weight[...]).astype(BF16)
    panel = lax.dot_general(
        place, mixed, (((0,), (0,)), ((), ())), preferred_element_type=F32
    ).astype(BF16)
    for h in range(2):
        panels[h, rows(b), :] = panel[:, h * half:(h + 1) * half]
    pl.semaphore_wait(barrier, len(peers))

    for h in range(2):
        at = panels.at[h, rows(b)]
        for k, to, _ in chips:
            send(at, at, ag_s.at[h, 0], ag_r.at[h, b], 2 * to + core, c, keep=False)
        send(at, at, ag_s.at[h, 0], ag_r.at[h, sib], sib, c, keep=False)

    feat_t[...] = lax.dot_general(
        feat[...], place, (((0,), (0,)), ((), ())), preferred_element_type=F32
    ).astype(BF16)
    feat_all[:, rows(b)] = feat_t[rows(core, fhalf), :]

    loads[3].wait()

    def build(g, _):
        held = [tiles[g * SLOTS + s] for s in range(SLOTS)]
        ids = [list_ref[0, g * SLOTS + s] - b * n_col for s in range(SLOTS)]
        for r in range(n_col):
            block = jnp.zeros((tile, tile), BF16)
            for t, i in zip(held, ids):
                block = block + jnp.where(i == r, t, jnp.zeros_like(t))
            adj[r * tile:(r + 1) * tile, rows(g)] = block
        return 0

    lax.fori_loop(0, n_blk, build, 0)
    step = 4 * tile if n_col % 4 == 0 else tile
    for h in range(2):
        for k, _, src in chips:
            at = panels.at[h, rows(2 * src + core)]
            arrive(at, ag_s.at[h, 0], ag_r.at[h, 2 * src + core])
            send(at, at, ag_s.at[h, 0], ag_r.at[h, sib], sib, c, keep=False)
        arrive(panels.at[h, pl.ds(0, n_chip * tile)], ag_s.at[h, 0], ag_r.at[h, b])

        def forward(i, _):
            got = dot(adj[rows(i, step), :], panels[h])
            part[h, rows(i, step), :] = got
            part16[h, rows(i, step), :] = got.astype(BF16)
            return 0

        lax.fori_loop(0, n_col * tile // step, forward, 0)
        for k, to, _ in cols:
            send(
                part16.at[h, rows(to)], agg_in.at[h, rows(c)], rc_s.at[h, 0], rc_r.at[h, 0], b, to,
                keep=False,
            )

    for k, to, _ in chips:
        for q in range(2):
            at = feat_all.at[:, rows(b)]
            send(feat_t.at[pl.ds(q * fhalf, fhalf)], at, fe_s.at[0], fe_r.at[0], 2 * to + q, c, keep=False)
    send(
        feat_t.at[rows(1 - core, fhalf)], feat_all.at[:, rows(b)], fe_s.at[0], fe_r.at[0], sib, c,
        keep=False,
    )

    def turn(g, _):
        for r in range(n_col):
            adj_t[rows(g), r * tile:(r + 1) * tile] = (
                adj[r * tile:(r + 1) * tile, rows(g)].T
            )
        return 0

    turned = adj_t.shape[0] > tile
    if turned:
        lax.fori_loop(0, n_blk, turn, 0)
    loads[4].wait()

    root = 0.7978845608028654
    for h in range(2):
        agg = part[h, rows(c), :]
        arrive(agg_in.at[h, pl.ds(0, (n_col - 1) * tile)], rc_s.at[h, 0], rc_r.at[h, 0])
        for k, _, src in cols:
            agg = agg + agg_in[h, rows(src), :].astype(F32)
        inner = root * (agg + 0.044715 * agg * agg * agg)
        th = jnp.tanh(inner)
        slope = 0.5 * (1.0 + th) + 0.5 * agg * (1.0 - th * th) * (
            root * (1.0 + 3 * 0.044715 * agg * agg)
        )
        lanes = slice(h * half, (h + 1) * half)
        grads[h, rows(c), :] = (cot[:, lanes].astype(F32) * slope).astype(BF16)
        at = grads.at[h, rows(c)]
        for k, to, _ in cols:
            send(at, at, gc_s.at[h, 0], gc_r.at[h, 0], b, to, keep=False)
        hidden[:, lanes] = (0.5 * agg * (1.0 + th)).astype(BF16)
    outs = [pltpu.make_async_copy(hidden, hidden_h, out_sem.at[0])]
    outs[0].start()
    for h in range(2):
        sent(panels.at[h, pl.ds(0, (n_blk - 1) * tile)], ag_s.at[h, 0])
        sent(part16.at[h, pl.ds(0, (n_col - 1) * tile)], rc_s.at[h, 0])

    bstep = 4 * tile if n_blk % 4 == 0 else tile
    others = [
        ((chip + i) % n_chip, (c + j) % n_col, (chip + n_chip - i) % n_chip, (c + n_col - j) % n_col)
        for i in range(n_chip) for j in range(n_col) if i + j > 0
    ]
    mine = chip * n_col + c

    def pair_start(h):
        arrive(grads.at[h, pl.ds(0, (n_col - 1) * tile)], gc_s.at[h, 0], gc_r.at[h, 0])

        def backward(i, _):
            if turned:
                got = dot(adj_t[rows(i, bstep), :], grads[h])
            else:
                got = lax.dot_general(
                    adj[:, rows(i, bstep)], grads[h], (((0,), (0,)), ((), ())),
                    preferred_element_type=F32,
                )
            pg_part[h, rows(i, bstep), :] = got
            pg16[h, rows(i, bstep), :] = got.astype(BF16)
            return 0

        lax.fori_loop(0, n_blk * tile // bstep, backward, 0)
        send(pg16.at[h], pair_in.at[h], pp_s.at[h], pp_r.at[h], sib, c)

    def features_arrive():
        arrive(feat_all.at[:, pl.ds(0, (n_blk - 1) * tile)], fe_s.at[0], fe_r.at[0])

    def terms_start():
        for h in range(2):
            arrive(pair_in.at[h], pp_s.at[h], pp_r.at[h])
            both16[h] = (pg_part[h] + pair_in[h].astype(F32)).astype(BF16)
        for h in range(2):
            term = dot(feat_all[...], both16[h])
            dw_sum[h, 0:fhalf, :] = term
            dw16[h, 0:fhalf, :] = term.astype(BF16)
            if n_chip * r1 > fhalf and not direct:
                rest = jnp.zeros((n_chip * r1 - fhalf, half), F32)
                dw_sum[h, fhalf:, :] = rest
                dw16[h, fhalf:, :] = rest.astype(BF16)
        if direct:
            for to, to_col, _, _ in others:
                owner = to * n_col + to_col
                send(
                    dw16.at[:, rows(owner, r1)], dw_in.at[:, rows(mine, r1)],
                    dc_s.at[0, 0], dc_r.at[0, 0], 2 * to + core, to_col, owner < n_own, keep=False,
                )
            return
        for h in range(2):
            for k, to, _ in chips:
                send(
                    dw16.at[h, rows(to, r1)], dw_in.at[h, rows(chip, r1)],
                    dc_s.at[h, k], dc_r.at[h, chip], 2 * to + core, c,
                )

    def owners_start():
        for k, to, _ in chips:
            send(
                both16.at[:, rows(2 * to + core)], chip_in.at[:, rows(chip)],
                pc_s.at[0, 0], pc_r.at[0, 0], 2 * to + core, c, keep=False,
            )

    def result_direct():
        count = len(others) * r1

        @pl.when(mine < n_own)
        def _():
            arrive(dw_in.at[:, pl.ds(0, count)], dc_s.at[0, 0], dc_r.at[0, 0])
            piece = dw_sum[:, rows(mine, r1), :]
            for _, _, src, src_col in others:
                piece = piece + dw_in[:, rows(src * n_col + src_col, r1), :].astype(F32)
            dw_all[core, :, rows(mine, r1), :] = piece.astype(BF16)

        at = dw_all.at[core, :, rows(mine, r1)]
        for to, to_col, _, _ in others:
            send(
                at, at, dg_s.at[0, 0], dg_r.at[0, 0], 2 * to + core, to_col, mine < n_own,
                keep=False,
            )

    def pass_direct():
        for owns in range(2):
            rest = (n_own - owns) * r1

            @pl.when((mine < n_own) == bool(owns))
            def _():
                sent(dw16.at[:, pl.ds(0, rest)], dc_s.at[0, 0])
                arrive(dw_all.at[core, :, pl.ds(0, rest)], dg_s.at[0, 0], dg_r.at[0, 0])

        send(dw_all.at[core], dw_all.at[core], di_s.at[0, 0], di_r.at[0, 0], sib, c)

    def result_start(h):
        piece = dw_sum[h, rows(chip, r1), :]
        for k, _, src in chips:
            arrive(dw_in.at[h, rows(src, r1)], dc_s.at[h, k], dc_r.at[h, src])
            piece = piece + dw_in[h, rows(src, r1), :].astype(F32)
        dw_mid[h, 0:r1, :] = piece
        dw_mid16[h, 0:r1, :] = piece.astype(BF16)
        if n_col * r2 > r1:
            rest = jnp.zeros((n_col * r2 - r1, half), F32)
            dw_mid[h, r1:, :] = rest
            dw_mid16[h, r1:, :] = rest.astype(BF16)
        for k, to, _ in cols:
            send(
                dw_mid16.at[h, rows(to, r2)], dw_col.at[h, rows(c, r2)],
                dz_s.at[h, k], dz_r.at[h, c], b, to,
            )
        piece = dw_mid[h, rows(c, r2), :]
        for k, _, src in cols:
            arrive(dw_col.at[h, rows(src, r2)], dz_s.at[h, k], dz_r.at[h, src])
            piece = piece + dw_col[h, rows(src, r2), :].astype(F32)
        dw_all[core, h, chip, rows(c, r2), :] = piece.astype(BF16)
        at = dw_all.at[core, h, chip, rows(c, r2)]
        for k, to, _ in cols:
            send(at, at, dg_s.at[h, k], dg_r.at[h, c], b, to)
        for k, _, src in cols:
            at = dw_all.at[core, h, chip, rows(src, r2)]
            arrive(at, dg_s.at[h, k], dg_r.at[h, src])
        at = dw_all.at[core, h, chip, pl.ds(0, r1)]
        for k, to, _ in chips:
            send(at, at, dh_s.at[h, k], dh_r.at[h, chip], 2 * to + core, c)
        send(at, at, di_s.at[h, chip], di_r.at[h, chip], sib, c)

    def result_pass(h):
        for k, _, src in chips:
            at = dw_all.at[core, h, src, pl.ds(0, r1)]
            arrive(at, dh_s.at[h, k], dh_r.at[h, src])
            send(at, at, di_s.at[h, src], di_r.at[h, src], sib, c)

    def result_arrive(h):
        for src in range(n_chip):
            at = dw_all.at[1 - core, h, src, pl.ds(0, r1)]
            arrive(at, di_s.at[h, src], di_r.at[h, src])

    def own_features():
        sums = []
        arrive(chip_in.at[:, pl.ds(0, (n_chip - 1) * tile)], pc_s.at[0, 0], pc_r.at[0, 0])
        for h in range(2):
            total = pg_part[h, rows(b), :] + pair_in[h, rows(b), :].astype(F32)
            for k, _, src in chips:
                total = total + chip_in[h, rows(src), :].astype(F32)
            sums.append(total.astype(BF16))
        back = dot(place, jnp.concatenate(sums, axis=1)).astype(BF16)
        xgrad[...] = lax.dot_general(
            back, weight[...], (((1,), (1,)), ((), ())), preferred_element_type=F32
        ).astype(BF16)
        outs.append(pltpu.make_async_copy(xgrad, xgrad_h, out_sem.at[1]))
        outs[1].start()

    pair_start(0)
    pair_start(1)
    features_arrive()
    terms_start()
    owners_start()
    for h in range(2):
        sent(grads.at[h, pl.ds(0, (n_col - 1) * tile)], gc_s.at[h, 0])
    sent(feat_all.at[:, pl.ds(0, (n_blk - 1) * tile)], fe_s.at[0])
    if direct:
        result_direct()
        own_features()
        pass_direct()
        arrive(dw_all.at[1 - core], di_s.at[0, 0], di_r.at[0, 0])
    else:
        result_start(0)
        result_start(1)
        own_features()
        result_pass(0)
        result_pass(1)
        result_arrive(0)
        result_arrive(1)
    if direct:
        outs.append(pltpu.make_async_copy(dw_all, wgrad_h, out_sem.at[2]))
    else:
        outs.append(
            pltpu.make_async_copy(dw_all.at[:, :, :, pl.ds(0, r1)], wgrad_h, out_sem.at[2])
        )
    outs[2].start()
    sent(both16.at[:, pl.ds(0, (n_chip - 1) * tile)], pc_s.at[0, 0])
    if direct:
        @pl.when(mine < n_own)
        def _():
            sent(dw_in.at[:, pl.ds(0, len(others) * r1)], dg_s.at[0, 0])

    for copy, only in sends:
        if only is None:
            copy.wait_send()
        else:
            pl.when(only)(copy.wait_send)
    for copy in outs:
        copy.wait()


def finish(scale, r1, hidden_in, xgrad_in, wgrad_in, hidden_ref, xgrad_ref, wgrad_ref):
    hidden_ref[...] = hidden_in[...]
    xgrad_ref[...] = xgrad_in[...]
    n_part, half = wgrad_in.shape[2], wgrad_in.shape[4]
    fhalf = wgrad_ref.shape[0] // 2
    for core in range(2):
        for i in range(n_part):
            count = min(r1, fhalf - i * r1)
            if count > 0:
                start = core * fhalf + i * r1
                for h in range(2):
                    wgrad_ref[start:start + count, h * half:(h + 1) * half] = (
                        wgrad_in[core, h, i, 0:count, :].astype(F32) * scale
                    )


def per_device(features, node_order, weight, cotangent, tile_list, tile_values):
    n_blk, n_col = lax.axis_size("blk"), lax.axis_size("col")
    slots, tile, _ = tile_values.shape
    fin, hid = weight.shape
    n_chip = n_blk // 2
    half, fhalf = hid // 2, fin // 2
    scale = float(n_blk * n_col * tile) ** -0.5
    direct = n_chip * n_col <= 16
    n_sum = n_chip * n_col if direct else n_chip
    r1 = -(-fhalf // (16 * n_sum)) * 16
    direct = direct and fhalf % r1 == 0
    r2 = 16 if direct else -(-r1 // (16 * n_col)) * 16
    padded = fhalf if direct else n_chip * r1
    dma = lambda *n: pltpu.SemaphoreType.DMA(n)
    vmem = pltpu.VMEM
    wide, tall = n_blk * tile, n_col * tile
    turned = wide * tall <= 2 ** 21
    scratch = [
        vmem((tile, fin), BF16), vmem((1, tile), jnp.int32), vmem((fin, hid), BF16),
        vmem((tile, hid), BF16), vmem((slots, tile, tile), BF16),
        vmem((tile, hid), BF16), vmem((tile, fin), BF16),
        vmem((tall, wide), BF16), vmem((wide if turned else tile, tall), BF16),
        vmem((fin, tile), BF16), vmem((fhalf, wide), BF16),
        vmem((2, wide, half), BF16),
        vmem((2, tall, half), F32), vmem((2, tall, half), BF16), vmem((2, tall, half), BF16),
        vmem((2, tall, half), BF16),
        vmem((2, wide, half), F32), vmem((2, wide, half), BF16), vmem((2, wide, half), BF16),
        vmem((2, wide, half), BF16), vmem((2, n_chip * tile, half), BF16),
        vmem((2, padded, half), F32), vmem((2, padded, half), BF16),
        vmem((2, n_sum * r1, half), BF16),
        vmem((2, n_col * r2, half), F32), vmem((2, n_col * r2, half), BF16),
        vmem((2, n_col * r2, half), BF16), vmem((2, 2, fhalf, half) if direct else (2, 2, n_chip, n_col * r2, half), BF16),
        dma(5), dma(3), dma(2, 2 * n_chip), dma(2, n_blk),
        dma(2, n_col), dma(2, n_col), dma(2, n_col), dma(2, n_col),
        dma(2), dma(2), dma(2, n_chip), dma(2, n_chip),
        dma(2 * n_chip), dma(n_blk), dma(2, n_sum), dma(2, n_sum),
        dma(2, n_col), dma(2, n_col), dma(2, n_sum + n_col), dma(2, n_sum + n_col),
        dma(2, n_chip), dma(2, n_chip), dma(2, n_sum), dma(2, n_sum),
    ]
    far = pl.BlockSpec(memory_space=pltpu.HBM)
    free = pl.BlockSpec(memory_space=pl.ANY)
    inside = pl.BlockSpec(memory_space=pltpu.VMEM)
    limit = 60 * 1024 * 1024
    hidden, xgrad, wgrad = pl.pallas_call(
        functools.partial(kernel, (n_blk, n_col, tile, fin, hid, r1, r2, direct)),
        out_shape=(
            jax.ShapeDtypeStruct((tile, hid), BF16),
            jax.ShapeDtypeStruct((tile, fin), BF16),
            jax.ShapeDtypeStruct(
                (2, 2, fhalf, half) if direct else (2, 2, n_chip, r1, half), BF16
            ),
        ),
        in_specs=[far, far, far, far, pl.BlockSpec(memory_space=pltpu.SMEM), far],
        out_specs=(free, free, free),
        scratch_shapes=scratch,
        compiler_params=pltpu.CompilerParams(
            collective_id=0, has_side_effects=True, vmem_limit_bytes=limit
        ),
        cost_estimate=pl.CostEstimate(
            flops=4 * slots * tile * tile * hid, bytes_accessed=4 * 1024 * 1024,
            transcendentals=tile * hid,
        ),
    )(features, node_order, weight, cotangent, tile_list.T, tile_values)
    if direct:
        wgrad, r1 = wgrad.reshape(2, 2, 1, fhalf, half), fhalf
    return pl.pallas_call(
        functools.partial(finish, scale, r1),
        out_shape=(
            jax.ShapeDtypeStruct((tile, hid), BF16),
            jax.ShapeDtypeStruct((tile, fin), BF16),
            jax.ShapeDtypeStruct((fin, hid), F32),
        ),
        in_specs=[inside] * 3,
        out_specs=(inside,) * 3,
        compiler_params=pltpu.CompilerParams(vmem_limit_bytes=limit),
    )(hidden, xgrad, wgrad)


def solution(mesh):
    in_specs = (
        P(("blk", "col"), None),
        P(("blk", "col"), None),
        P(),
        P(("blk", "col"), None),
        P(("blk", "col"), None),
        P(("blk", "col"), None, None),
    )
    out_specs = (P(("blk", "col"), None), P(("blk", "col"), None), P())
    return jax.shard_map(
        per_device, mesh=mesh, in_specs=in_specs, out_specs=out_specs, check_vma=False
    )
```

```python
import functools

import jax
import jax.numpy as jnp
from jax import lax
from jax.experimental import pallas as pl
from jax.experimental.pallas import tpu as pltpu
from jax.sharding import PartitionSpec as P

SLOTS = 3
MESH = pl.DeviceIdType.MESH
F32 = jnp.float32
BF16 = jnp.bfloat16


def dot(a, b):
    return jnp.dot(a, b, preferred_element_type=F32)


def kernel(
    dims,
    feat_h, order_h, weight_h, cot_h, list_ref, tiles_h,
    hidden_h, xgrad_h, wgrad_h,
    feat, order, weight, cot, tiles, hidden, xgrad,
    adj, adj_t, feat_t, feat_all, panels, part, part16, agg_in, grads, pg_part, pg16,
    pair_in, both16, chip_in, dw_sum, dw16, dw_in, dw_mid, dw_mid16, dw_col, dw_all,
    in_sem, out_sem, ag_s, ag_r, rc_s, rc_r, gc_s, gc_r, pp_s, pp_r, pc_s, pc_r,
    fe_s, fe_r, dc_s, dc_r, dz_s, dz_r, dg_s, dg_r, dh_s, dh_r, di_s, di_r,
):
    n_blk, n_col, tile, fin, hid, r1, r2, direct = dims
    n_chip = n_blk // 2
    half = hid // 2
    fhalf = fin // 2
    n_own = fhalf // r1
    b = lax.axis_index("blk")
    c = lax.axis_index("col")
    chip = b // 2
    core = b % 2
    sib = b + 1 - 2 * core
    sends = []

    def rows(i, n=tile):
        return pl.ds(pl.multiple_of(i * n, n), n)

    def send(src, dst, s_sem, r_sem, blk, col, only=None, keep=True):
        copy = pltpu.make_async_remote_copy(
            src_ref=src, dst_ref=dst, send_sem=s_sem, recv_sem=r_sem,
            device_id=(blk, col), device_id_type=MESH,
        )
        if only is None:
            copy.start()
        else:
            pl.when(only)(copy.start)
        if keep:
            sends.append((copy, only))

    def arrive(dst, s_sem, r_sem):
        pltpu.make_async_remote_copy(
            src_ref=dst, dst_ref=dst, send_sem=s_sem, recv_sem=r_sem,
            device_id=(sib, c), device_id_type=MESH,
        ).wait_recv()

    def sent(like, s_sem):
        pltpu.make_async_remote_copy(
            src_ref=like, dst_ref=like, send_sem=s_sem, recv_sem=pp_r.at[0],
            device_id=(sib, c), device_id_type=MESH,
        ).wait_send()

    chips = [(k, (chip + k) % n_chip, (chip + n_chip - k) % n_chip) for k in range(1, n_chip)]
    cols = [(k, (c + k) % n_col, (c + n_col - k) % n_col) for k in range(1, n_col)]

    loads = []
    for i, (src, dst) in enumerate(
        ((feat_h, feat), (weight_h, weight), (order_h, order), (tiles_h, tiles), (cot_h, cot))
    ):
        copy = pltpu.make_async_copy(src, dst, in_sem.at[i])
        copy.start()
        loads.append(copy)

    barrier = pltpu.get_barrier_semaphore()
    peers = [(sib, c)]
    peers += [(2 * to + core, c) for _, to, _ in chips]
    peers += [(2 * to + 1 - core, c) for _, to, _ in chips]
    peers += [(b, to) for _, to, _ in cols]
    if direct:
        peers += [(2 * to + core, at) for _, to, _ in chips for _, at, _ in cols]
    for peer in peers:
        pl.semaphore_signal(barrier, inc=1, device_id=peer, device_id_type=MESH)

    loads[0].wait()
    loads[1].wait()
    loads[2].wait()
    place = (
        lax.broadcasted_iota(jnp.int32, (tile, tile), 0) == order[...]
    ).astype(F32).astype(BF16)
    mixed = dot(feat[...], weight[...]).astype(BF16)
    panel = lax.dot_general(
        place, mixed, (((0,), (0,)), ((), ())), preferred_element_type=F32
    ).astype(BF16)
    for h in range(2):
        panels[h, rows(b), :] = panel[:, h * half:(h + 1) * half]
    pl.semaphore_wait(barrier, len(peers))

    for h in range(2):
        at = panels.at[h, rows(b)]
        for k, to, _ in chips:
            send(at, at, ag_s.at[h, 0], ag_r.at[h, b], 2 * to + core, c, keep=False)
        send(at, at, ag_s.at[h, 0], ag_r.at[h, sib], sib, c, keep=False)

    feat_t[...] = lax.dot_general(
        feat[...], place, (((0,), (0,)), ((), ())), preferred_element_type=F32
    ).astype(BF16)
    feat_all[:, rows(b)] = feat_t[rows(core, fhalf), :]

    loads[3].wait()

    def build(g, _):
        held = [tiles[g * SLOTS + s] for s in range(SLOTS)]
        ids = [list_ref[0, g * SLOTS + s] - b * n_col for s in range(SLOTS)]
        for r in range(n_col):
            block = jnp.zeros((tile, tile), BF16)
            for t, i in zip(held, ids):
                block = block + jnp.where(i == r, t, jnp.zeros_like(t))
            adj[r * tile:(r + 1) * tile, rows(g)] = block
        return 0

    lax.fori_loop(0, n_blk, build, 0)
    step = 4 * tile if n_col % 4 == 0 else tile
    for h in range(2):
        for k, _, src in chips:
            at = panels.at[h, rows(2 * src + core)]
            arrive(at, ag_s.at[h, 0], ag_r.at[h, 2 * src + core])
            send(at, at, ag_s.at[h, 0], ag_r.at[h, sib], sib, c, keep=False)
        arrive(panels.at[h, pl.ds(0, n_chip * tile)], ag_s.at[h, 0], ag_r.at[h, b])

        def forward(i, _):
            got = dot(adj[rows(i, step), :], panels[h])
            part[h, rows(i, step), :] = got
            part16[h, rows(i, step), :] = got.astype(BF16)
            return 0

        lax.fori_loop(0, n_col * tile // step, forward, 0)
        for k, to, _ in cols:
            send(
                part16.at[h, rows(to)], agg_in.at[h, rows(c)], rc_s.at[h, 0], rc_r.at[h, 0], b, to,
                keep=False,
            )

    for k, to, _ in chips:
        for q in range(2):
            at = feat_all.at[:, rows(b)]
            send(feat_t.at[pl.ds(q * fhalf, fhalf)], at, fe_s.at[0], fe_r.at[0], 2 * to + q, c, keep=False)
    send(
        feat_t.at[rows(1 - core, fhalf)], feat_all.at[:, rows(b)], fe_s.at[0], fe_r.at[0], sib, c,
        keep=False,
    )

    def turn(g, _):
        for r in range(n_col):
            adj_t[rows(g), r * tile:(r + 1) * tile] = (
                adj[r * tile:(r + 1) * tile, rows(g)].T
            )
        return 0

    turned = adj_t.shape[0] > tile
    if turned:
        lax.fori_loop(0, n_blk, turn, 0)
    loads[4].wait()

    root = 0.7978845608028654
    for h in range(2):
        agg = part[h, rows(c), :]
        arrive(agg_in.at[h, pl.ds(0, (n_col - 1) * tile)], rc_s.at[h, 0], rc_r.at[h, 0])
        for k, _, src in cols:
            agg = agg + agg_in[h, rows(src), :].astype(F32)
        inner = root * (agg + 0.044715 * agg * agg * agg)
        th = jnp.tanh(inner)
        slope = 0.5 * (1.0 + th) + 0.5 * agg * (1.0 - th * th) * (
            root * (1.0 + 3 * 0.044715 * agg * agg)
        )
        lanes = slice(h * half, (h + 1) * half)
        grads[h, rows(c), :] = (cot[:, lanes].astype(F32) * slope).astype(BF16)
        at = grads.at[h, rows(c)]
        for k, to, _ in cols:
            send(at, at, gc_s.at[h, 0], gc_r.at[h, 0], b, to, keep=False)
        hidden[:, lanes] = (0.5 * agg * (1.0 + th)).astype(BF16)
    outs = [pltpu.make_async_copy(hidden, hidden_h, out_sem.at[0])]
    outs[0].start()
    for h in range(2):
        sent(panels.at[h, pl.ds(0, (n_blk - 1) * tile)], ag_s.at[h, 0])
        sent(part16.at[h, pl.ds(0, (n_col - 1) * tile)], rc_s.at[h, 0])

    bstep = 4 * tile if n_blk % 4 == 0 else tile
    others = [
        ((chip + i) % n_chip, (c + j) % n_col, (chip + n_chip - i) % n_chip, (c + n_col - j) % n_col)
        for i in range(n_chip) for j in range(n_col) if i + j > 0
    ]
    mine = chip * n_col + c

    def pair_start(h):
        arrive(grads.at[h, pl.ds(0, (n_col - 1) * tile)], gc_s.at[h, 0], gc_r.at[h, 0])

        def backward(i, _):
            if turned:
                got = dot(adj_t[rows(i, bstep), :], grads[h])
            else:
                got = lax.dot_general(
                    adj[:, rows(i, bstep)], grads[h], (((0,), (0,)), ((), ())),
                    preferred_element_type=F32,
                )
            pg_part[h, rows(i, bstep), :] = got
            pg16[h, rows(i, bstep), :] = got.astype(BF16)
            return 0

        lax.fori_loop(0, n_blk * tile // bstep, backward, 0)
        send(pg16.at[h], pair_in.at[h], pp_s.at[h], pp_r.at[h], sib, c)

    def features_arrive():
        arrive(feat_all.at[:, pl.ds(0, (n_blk - 1) * tile)], fe_s.at[0], fe_r.at[0])

    def terms_start(h):
        arrive(pair_in.at[h], pp_s.at[h], pp_r.at[h])
        both16[h] = (pg_part[h] + pair_in[h].astype(F32)).astype(BF16)
        term = dot(feat_all[...], both16[h])
        dw_sum[h, 0:fhalf, :] = term
        dw16[h, 0:fhalf, :] = term.astype(BF16)
        if direct:
            for to, to_col, _, _ in others:
                owner = to * n_col + to_col
                send(
                    dw16.at[h, rows(owner, r1)], dw_in.at[h, rows(mine, r1)],
                    dc_s.at[h, 0], dc_r.at[h, 0], 2 * to + core, to_col, owner < n_own, keep=False,
                )
            return
        if n_chip * r1 > fhalf:
            rest = jnp.zeros((n_chip * r1 - fhalf, half), F32)
            dw_sum[h, fhalf:, :] = rest
            dw16[h, fhalf:, :] = rest.astype(BF16)
        for k, to, _ in chips:
            send(
                dw16.at[h, rows(to, r1)], dw_in.at[h, rows(chip, r1)],
                dc_s.at[h, k], dc_r.at[h, chip], 2 * to + core, c,
            )

    def owners_start():
        for k, to, _ in chips:
            send(
                both16.at[:, rows(2 * to + core)], chip_in.at[:, rows(chip)],
                pc_s.at[0, 0], pc_r.at[0, 0], 2 * to + core, c, keep=False,
            )

    def result_direct(h):
        count = len(others) * r1

        @pl.when(mine < n_own)
        def _():
            arrive(dw_in.at[h, pl.ds(0, count)], dc_s.at[h, 0], dc_r.at[h, 0])
            piece = dw_sum[h, rows(mine, r1), :]
            for _, _, src, src_col in others:
                piece = piece + dw_in[h, rows(src * n_col + src_col, r1), :].astype(F32)
            dw_all[core, h, rows(mine, r1), :] = piece.astype(BF16)

        at = dw_all.at[core, h, rows(mine, r1)]
        for to, to_col, _, _ in others:
            send(
                at, at, dg_s.at[h, 0], dg_r.at[h, 0], 2 * to + core, to_col, mine < n_own,
                keep=False,
            )

    def pass_direct(h):
        for owns in range(2):
            rest = (n_own - owns) * r1

            @pl.when((mine < n_own) == bool(owns))
            def _():
                sent(dw16.at[h, pl.ds(0, rest)], dc_s.at[h, 0])
                arrive(dw_all.at[core, h, pl.ds(0, rest)], dg_s.at[h, 0], dg_r.at[h, 0])

        at = dw_all.at[core, h]
        send(at, at, di_s.at[h, 0], di_r.at[h, 0], sib, c)

    def result_start(h):
        piece = dw_sum[h, rows(chip, r1), :]
        for k, _, src in chips:
            arrive(dw_in.at[h, rows(src, r1)], dc_s.at[h, k], dc_r.at[h, src])
            piece = piece + dw_in[h, rows(src, r1), :].astype(F32)
        dw_mid[h, 0:r1, :] = piece
        dw_mid16[h, 0:r1, :] = piece.astype(BF16)
        if n_col * r2 > r1:
            rest = jnp.zeros((n_col * r2 - r1, half), F32)
            dw_mid[h, r1:, :] = rest
            dw_mid16[h, r1:, :] = rest.astype(BF16)
        for k, to, _ in cols:
            send(
                dw_mid16.at[h, rows(to, r2)], dw_col.at[h, rows(c, r2)],
                dz_s.at[h, k], dz_r.at[h, c], b, to,
            )
        piece = dw_mid[h, rows(c, r2), :]
        for k, _, src in cols:
            arrive(dw_col.at[h, rows(src, r2)], dz_s.at[h, k], dz_r.at[h, src])
            piece = piece + dw_col[h, rows(src, r2), :].astype(F32)
        dw_all[core, h, chip, rows(c, r2), :] = piece.astype(BF16)
        at = dw_all.at[core, h, chip, rows(c, r2)]
        for k, to, _ in cols:
            send(at, at, dg_s.at[h, k], dg_r.at[h, c], b, to)
        for k, _, src in cols:
            at = dw_all.at[core, h, chip, rows(src, r2)]
            arrive(at, dg_s.at[h, k], dg_r.at[h, src])
        at = dw_all.at[core, h, chip, pl.ds(0, r1)]
        for k, to, _ in chips:
            send(at, at, dh_s.at[h, k], dh_r.at[h, chip], 2 * to + core, c)
        send(at, at, di_s.at[h, chip], di_r.at[h, chip], sib, c)

    def result_pass(h):
        for k, _, src in chips:
            at = dw_all.at[core, h, src, pl.ds(0, r1)]
            arrive(at, dh_s.at[h, k], dh_r.at[h, src])
            send(at, at, di_s.at[h, src], di_r.at[h, src], sib, c)

    def result_arrive(h):
        for src in range(n_chip):
            at = dw_all.at[1 - core, h, src, pl.ds(0, r1)]
            arrive(at, di_s.at[h, src], di_r.at[h, src])

    def own_features():
        sums = []
        arrive(chip_in.at[:, pl.ds(0, (n_chip - 1) * tile)], pc_s.at[0, 0], pc_r.at[0, 0])
        for h in range(2):
            total = pg_part[h, rows(b), :] + pair_in[h, rows(b), :].astype(F32)
            for k, _, src in chips:
                total = total + chip_in[h, rows(src), :].astype(F32)
            sums.append(total.astype(BF16))
        back = dot(place, jnp.concatenate(sums, axis=1)).astype(BF16)
        xgrad[...] = lax.dot_general(
            back, weight[...], (((1,), (1,)), ((), ())), preferred_element_type=F32
        ).astype(BF16)
        outs.append(pltpu.make_async_copy(xgrad, xgrad_h, out_sem.at[1]))
        outs[1].start()

    pair_start(0)
    pair_start(1)
    features_arrive()
    terms_start(0)
    terms_start(1)
    owners_start()
    for h in range(2):
        sent(grads.at[h, pl.ds(0, (n_col - 1) * tile)], gc_s.at[h, 0])
    if direct:
        result_direct(0)
        result_direct(1)
        own_features()
        pass_direct(0)
        pass_direct(1)
        for h in range(2):
            arrive(dw_all.at[1 - core, h], di_s.at[h, 0], di_r.at[h, 0])
    else:
        result_start(0)
        result_start(1)
        own_features()
        result_pass(0)
        result_pass(1)
        result_arrive(0)
        result_arrive(1)
    if direct:
        outs.append(pltpu.make_async_copy(dw_all, wgrad_h, out_sem.at[2]))
    else:
        outs.append(
            pltpu.make_async_copy(dw_all.at[:, :, :, pl.ds(0, r1)], wgrad_h, out_sem.at[2])
        )
    outs[2].start()
    sent(both16.at[:, pl.ds(0, (n_chip - 1) * tile)], pc_s.at[0, 0])
    sent(feat_all.at[:, pl.ds(0, (n_blk - 1) * tile)], fe_s.at[0])
    if direct:
        @pl.when(mine < n_own)
        def _():
            for h in range(2):
                sent(dw_in.at[h, pl.ds(0, len(others) * r1)], dg_s.at[h, 0])

    for copy, only in sends:
        if only is None:
            copy.wait_send()
        else:
            pl.when(only)(copy.wait_send)
    for copy in outs:
        copy.wait()


def finish(scale, r1, hidden_in, xgrad_in, wgrad_in, hidden_ref, xgrad_ref, wgrad_ref):
    hidden_ref[...] = hidden_in[...]
    xgrad_ref[...] = xgrad_in[...]
    n_part, half = wgrad_in.shape[2], wgrad_in.shape[4]
    fhalf = wgrad_ref.shape[0] // 2
    for core in range(2):
        for i in range(n_part):
            count = min(r1, fhalf - i * r1)
            if count > 0:
                start = core * fhalf + i * r1
                for h in range(2):
                    wgrad_ref[start:start + count, h * half:(h + 1) * half] = (
                        wgrad_in[core, h, i, 0:count, :].astype(F32) * scale
                    )


def per_device(features, node_order, weight, cotangent, tile_list, tile_values):
    n_blk, n_col = lax.axis_size("blk"), lax.axis_size("col")
    slots, tile, _ = tile_values.shape
    fin, hid = weight.shape
    n_chip = n_blk // 2
    half, fhalf = hid // 2, fin // 2
    scale = float(n_blk * n_col * tile) ** -0.5
    direct = n_chip * n_col <= 16
    n_sum = n_chip * n_col if direct else n_chip
    r1 = -(-fhalf // (16 * n_sum)) * 16
    direct = direct and fhalf % r1 == 0
    r2 = 16 if direct else -(-r1 // (16 * n_col)) * 16
    padded = fhalf if direct else n_chip * r1
    dma = lambda *n: pltpu.SemaphoreType.DMA(n)
    vmem = pltpu.VMEM
    wide, tall = n_blk * tile, n_col * tile
    turned = wide * tall <= 2 ** 21
    scratch = [
        vmem((tile, fin), BF16), vmem((1, tile), jnp.int32), vmem((fin, hid), BF16),
        vmem((tile, hid), BF16), vmem((slots, tile, tile), BF16),
        vmem((tile, hid), BF16), vmem((tile, fin), BF16),
        vmem((tall, wide), BF16), vmem((wide if turned else tile, tall), BF16),
        vmem((fin, tile), BF16), vmem((fhalf, wide), BF16),
        vmem((2, wide, half), BF16),
        vmem((2, tall, half), F32), vmem((2, tall, half), BF16), vmem((2, tall, half), BF16),
        vmem((2, tall, half), BF16),
        vmem((2, wide, half), F32), vmem((2, wide, half), BF16), vmem((2, wide, half), BF16),
        vmem((2, wide, half), BF16), vmem((2, n_chip * tile, half), BF16),
        vmem((2, padded, half), F32), vmem((2, padded, half), BF16),
        vmem((2, n_sum * r1, half), BF16),
        vmem((2, n_col * r2, half), F32), vmem((2, n_col * r2, half), BF16),
        vmem((2, n_col * r2, half), BF16), vmem((2, 2, fhalf, half) if direct else (2, 2, n_chip, n_col * r2, half), BF16),
        dma(5), dma(3), dma(2, 2 * n_chip), dma(2, n_blk),
        dma(2, n_col), dma(2, n_col), dma(2, n_col), dma(2, n_col),
        dma(2), dma(2), dma(2, n_chip), dma(2, n_chip),
        dma(2 * n_chip), dma(n_blk), dma(2, n_sum), dma(2, n_sum),
        dma(2, n_col), dma(2, n_col), dma(2, n_sum + n_col), dma(2, n_sum + n_col),
        dma(2, n_chip), dma(2, n_chip), dma(2, n_sum), dma(2, n_sum),
    ]
    far = pl.BlockSpec(memory_space=pltpu.HBM)
    free = pl.BlockSpec(memory_space=pl.ANY)
    inside = pl.BlockSpec(memory_space=pltpu.VMEM)
    limit = 60 * 1024 * 1024
    hidden, xgrad, wgrad = pl.pallas_call(
        functools.partial(kernel, (n_blk, n_col, tile, fin, hid, r1, r2, direct)),
        out_shape=(
            jax.ShapeDtypeStruct((tile, hid), BF16),
            jax.ShapeDtypeStruct((tile, fin), BF16),
            jax.ShapeDtypeStruct(
                (2, 2, fhalf, half) if direct else (2, 2, n_chip, r1, half), BF16
            ),
        ),
        in_specs=[far, far, far, far, pl.BlockSpec(memory_space=pltpu.SMEM), far],
        out_specs=(free, free, free),
        scratch_shapes=scratch,
        compiler_params=pltpu.CompilerParams(
            collective_id=0, has_side_effects=True, vmem_limit_bytes=limit
        ),
        cost_estimate=pl.CostEstimate(
            flops=4 * slots * tile * tile * hid, bytes_accessed=4 * 1024 * 1024,
            transcendentals=tile * hid,
        ),
    )(features, node_order, weight, cotangent, tile_list.T, tile_values)
    if direct:
        wgrad, r1 = wgrad.reshape(2, 2, 1, fhalf, half), fhalf
    return pl.pallas_call(
        functools.partial(finish, scale, r1),
        out_shape=(
            jax.ShapeDtypeStruct((tile, hid), BF16),
            jax.ShapeDtypeStruct((tile, fin), BF16),
            jax.ShapeDtypeStruct((fin, hid), F32),
        ),
        in_specs=[inside] * 3,
        out_specs=(inside,) * 3,
        compiler_params=pltpu.CompilerParams(vmem_limit_bytes=limit),
    )(hidden, xgrad, wgrad)


def solution(mesh):
    in_specs = (
        P(("blk", "col"), None),
        P(("blk", "col"), None),
        P(),
        P(("blk", "col"), None),
        P(("blk", "col"), None),
        P(("blk", "col"), None, None),
    )
    out_specs = (P(("blk", "col"), None), P(("blk", "col"), None), P())
    return jax.shard_map(
        per_device, mesh=mesh, in_specs=in_specs, out_specs=out_specs, check_vma=False
    )
```

```python
import functools

import jax
import jax.numpy as jnp
from jax import lax
from jax.experimental import pallas as pl
from jax.experimental.pallas import tpu as pltpu
from jax.sharding import PartitionSpec as P

SLOTS = 3
MESH = pl.DeviceIdType.MESH
F32 = jnp.float32
BF16 = jnp.bfloat16


def dot(a, b):
    return jnp.dot(a, b, preferred_element_type=F32)


def kernel(
    dims,
    feat_h, order_h, weight_h, cot_h, list_ref, tiles_h,
    hidden_h, xgrad_h, wgrad_h,
    feat, order, weight, cot, tiles, hidden, xgrad,
    adj, adj_t, feat_t, feat_all, panels, part, part16, agg_in, grads, pg_part, pg16,
    pair_in, both16, chip_in, dw_sum, dw16, dw_in, dw_mid, dw_mid16, dw_col, dw_all, relay_in, relay_out,
    in_sem, out_sem, ag_s, ag_r, rc_s, rc_r, gc_s, gc_r, pp_s, pp_r, pc_s, pc_r,
    fe_s, fe_r, dc_s, dc_r, dz_s, dz_r, dg_s, dg_r, dh_s, dh_r, di_s, di_r, rl_s, rl_r,
):
    n_blk, n_col, tile, fin, hid, r1, r2, direct = dims
    n_chip = n_blk // 2
    half = hid // 2
    fhalf = fin // 2
    n_own = fhalf // r1
    b = lax.axis_index("blk")
    c = lax.axis_index("col")
    chip = b // 2
    core = b % 2
    sib = b + 1 - 2 * core
    sends = []

    def rows(i, n=tile):
        return pl.ds(pl.multiple_of(i * n, n), n)

    def send(src, dst, s_sem, r_sem, blk, col, only=None, keep=True):
        copy = pltpu.make_async_remote_copy(
            src_ref=src, dst_ref=dst, send_sem=s_sem, recv_sem=r_sem,
            device_id=(blk, col), device_id_type=MESH,
        )
        if only is None:
            copy.start()
        else:
            pl.when(only)(copy.start)
        if keep:
            sends.append((copy, only))

    def arrive(dst, s_sem, r_sem):
        pltpu.make_async_remote_copy(
            src_ref=dst, dst_ref=dst, send_sem=s_sem, recv_sem=r_sem,
            device_id=(sib, c), device_id_type=MESH,
        ).wait_recv()

    def sent(like, s_sem):
        pltpu.make_async_remote_copy(
            src_ref=like, dst_ref=like, send_sem=s_sem, recv_sem=pp_r.at[0],
            device_id=(sib, c), device_id_type=MESH,
        ).wait_send()

    chips = [(k, (chip + k) % n_chip, (chip + n_chip - k) % n_chip) for k in range(1, n_chip)]
    cols = [(k, (c + k) % n_col, (c + n_col - k) % n_col) for k in range(1, n_col)]

    line = n_col == 4
    ends = c % 3 == 0
    far = 3 * (c % 2)
    if line:
        for h in range(2):
            @pl.when(ends)
            def _():
                agg_in[h, rows(3 - c), :] = jnp.zeros((tile, half), BF16)

    loads = []
    for i, (src, dst) in enumerate(
        ((feat_h, feat), (weight_h, weight), (order_h, order), (tiles_h, tiles), (cot_h, cot))
    ):
        copy = pltpu.make_async_copy(src, dst, in_sem.at[i])
        copy.start()
        loads.append(copy)

    barrier = pltpu.get_barrier_semaphore()
    peers = [(sib, c)]
    peers += [(2 * to + core, c) for _, to, _ in chips]
    peers += [(2 * to + 1 - core, c) for _, to, _ in chips]
    peers += [(b, to) for _, to, _ in cols]
    if direct:
        peers += [(2 * to + core, at) for _, to, _ in chips for _, at, _ in cols]
    for peer in peers:
        pl.semaphore_signal(barrier, inc=1, device_id=peer, device_id_type=MESH)

    loads[0].wait()
    loads[1].wait()
    loads[2].wait()
    place = (
        lax.broadcasted_iota(jnp.int32, (tile, tile), 0) == order[...]
    ).astype(F32).astype(BF16)
    mixed = dot(feat[...], weight[...]).astype(BF16)
    panel = lax.dot_general(
        place, mixed, (((0,), (0,)), ((), ())), preferred_element_type=F32
    ).astype(BF16)
    for h in range(2):
        panels[h, rows(b), :] = panel[:, h * half:(h + 1) * half]
    pl.semaphore_wait(barrier, len(peers))

    for h in range(2):
        at = panels.at[h, rows(b)]
        for k, to, _ in chips:
            send(at, at, ag_s.at[h, 0], ag_r.at[h, b], 2 * to + core, c, keep=False)
        send(at, at, ag_s.at[h, 0], ag_r.at[h, sib], sib, c, keep=False)

    feat_t[...] = lax.dot_general(
        feat[...], place, (((0,), (0,)), ((), ())), preferred_element_type=F32
    ).astype(BF16)
    feat_all[:, rows(b)] = feat_t[rows(core, fhalf), :]

    loads[3].wait()

    def build(g, _):
        held = [tiles[g * SLOTS + s] for s in range(SLOTS)]
        ids = [list_ref[0, g * SLOTS + s] - b * n_col for s in range(SLOTS)]
        for r in range(n_col):
            block = jnp.zeros((tile, tile), BF16)
            for t, i in zip(held, ids):
                block = block + jnp.where(i == r, t, jnp.zeros_like(t))
            adj[r * tile:(r + 1) * tile, rows(g)] = block
        return 0

    lax.fori_loop(0, n_blk, build, 0)
    step = 4 * tile if n_col % 4 == 0 else tile
    for h in range(2):
        for k, _, src in chips:
            at = panels.at[h, rows(2 * src + core)]
            arrive(at, ag_s.at[h, 0], ag_r.at[h, 2 * src + core])
            send(at, at, ag_s.at[h, 0], ag_r.at[h, sib], sib, c, keep=False)
        arrive(panels.at[h, pl.ds(0, n_chip * tile)], ag_s.at[h, 0], ag_r.at[h, b])

        def forward(i, _):
            got = dot(adj[rows(i, step), :], panels[h])
            part[h, rows(i, step), :] = got
            part16[h, rows(i, step), :] = got.astype(BF16)
            return 0

        lax.fori_loop(0, n_col * tile // step, forward, 0)
        if line:
            send(
                part16.at[h, rows(3 - c)], relay_in.at[h], rl_s.at[h, 0], rl_r.at[h],
                b, 1 + c // 3, ends,
            )
        for k, to, _ in cols:
            only = {1: c != 3, 2: ends, 3: c != 0}[k] if line else None
            send(
                part16.at[h, rows(to)], agg_in.at[h, rows(c)], rc_s.at[h, k], rc_r.at[h, c], b, to,
                only,
            )

    for k, to, _ in chips:
        for q in range(2):
            at = feat_all.at[:, rows(b)]
            send(feat_t.at[pl.ds(q * fhalf, fhalf)], at, fe_s.at[0], fe_r.at[0], 2 * to + q, c, keep=False)
    send(
        feat_t.at[rows(1 - core, fhalf)], feat_all.at[:, rows(b)], fe_s.at[0], fe_r.at[0], sib, c,
        keep=False,
    )

    if line:
        for h in range(2):
            @pl.when(c % 3 != 0)
            def _():
                arrive(relay_in.at[h], rl_s.at[h, 0], rl_r.at[h])
                both = part[h, rows(far), :] + relay_in[h].astype(F32)
                relay_out[h] = both.astype(BF16)

            send(
                relay_out.at[h], agg_in.at[h, rows(c)], rl_s.at[h, 1], rc_r.at[h, c],
                b, far, c % 3 != 0,
            )

    def turn(g, _):
        for r in range(n_col):
            adj_t[rows(g), r * tile:(r + 1) * tile] = (
                adj[r * tile:(r + 1) * tile, rows(g)].T
            )
        return 0

    turned = adj_t.shape[0] > tile
    if turned:
        lax.fori_loop(0, n_blk, turn, 0)
    loads[4].wait()

    root = 0.7978845608028654
    for h in range(2):
        agg = part[h, rows(c), :]
        for k, _, src in cols:
            come = functools.partial(arrive, agg_in.at[h, rows(src)], rc_s.at[h, k], rc_r.at[h, src])
            if line and k != 2:
                pl.when(c != (3 if k == 3 else 0))(come)
            else:
                come()
        for k, _, src in cols:
            agg = agg + agg_in[h, rows(src), :].astype(F32)
        inner = root * (agg + 0.044715 * agg * agg * agg)
        th = jnp.tanh(inner)
        slope = 0.5 * (1.0 + th) + 0.5 * agg * (1.0 - th * th) * (
            root * (1.0 + 3 * 0.044715 * agg * agg)
        )
        lanes = slice(h * half, (h + 1) * half)
        grads[h, rows(c), :] = (cot[:, lanes].astype(F32) * slope).astype(BF16)
        at = grads.at[h, rows(c)]
        for k, to, _ in cols:
            only = {1: c != 3, 2: None, 3: c != 0}[k] if line else None
            send(at, at, gc_s.at[h, k], gc_r.at[h, c], b, to, only)
        hidden[:, lanes] = (0.5 * agg * (1.0 + th)).astype(BF16)
    outs = [pltpu.make_async_copy(hidden, hidden_h, out_sem.at[0])]
    outs[0].start()
    for h in range(2):
        sent(panels.at[h, pl.ds(0, (n_blk - 1) * tile)], ag_s.at[h, 0])

    bstep = 4 * tile if n_blk % 4 == 0 else tile
    others = [
        ((chip + i) % n_chip, (c + j) % n_col, (chip + n_chip - i) % n_chip, (c + n_col - j) % n_col)
        for i in range(n_chip) for j in range(n_col) if i + j > 0
    ]
    mine = chip * n_col + c

    def pair_start(h):
        for k, _, src in cols:
            come = functools.partial(arrive, grads.at[h, rows(src)], gc_s.at[h, k], gc_r.at[h, src])
            if line and k == 2:
                pl.when(ends)(come)
            else:
                come()

        def backward(i, _):
            if turned:
                got = dot(adj_t[rows(i, bstep), :], grads[h])
            else:
                got = lax.dot_general(
                    adj[:, rows(i, bstep)], grads[h], (((0,), (0,)), ((), ())),
                    preferred_element_type=F32,
                )
            pg_part[h, rows(i, bstep), :] = got
            pg16[h, rows(i, bstep), :] = got.astype(BF16)
            return 0

        lax.fori_loop(0, n_blk * tile // bstep, backward, 0)
        send(pg16.at[h], pair_in.at[h], pp_s.at[h], pp_r.at[h], sib, c)

    def features_arrive():
        arrive(feat_all.at[:, pl.ds(0, (n_blk - 1) * tile)], fe_s.at[0], fe_r.at[0])

    def terms_start(h):
        arrive(pair_in.at[h], pp_s.at[h], pp_r.at[h])
        both16[h] = (pg_part[h] + pair_in[h].astype(F32)).astype(BF16)
        term = dot(feat_all[...], both16[h])
        dw_sum[h, 0:fhalf, :] = term
        dw16[h, 0:fhalf, :] = term.astype(BF16)
        if direct:
            for to, to_col, _, _ in others:
                owner = to * n_col + to_col
                send(
                    dw16.at[h, rows(owner, r1)], dw_in.at[h, rows(mine, r1)],
                    dc_s.at[h, 0], dc_r.at[h, 0], 2 * to + core, to_col, owner < n_own, keep=False,
                )
            return
        if n_chip * r1 > fhalf:
            rest = jnp.zeros((n_chip * r1 - fhalf, half), F32)
            dw_sum[h, fhalf:, :] = rest
            dw16[h, fhalf:, :] = rest.astype(BF16)
        for k, to, _ in chips:
            send(
                dw16.at[h, rows(to, r1)], dw_in.at[h, rows(chip, r1)],
                dc_s.at[h, k], dc_r.at[h, chip], 2 * to + core, c,
            )

    def owners_start():
        for k, to, _ in chips:
            send(
                both16.at[:, rows(2 * to + core)], chip_in.at[:, rows(chip)],
                pc_s.at[0, 0], pc_r.at[0, 0], 2 * to + core, c, keep=False,
            )

    def result_direct(h):
        count = len(others) * r1

        @pl.when(mine < n_own)
        def _():
            arrive(dw_in.at[h, pl.ds(0, count)], dc_s.at[h, 0], dc_r.at[h, 0])
            piece = dw_sum[h, rows(mine, r1), :]
            for _, _, src, src_col in others:
                piece = piece + dw_in[h, rows(src * n_col + src_col, r1), :].astype(F32)
            dw_all[core, h, rows(mine, r1), :] = piece.astype(BF16)

        at = dw_all.at[core, h, rows(mine, r1)]
        for to, to_col, _, _ in others:
            send(
                at, at, dg_s.at[h, 0], dg_r.at[h, 0], 2 * to + core, to_col, mine < n_own,
                keep=False,
            )

    def pass_direct(h):
        for owns in range(2):
            rest = (n_own - owns) * r1

            @pl.when((mine < n_own) == bool(owns))
            def _():
                sent(dw16.at[h, pl.ds(0, rest)], dc_s.at[h, 0])
                arrive(dw_all.at[core, h, pl.ds(0, rest)], dg_s.at[h, 0], dg_r.at[h, 0])

        at = dw_all.at[core, h]
        send(at, at, di_s.at[h, 0], di_r.at[h, 0], sib, c)

    def result_start(h):
        piece = dw_sum[h, rows(chip, r1), :]
        for k, _, src in chips:
            arrive(dw_in.at[h, rows(src, r1)], dc_s.at[h, k], dc_r.at[h, src])
            piece = piece + dw_in[h, rows(src, r1), :].astype(F32)
        dw_mid[h, 0:r1, :] = piece
        dw_mid16[h, 0:r1, :] = piece.astype(BF16)
        if n_col * r2 > r1:
            rest = jnp.zeros((n_col * r2 - r1, half), F32)
            dw_mid[h, r1:, :] = rest
            dw_mid16[h, r1:, :] = rest.astype(BF16)
        for k, to, _ in cols:
            send(
                dw_mid16.at[h, rows(to, r2)], dw_col.at[h, rows(c, r2)],
                dz_s.at[h, k], dz_r.at[h, c], b, to,
            )
        piece = dw_mid[h, rows(c, r2), :]
        for k, _, src in cols:
            arrive(dw_col.at[h, rows(src, r2)], dz_s.at[h, k], dz_r.at[h, src])
            piece = piece + dw_col[h, rows(src, r2), :].astype(F32)
        dw_all[core, h, chip, rows(c, r2), :] = piece.astype(BF16)
        at = dw_all.at[core, h, chip, rows(c, r2)]
        for k, to, _ in cols:
            send(at, at, dg_s.at[h, k], dg_r.at[h, c], b, to)
        for k, _, src in cols:
            at = dw_all.at[core, h, chip, rows(src, r2)]
            arrive(at, dg_s.at[h, k], dg_r.at[h, src])
        at = dw_all.at[core, h, chip, pl.ds(0, r1)]
        for k, to, _ in chips:
            send(at, at, dh_s.at[h, k], dh_r.at[h, chip], 2 * to + core, c)
        send(at, at, di_s.at[h, chip], di_r.at[h, chip], sib, c)

    def result_pass(h):
        for k, _, src in chips:
            at = dw_all.at[core, h, src, pl.ds(0, r1)]
            arrive(at, dh_s.at[h, k], dh_r.at[h, src])
            send(at, at, di_s.at[h, src], di_r.at[h, src], sib, c)

    def result_arrive(h):
        for src in range(n_chip):
            at = dw_all.at[1 - core, h, src, pl.ds(0, r1)]
            arrive(at, di_s.at[h, src], di_r.at[h, src])

    def own_features():
        sums = []
        arrive(chip_in.at[:, pl.ds(0, (n_chip - 1) * tile)], pc_s.at[0, 0], pc_r.at[0, 0])
        for h in range(2):
            total = pg_part[h, rows(b), :] + pair_in[h, rows(b), :].astype(F32)
            for k, _, src in chips:
                total = total + chip_in[h, rows(src), :].astype(F32)
            sums.append(total.astype(BF16))
        back = dot(place, jnp.concatenate(sums, axis=1)).astype(BF16)
        xgrad[...] = lax.dot_general(
            back, weight[...], (((1,), (1,)), ((), ())), preferred_element_type=F32
        ).astype(BF16)
        outs.append(pltpu.make_async_copy(xgrad, xgrad_h, out_sem.at[1]))
        outs[1].start()

    if line:
        for h in range(2):
            at = grads.at[h, rows(far)]
            pl.when(c % 3 != 0)(
                functools.partial(arrive, at, gc_s.at[h, 0], gc_r.at[h, far])
            )
            send(at, at, gc_s.at[h, 0], gc_r.at[h, far], b, 3 - far, c % 3 != 0)
    pair_start(0)
    pair_start(1)
    features_arrive()
    terms_start(0)
    terms_start(1)
    owners_start()
    if direct:
        result_direct(0)
        result_direct(1)
        own_features()
        pass_direct(0)
        pass_direct(1)
        for h in range(2):
            arrive(dw_all.at[1 - core, h], di_s.at[h, 0], di_r.at[h, 0])
    else:
        result_start(0)
        result_start(1)
        own_features()
        result_pass(0)
        result_pass(1)
        result_arrive(0)
        result_arrive(1)
    if direct:
        outs.append(pltpu.make_async_copy(dw_all, wgrad_h, out_sem.at[2]))
    else:
        outs.append(
            pltpu.make_async_copy(dw_all.at[:, :, :, pl.ds(0, r1)], wgrad_h, out_sem.at[2])
        )
    outs[2].start()
    sent(both16.at[:, pl.ds(0, (n_chip - 1) * tile)], pc_s.at[0, 0])
    sent(feat_all.at[:, pl.ds(0, (n_blk - 1) * tile)], fe_s.at[0])
    if direct:
        @pl.when(mine < n_own)
        def _():
            for h in range(2):
                sent(dw_in.at[h, pl.ds(0, len(others) * r1)], dg_s.at[h, 0])

    for copy, only in sends:
        if only is None:
            copy.wait_send()
        else:
            pl.when(only)(copy.wait_send)
    for copy in outs:
        copy.wait()


def finish(scale, r1, hidden_in, xgrad_in, wgrad_in, hidden_ref, xgrad_ref, wgrad_ref):
    hidden_ref[...] = hidden_in[...]
    xgrad_ref[...] = xgrad_in[...]
    n_part, half = wgrad_in.shape[2], wgrad_in.shape[4]
    fhalf = wgrad_ref.shape[0] // 2
    for core in range(2):
        for i in range(n_part):
            count = min(r1, fhalf - i * r1)
            if count > 0:
                start = core * fhalf + i * r1
                for h in range(2):
                    wgrad_ref[start:start + count, h * half:(h + 1) * half] = (
                        wgrad_in[core, h, i, 0:count, :].astype(F32) * scale
                    )


def per_device(features, node_order, weight, cotangent, tile_list, tile_values):
    n_blk, n_col = lax.axis_size("blk"), lax.axis_size("col")
    slots, tile, _ = tile_values.shape
    fin, hid = weight.shape
    n_chip = n_blk // 2
    half, fhalf = hid // 2, fin // 2
    scale = float(n_blk * n_col * tile) ** -0.5
    direct = n_chip * n_col <= 16
    n_sum = n_chip * n_col if direct else n_chip
    r1 = -(-fhalf // (16 * n_sum)) * 16
    direct = direct and fhalf % r1 == 0
    r2 = 16 if direct else -(-r1 // (16 * n_col)) * 16
    padded = fhalf if direct else n_chip * r1
    dma = lambda *n: pltpu.SemaphoreType.DMA(n)
    vmem = pltpu.VMEM
    wide, tall = n_blk * tile, n_col * tile
    turned = wide * tall <= 2 ** 21
    scratch = [
        vmem((tile, fin), BF16), vmem((1, tile), jnp.int32), vmem((fin, hid), BF16),
        vmem((tile, hid), BF16), vmem((slots, tile, tile), BF16),
        vmem((tile, hid), BF16), vmem((tile, fin), BF16),
        vmem((tall, wide), BF16), vmem((wide if turned else tile, tall), BF16),
        vmem((fin, tile), BF16), vmem((fhalf, wide), BF16),
        vmem((2, wide, half), BF16),
        vmem((2, tall, half), F32), vmem((2, tall, half), BF16), vmem((2, tall, half), BF16),
        vmem((2, tall, half), BF16),
        vmem((2, wide, half), F32), vmem((2, wide, half), BF16), vmem((2, wide, half), BF16),
        vmem((2, wide, half), BF16), vmem((2, n_chip * tile, half), BF16),
        vmem((2, padded, half), F32), vmem((2, padded, half), BF16),
        vmem((2, n_sum * r1, half), BF16),
        vmem((2, n_col * r2, half), F32), vmem((2, n_col * r2, half), BF16),
        vmem((2, n_col * r2, half), BF16), vmem((2, 2, fhalf, half) if direct else (2, 2, n_chip, n_col * r2, half), BF16),
        vmem((2, tile, half), BF16), vmem((2, tile, half), BF16),
        dma(5), dma(3), dma(2, 2 * n_chip), dma(2, n_blk),
        dma(2, n_col), dma(2, n_col), dma(2, n_col), dma(2, n_col),
        dma(2), dma(2), dma(2, n_chip), dma(2, n_chip),
        dma(2 * n_chip), dma(n_blk), dma(2, n_sum), dma(2, n_sum),
        dma(2, n_col), dma(2, n_col), dma(2, n_sum + n_col), dma(2, n_sum + n_col),
        dma(2, n_chip), dma(2, n_chip), dma(2, n_sum), dma(2, n_sum), dma(2, 2), dma(2),
    ]
    far = pl.BlockSpec(memory_space=pltpu.HBM)
    free = pl.BlockSpec(memory_space=pl.ANY)
    inside = pl.BlockSpec(memory_space=pltpu.VMEM)
    limit = 60 * 1024 * 1024
    hidden, xgrad, wgrad = pl.pallas_call(
        functools.partial(kernel, (n_blk, n_col, tile, fin, hid, r1, r2, direct)),
        out_shape=(
            jax.ShapeDtypeStruct((tile, hid), BF16),
            jax.ShapeDtypeStruct((tile, fin), BF16),
            jax.ShapeDtypeStruct(
                (2, 2, fhalf, half) if direct else (2, 2, n_chip, r1, half), BF16
            ),
        ),
        in_specs=[far, far, far, far, pl.BlockSpec(memory_space=pltpu.SMEM), far],
        out_specs=(free, free, free),
        scratch_shapes=scratch,
        compiler_params=pltpu.CompilerParams(
            collective_id=0, has_side_effects=True, vmem_limit_bytes=limit
        ),
        cost_estimate=pl.CostEstimate(
            flops=4 * slots * tile * tile * hid, bytes_accessed=4 * 1024 * 1024,
            transcendentals=tile * hid,
        ),
    )(features, node_order, weight, cotangent, tile_list.T, tile_values)
    if direct:
        wgrad, r1 = wgrad.reshape(2, 2, 1, fhalf, half), fhalf
    return pl.pallas_call(
        functools.partial(finish, scale, r1),
        out_shape=(
            jax.ShapeDtypeStruct((tile, hid), BF16),
            jax.ShapeDtypeStruct((tile, fin), BF16),
            jax.ShapeDtypeStruct((fin, hid), F32),
        ),
        in_specs=[inside] * 3,
        out_specs=(inside,) * 3,
        compiler_params=pltpu.CompilerParams(vmem_limit_bytes=limit),
    )(hidden, xgrad, wgrad)


def solution(mesh):
    in_specs = (
        P(("blk", "col"), None),
        P(("blk", "col"), None),
        P(),
        P(("blk", "col"), None),
        P(("blk", "col"), None),
        P(("blk", "col"), None, None),
    )
    out_specs = (P(("blk", "col"), None), P(("blk", "col"), None), P())
    return jax.shard_map(
        per_device, mesh=mesh, in_specs=in_specs, out_specs=out_specs, check_vma=False
    )
```

```python
import functools

import jax
import jax.numpy as jnp
from jax import lax
from jax.experimental import pallas as pl
from jax.experimental.pallas import tpu as pltpu
from jax.sharding import PartitionSpec as P

SLOTS = 3
MESH = pl.DeviceIdType.MESH
F32 = jnp.float32
BF16 = jnp.bfloat16


def dot(a, b):
    return jnp.dot(a, b, preferred_element_type=F32)


def kernel(
    dims,
    feat_h, order_h, weight_h, cot_h, list_ref, tiles_h,
    hidden_h, xgrad_h, wgrad_h,
    feat, order, weight, cot, tiles, hidden, xgrad,
    adj, adj_t, feat_t, feat_all, panels, part, part16, agg_in, grads, pg_part, pg16,
    pair_in, both16, chip_in, dw_sum, dw16, dw_in, dw_mid, dw_mid16, dw_col, dw_all,
    in_sem, out_sem, ag_s, ag_r, rc_s, rc_r, gc_s, gc_r, pp_s, pp_r, pc_s, pc_r,
    fe_s, fe_r, dc_s, dc_r, dz_s, dz_r, dg_s, dg_r, dh_s, dh_r, di_s, di_r,
):
    n_blk, n_col, tile, fin, hid, r1, r2, direct = dims
    n_chip = n_blk // 2
    half = hid // 2
    fhalf = fin // 2
    n_own = fhalf // r1
    b = lax.axis_index("blk")
    c = lax.axis_index("col")
    chip = b // 2
    core = b % 2
    sib = b + 1 - 2 * core
    sends = []

    def rows(i, n=tile):
        return pl.ds(pl.multiple_of(i * n, n), n)

    def send(src, dst, s_sem, r_sem, blk, col, only=None):
        copy = pltpu.make_async_remote_copy(
            src_ref=src, dst_ref=dst, send_sem=s_sem, recv_sem=r_sem,
            device_id=(blk, col), device_id_type=MESH,
        )
        if only is None:
            copy.start()
        else:
            pl.when(only)(copy.start)
        sends.append((copy, only))

    def arrive(dst, s_sem, r_sem):
        pltpu.make_async_remote_copy(
            src_ref=dst, dst_ref=dst, send_sem=s_sem, recv_sem=r_sem,
            device_id=(sib, c), device_id_type=MESH,
        ).wait_recv()

    chips = [(k, (chip + k) % n_chip, (chip + n_chip - k) % n_chip) for k in range(1, n_chip)]
    cols = [(k, (c + k) % n_col, (c + n_col - k) % n_col) for k in range(1, n_col)]

    loads = []
    for i, (src, dst) in enumerate(
        ((feat_h, feat), (weight_h, weight), (order_h, order), (tiles_h, tiles), (cot_h, cot))
    ):
        copy = pltpu.make_async_copy(src, dst, in_sem.at[i])
        copy.start()
        loads.append(copy)

    barrier = pltpu.get_barrier_semaphore()
    peers = [(sib, c)]
    peers += [(2 * to + core, c) for _, to, _ in chips]
    peers += [(2 * to + 1 - core, c) for _, to, _ in chips]
    peers += [(b, to) for _, to, _ in cols]
    if direct:
        peers += [(2 * to + core, at) for _, to, _ in chips for _, at, _ in cols]
    for peer in peers:
        pl.semaphore_signal(barrier, inc=1, device_id=peer, device_id_type=MESH)

    loads[0].wait()
    loads[1].wait()
    loads[2].wait()
    place = (
        lax.broadcasted_iota(jnp.int32, (tile, tile), 0) == order[...]
    ).astype(F32).astype(BF16)
    mixed = dot(feat[...], weight[...]).astype(BF16)
    panel = lax.dot_general(
        place, mixed, (((0,), (0,)), ((), ())), preferred_element_type=F32
    ).astype(BF16)
    for h in range(2):
        panels[h, rows(b), :] = panel[:, h * half:(h + 1) * half]
    pl.semaphore_wait(barrier, len(peers))

    for h in range(2):
        at = panels.at[h, rows(b)]
        for k, to, _ in chips:
            send(at, at, ag_s.at[h, k], ag_r.at[h, b], 2 * to + core, c)
        send(at, at, ag_s.at[h, 0], ag_r.at[h, b], sib, c)

    loads[3].wait()

    def build(g, _):
        held = [tiles[g * SLOTS + s] for s in range(SLOTS)]
        ids = [list_ref[0, g * SLOTS + s] - b * n_col for s in range(SLOTS)]
        for r in range(n_col):
            block = jnp.zeros((tile, tile), BF16)
            for t, i in zip(held, ids):
                block = block + jnp.where(i == r, t, jnp.zeros_like(t))
            adj[r * tile:(r + 1) * tile, rows(g)] = block
        return 0

    lax.fori_loop(0, n_blk, build, 0)
    feat_t[...] = lax.dot_general(
        feat[...], place, (((0,), (0,)), ((), ())), preferred_element_type=F32
    ).astype(BF16)
    feat_all[:, rows(b)] = feat_t[rows(core, fhalf), :]

    step = 4 * tile if n_col % 4 == 0 else tile
    for h in range(2):
        for k, _, src in chips:
            at = panels.at[h, rows(2 * src + core)]
            arrive(at, ag_s.at[h, k], ag_r.at[h, 2 * src + core])
            send(at, at, ag_s.at[h, n_chip + k], ag_r.at[h, 2 * src + core], sib, c)
        arrive(panels.at[h, rows(sib)], ag_s.at[h, 0], ag_r.at[h, sib])
        for k, _, src in chips:
            at = 2 * src + 1 - core
            arrive(panels.at[h, rows(at)], ag_s.at[h, k], ag_r.at[h, at])

        def forward(i, _):
            got = dot(adj[rows(i, step), :], panels[h])
            part[h, rows(i, step), :] = got
            part16[h, rows(i, step), :] = got.astype(BF16)
            return 0

        lax.fori_loop(0, n_col * tile // step, forward, 0)
        for k, to, _ in cols:
            send(part16.at[h, rows(to)], agg_in.at[h, rows(c)], rc_s.at[h, k], rc_r.at[h, c], b, to)

    for k, to, _ in chips:
        for q in range(2):
            at = feat_all.at[:, rows(b)]
            send(feat_t.at[pl.ds(q * fhalf, fhalf)], at, fe_s.at[2 * k + q], fe_r.at[b], 2 * to + q, c)
    send(feat_t.at[rows(1 - core, fhalf)], feat_all.at[:, rows(b)], fe_s.at[0], fe_r.at[b], sib, c)

    def turn(g, _):
        for r in range(n_col):
            adj_t[rows(g), r * tile:(r + 1) * tile] = (
                adj[r * tile:(r + 1) * tile, rows(g)].T
            )
        return 0

    turned = adj_t.shape[0] > tile
    if turned:
        lax.fori_loop(0, n_blk, turn, 0)
    loads[4].wait()

    root = 0.7978845608028654
    for h in range(2):
        agg = part[h, rows(c), :]
        for k, _, src in cols:
            arrive(agg_in.at[h, rows(src)], rc_s.at[h, k], rc_r.at[h, src])
            agg = agg + agg_in[h, rows(src), :].astype(F32)
        inner = root * (agg + 0.044715 * agg * agg * agg)
        th = jnp.tanh(inner)
        slope = 0.5 * (1.0 + th) + 0.5 * agg * (1.0 - th * th) * (
            root * (1.0 + 3 * 0.044715 * agg * agg)
        )
        lanes = slice(h * half, (h + 1) * half)
        grads[h, rows(c), :] = (cot[:, lanes].astype(F32) * slope).astype(BF16)
        at = grads.at[h, rows(c)]
        for k, to, _ in cols:
            send(at, at, gc_s.at[h, k], gc_r.at[h, c], b, to)
        hidden[:, lanes] = (0.5 * agg * (1.0 + th)).astype(BF16)
    outs = [pltpu.make_async_copy(hidden, hidden_h, out_sem.at[0])]
    outs[0].start()

    bstep = 4 * tile if n_blk % 4 == 0 else tile
    others = [
        ((chip + i) % n_chip, (c + j) % n_col, (chip + n_chip - i) % n_chip, (c + n_col - j) % n_col)
        for i in range(n_chip) for j in range(n_col) if i + j > 0
    ]
    mine = chip * n_col + c

    def pair_start(h):
        for k, _, src in cols:
            arrive(grads.at[h, rows(src)], gc_s.at[h, k], gc_r.at[h, src])

        def backward(i, _):
            if turned:
                got = dot(adj_t[rows(i, bstep), :], grads[h])
            else:
                got = lax.dot_general(
                    adj[:, rows(i, bstep)], grads[h], (((0,), (0,)), ((), ())),
                    preferred_element_type=F32,
                )
            pg_part[h, rows(i, bstep), :] = got
            pg16[h, rows(i, bstep), :] = got.astype(BF16)
            return 0

        lax.fori_loop(0, n_blk * tile // bstep, backward, 0)
        send(pg16.at[h], pair_in.at[h], pp_s.at[h], pp_r.at[h], sib, c)

    def features_arrive():
        for k, _, src in chips:
            for q in range(2):
                at = feat_all.at[:, rows(2 * src + q)]
                arrive(at, fe_s.at[0], fe_r.at[2 * src + q])
        arrive(feat_all.at[:, rows(sib)], fe_s.at[0], fe_r.at[sib])

    def terms_start(h):
        arrive(pair_in.at[h], pp_s.at[h], pp_r.at[h])
        both16[h] = (pg_part[h] + pair_in[h].astype(F32)).astype(BF16)
        term = dot(feat_all[...], both16[h])
        dw_sum[h, 0:fhalf, :] = term
        dw16[h, 0:fhalf, :] = term.astype(BF16)
        if direct:
            for i, (to, to_col, _, _) in enumerate(others):
                owner = to * n_col + to_col
                send(
                    dw16.at[h, rows(owner, r1)], dw_in.at[h, rows(mine, r1)],
                    dc_s.at[h, i], dc_r.at[h, mine], 2 * to + core, to_col, owner < n_own,
                )
            return
        if n_chip * r1 > fhalf:
            rest = jnp.zeros((n_chip * r1 - fhalf, half), F32)
            dw_sum[h, fhalf:, :] = rest
            dw16[h, fhalf:, :] = rest.astype(BF16)
        for k, to, _ in chips:
            send(
                dw16.at[h, rows(to, r1)], dw_in.at[h, rows(chip, r1)],
                dc_s.at[h, k], dc_r.at[h, chip], 2 * to + core, c,
            )

    def owners_start(h):
        for k, to, _ in chips:
            send(
                both16.at[h, rows(2 * to + core)], chip_in.at[h, rows(chip)],
                pc_s.at[h, k], pc_r.at[h, chip], 2 * to + core, c,
            )

    def result_start(h):
        if direct:
            @pl.when(mine < n_own)
            def _():
                piece = dw_sum[h, rows(mine, r1), :]
                for i, (_, _, src, src_col) in enumerate(others):
                    at = src * n_col + src_col
                    arrive(dw_in.at[h, rows(at, r1)], dc_s.at[h, i], dc_r.at[h, at])
                    piece = piece + dw_in[h, rows(at, r1), :].astype(F32)
                dw_all[core, h, rows(mine, r1), :] = piece.astype(BF16)

            at = dw_all.at[core, h, rows(mine, r1)]
            for i, (to, to_col, _, _) in enumerate(others):
                send(at, at, dg_s.at[h, i], dg_r.at[h, mine], 2 * to + core, to_col, mine < n_own)
            send(at, at, di_s.at[h, mine], di_r.at[h, mine], sib, c, mine < n_own)
            return
        piece = dw_sum[h, rows(chip, r1), :]
        for k, _, src in chips:
            arrive(dw_in.at[h, rows(src, r1)], dc_s.at[h, k], dc_r.at[h, src])
            piece = piece + dw_in[h, rows(src, r1), :].astype(F32)
        dw_mid[h, 0:r1, :] = piece
        dw_mid16[h, 0:r1, :] = piece.astype(BF16)
        if n_col * r2 > r1:
            rest = jnp.zeros((n_col * r2 - r1, half), F32)
            dw_mid[h, r1:, :] = rest
            dw_mid16[h, r1:, :] = rest.astype(BF16)
        for k, to, _ in cols:
            send(
                dw_mid16.at[h, rows(to, r2)], dw_col.at[h, rows(c, r2)],
                dz_s.at[h, k], dz_r.at[h, c], b, to,
            )
        piece = dw_mid[h, rows(c, r2), :]
        for k, _, src in cols:
            arrive(dw_col.at[h, rows(src, r2)], dz_s.at[h, k], dz_r.at[h, src])
            piece = piece + dw_col[h, rows(src, r2), :].astype(F32)
        dw_all[core, h, chip, rows(c, r2), :] = piece.astype(BF16)
        at = dw_all.at[core, h, chip, rows(c, r2)]
        for k, to, _ in cols:
            send(at, at, dg_s.at[h, k], dg_r.at[h, c], b, to)
        for k, _, src in cols:
            at = dw_all.at[core, h, chip, rows(src, r2)]
            arrive(at, dg_s.at[h, k], dg_r.at[h, src])
        at = dw_all.at[core, h, chip, pl.ds(0, r1)]
        for k, to, _ in chips:
            send(at, at, dh_s.at[h, k], dh_r.at[h, chip], 2 * to + core, c)
        send(at, at, di_s.at[h, chip], di_r.at[h, chip], sib, c)

    def result_pass(h):
        if direct:
            for i, (_, _, src, src_col) in enumerate(others):
                owner = src * n_col + src_col
                at = dw_all.at[core, h, rows(owner, r1)]

                @pl.when(owner < n_own)
                def _():
                    arrive(at, dg_s.at[h, i], dg_r.at[h, owner])

                send(at, at, di_s.at[h, owner], di_r.at[h, owner], sib, c, owner < n_own)
            return
        for k, _, src in chips:
            at = dw_all.at[core, h, src, pl.ds(0, r1)]
            arrive(at, dh_s.at[h, k], dh_r.at[h, src])
            send(at, at, di_s.at[h, src], di_r.at[h, src], sib, c)

    def result_arrive(h):
        if direct:
            for owner in range(n_own):
                at = dw_all.at[1 - core, h, rows(owner, r1)]
                arrive(at, di_s.at[h, owner], di_r.at[h, owner])
            return
        for src in range(n_chip):
            at = dw_all.at[1 - core, h, src, pl.ds(0, r1)]
            arrive(at, di_s.at[h, src], di_r.at[h, src])

    def own_features():
        sums = []
        for h in range(2):
            total = pg_part[h, rows(b), :] + pair_in[h, rows(b), :].astype(F32)
            for k, _, src in chips:
                arrive(chip_in.at[h, rows(src)], pc_s.at[h, k], pc_r.at[h, src])
                total = total + chip_in[h, rows(src), :].astype(F32)
            sums.append(total.astype(BF16))
        back = dot(place, jnp.concatenate(sums, axis=1)).astype(BF16)
        xgrad[...] = lax.dot_general(
            back, weight[...], (((1,), (1,)), ((), ())), preferred_element_type=F32
        ).astype(BF16)
        outs.append(pltpu.make_async_copy(xgrad, xgrad_h, out_sem.at[1]))
        outs[1].start()

    pair_start(0)
    pair_start(1)
    features_arrive()
    terms_start(0)
    terms_start(1)
    result_start(0)
    owners_start(0)
    owners_start(1)
    result_start(1)
    result_pass(0)
    result_pass(1)
    own_features()
    result_arrive(0)
    result_arrive(1)
    if direct:
        outs.append(pltpu.make_async_copy(dw_all, wgrad_h, out_sem.at[2]))
    else:
        outs.append(
            pltpu.make_async_copy(dw_all.at[:, :, :, pl.ds(0, r1)], wgrad_h, out_sem.at[2])
        )
    outs[2].start()
    for copy, only in sends:
        if only is None:
            copy.wait_send()
        else:
            pl.when(only)(copy.wait_send)
    for copy in outs:
        copy.wait()


def finish(scale, r1, hidden_in, xgrad_in, wgrad_in, hidden_ref, xgrad_ref, wgrad_ref):
    hidden_ref[...] = hidden_in[...]
    xgrad_ref[...] = xgrad_in[...]
    n_part, half = wgrad_in.shape[2], wgrad_in.shape[4]
    fhalf = wgrad_ref.shape[0] // 2
    for core in range(2):
        for i in range(n_part):
            count = min(r1, fhalf - i * r1)
            if count > 0:
                start = core * fhalf + i * r1
                for h in range(2):
                    wgrad_ref[start:start + count, h * half:(h + 1) * half] = (
                        wgrad_in[core, h, i, 0:count, :].astype(F32) * scale
                    )


def per_device(features, node_order, weight, cotangent, tile_list, tile_values):
    n_blk, n_col = lax.axis_size("blk"), lax.axis_size("col")
    slots, tile, _ = tile_values.shape
    fin, hid = weight.shape
    n_chip = n_blk // 2
    half, fhalf = hid // 2, fin // 2
    scale = float(n_blk * n_col * tile) ** -0.5
    direct = n_chip * n_col <= 16
    n_sum = n_chip * n_col if direct else n_chip
    r1 = -(-fhalf // (16 * n_sum)) * 16
    direct = direct and fhalf % r1 == 0
    r2 = 16 if direct else -(-r1 // (16 * n_col)) * 16
    padded = fhalf if direct else n_chip * r1
    dma = lambda *n: pltpu.SemaphoreType.DMA(n)
    vmem = pltpu.VMEM
    wide, tall = n_blk * tile, n_col * tile
    turned = wide * tall <= 2 ** 21
    scratch = [
        vmem((tile, fin), BF16), vmem((1, tile), jnp.int32), vmem((fin, hid), BF16),
        vmem((tile, hid), BF16), vmem((slots, tile, tile), BF16),
        vmem((tile, hid), BF16), vmem((tile, fin), BF16),
        vmem((tall, wide), BF16), vmem((wide if turned else tile, tall), BF16),
        vmem((fin, tile), BF16), vmem((fhalf, wide), BF16),
        vmem((2, wide, half), BF16),
        vmem((2, tall, half), F32), vmem((2, tall, half), BF16), vmem((2, tall, half), BF16),
        vmem((2, tall, half), BF16),
        vmem((2, wide, half), F32), vmem((2, wide, half), BF16), vmem((2, wide, half), BF16),
        vmem((2, wide, half), BF16), vmem((2, n_chip * tile, half), BF16),
        vmem((2, padded, half), F32), vmem((2, padded, half), BF16),
        vmem((2, n_sum * r1, half), BF16),
        vmem((2, n_col * r2, half), F32), vmem((2, n_col * r2, half), BF16),
        vmem((2, n_col * r2, half), BF16), vmem((2, 2, fhalf, half) if direct else (2, 2, n_chip, n_col * r2, half), BF16),
        dma(5), dma(3), dma(2, 2 * n_chip), dma(2, n_blk),
        dma(2, n_col), dma(2, n_col), dma(2, n_col), dma(2, n_col),
        dma(2), dma(2), dma(2, n_chip), dma(2, n_chip),
        dma(2 * n_chip), dma(n_blk), dma(2, n_sum), dma(2, n_sum),
        dma(2, n_col), dma(2, n_col), dma(2, n_sum + n_col), dma(2, n_sum + n_col),
        dma(2, n_chip), dma(2, n_chip), dma(2, n_sum), dma(2, n_sum),
    ]
    far = pl.BlockSpec(memory_space=pltpu.HBM)
    free = pl.BlockSpec(memory_space=pl.ANY)
    inside = pl.BlockSpec(memory_space=pltpu.VMEM)
    limit = 60 * 1024 * 1024
    hidden, xgrad, wgrad = pl.pallas_call(
        functools.partial(kernel, (n_blk, n_col, tile, fin, hid, r1, r2, direct)),
        out_shape=(
            jax.ShapeDtypeStruct((tile, hid), BF16),
            jax.ShapeDtypeStruct((tile, fin), BF16),
            jax.ShapeDtypeStruct(
                (2, 2, fhalf, half) if direct else (2, 2, n_chip, r1, half), BF16
            ),
        ),
        in_specs=[far, far, far, far, pl.BlockSpec(memory_space=pltpu.SMEM), far],
        out_specs=(free, free, free),
        scratch_shapes=scratch,
        compiler_params=pltpu.CompilerParams(
            collective_id=0, has_side_effects=True, vmem_limit_bytes=limit
        ),
        cost_estimate=pl.CostEstimate(
            flops=4 * slots * tile * tile * hid, bytes_accessed=4 * 1024 * 1024,
            transcendentals=tile * hid,
        ),
    )(features, node_order, weight, cotangent, tile_list.T, tile_values)
    if direct:
        wgrad, r1 = wgrad.reshape(2, 2, 1, fhalf, half), fhalf
    return pl.pallas_call(
        functools.partial(finish, scale, r1),
        out_shape=(
            jax.ShapeDtypeStruct((tile, hid), BF16),
            jax.ShapeDtypeStruct((tile, fin), BF16),
            jax.ShapeDtypeStruct((fin, hid), F32),
        ),
        in_specs=[inside] * 3,
        out_specs=(inside,) * 3,
        compiler_params=pltpu.CompilerParams(vmem_limit_bytes=limit),
    )(hidden, xgrad, wgrad)


def solution(mesh):
    in_specs = (
        P(("blk", "col"), None),
        P(("blk", "col"), None),
        P(),
        P(("blk", "col"), None),
        P(("blk", "col"), None),
        P(("blk", "col"), None, None),
    )
    out_specs = (P(("blk", "col"), None), P(("blk", "col"), None), P())
    return jax.shard_map(
        per_device, mesh=mesh, in_specs=in_specs, out_specs=out_specs, check_vma=False
    )
```
